32 devices in a mesh: rows: 8 (over y, x, core), width: 4 (over z).
Axes of the slice: x: 2, y: 2, z: 4, core: 2. Of those that a mesh axis runs over, the one named last changes fastest.
Arguments:
- history: bfloat16 [25, 768, 16384], P(None, 'width', 'rows'), may hold values from -24 to 24
- cotangent: bfloat16 [768, 16384], P('width', 'rows'), may hold values from -12 to 12
- segments: int32 [16, 1024], P('rows'), may hold values from 0 to 15, never falling along the last dimension, each value on 1 to 256 neighbouring positions
- w_attend: float32 [3, 768, 768], P(None, 'rows', 'width'), may hold values from -0.21875 to 0.21875
- m_attend: float32 [3, 768, 768], P(None, 'rows', 'width'), may hold values from -160 to 160
- v_attend: float32 [3, 768, 768], P(None, 'rows', 'width'), may hold values from 3276.8 to 13107.2
- w_output: float32 [768, 768], P('width', 'rows'), may hold values from -1.25 to 1.25
- m_output: float32 [768, 768], P('width', 'rows'), may hold values from -48 to 48
- v_output: float32 [768, 768], P('width', 'rows'), may hold values from 311.296 to 1245.184
- w_expand: float32 [768, 3072], P('rows', 'width'), may hold values from -0.21875 to 0.21875
- m_expand: float32 [768, 3072], P('rows', 'width'), may hold values from -96 to 96
- v_expand: float32 [768, 3072], P('rows', 'width'), may hold values from 1245.184 to 4915.2
- w_reduce: float32 [3072, 768], P('width', 'rows'), may hold values from -0.21875 to 0.21875
- m_reduce: float32 [3072, 768], P('width', 'rows'), may hold values from -112 to 112
- v_reduce: float32 [3072, 768], P('width', 'rows'), may hold values from 1638.4 to 6225.92
- gains: float32 [2, 768], P(None, 'width'), may hold values from 0.5 to 1.5
- m_gains: float32 [2, 768], P(None, 'width'), may hold values from -160 to 160
- v_gains: float32 [2, 768], P(None, 'width'), may hold values from 3276.8 to 13107.2
- mix: float32 [25], replicated, may hold values from -4 to 4
- m_mix: float32 [25], replicated, may hold values from -12288 to 12288
- v_mix: float32 [25], replicated, may hold values from 16357786 to 66689432
Outputs:
- block_output: bfloat16 [768, 16384], P('width', 'rows')
- history_grad: bfloat16 [25, 768, 16384], P(None, 'width', 'rows')
- w_attend_new: float32 [3, 768, 768], P(None, 'rows', 'width')
- m_attend_new: float32 [3, 768, 768], P(None, 'rows', 'width')
- v_attend_new: float32 [3, 768, 768], P(None, 'rows', 'width')
- w_output_new: float32 [768, 768], P('width', 'rows')
- m_output_new: float32 [768, 768], P('width', 'rows')
- v_output_new: float32 [768, 768], P('width', 'rows')
- w_expand_new: float32 [768, 3072], P('rows', 'width')
- m_expand_new: float32 [768, 3072], P('rows', 'width')
- v_expand_new: float32 [768, 3072], P('rows', 'width')
- w_reduce_new: float32 [3072, 768], P('width', 'rows')
- m_reduce_new: float32 [3072, 768], P('width', 'rows')
- v_reduce_new: float32 [3072, 768], P('width', 'rows')
- gains_new: float32 [2, 768], P(None, 'width')
- m_gains_new: float32 [2, 768], P(None, 'width')
- v_gains_new: float32 [2, 768], P(None, 'width')
- mix_new: float32 [25], replicated
- m_mix_new: float32 [25], replicated
- v_mix_new: float32 [25], replicated
The draws below stay inside these ranges and needn't reach their ends.
Inputs may be any that keep to these rules, and one draw needn't show every extreme that they name: In each row of segments the numbers never fall; a run of equal numbers is one document.
All inputs are finite; a program needn't handle non-finite values.
Results may differ from the reference program's by a relative error of at most 0.012.
Values may be sent and summed in bfloat16 or wider, within the bound.
A program may use at most 192 MiB of HBM per device.

```python
import math
import jax
import jax.numpy as jnp
import numpy as np
from jax import lax

D = 768
HEADS = 12
HEAD = 64
FF = 3072
HIST = 25
SEQ = 1024
STEP = 10
SEQS = 16
TOKENS = 16384


def draw_history(key, part):
    key = jax.random.fold_in(key, 11)
    base_key, scale_key = jax.random.split(key)
    columns = jnp.arange(D, dtype=jnp.float32) / max(D - 1, 1)
    base_draw = jnp.clip(jax.random.normal(base_key, (HIST, D, TOKENS), jnp.float32), -4.0, 4.0)
    column_ramp = jnp.exp(columns * math.log(3.0))
    row_scale = jnp.exp(jax.random.uniform(scale_key, (HIST, 1, TOKENS), jnp.float32, -0.69, 0.69))
    return (base_draw * column_ramp[None, :, None] * row_scale).astype(jnp.bfloat16)


def draw_cotangent(key, part):
    key = jax.random.fold_in(key, 12)
    places = jnp.arange(TOKENS, dtype=jnp.float32) / max(TOKENS - 1, 1)
    base_draw = jnp.clip(jax.random.normal(key, (D, TOKENS), jnp.float32), -4.0, 4.0)
    token_ramp = jnp.exp(places * math.log(3.0))
    return (base_draw * token_ramp[None, :]).astype(jnp.bfloat16)


def levels(rng, extent, cuts, least, high):
    level, own = 1.0, jax.random.fold_in(rng, 6)
    for dim, blocks in cuts:
        draws = jnp.exp(jax.random.uniform(jax.random.fold_in(own, dim), (blocks,), jnp.float32, least / len(cuts), high / len(cuts)))
        level = level * jnp.repeat(draws, extent[dim] // blocks).reshape([-1 if axis == dim else 1 for axis in range(len(extent))])
    return level


def length_profile(amount, total, reach, skew):
    weights = [(1 << 20) // math.isqrt(standing ** skew) + 1 for standing in range(2, amount + 1)]
    spare, counts = total - reach - (amount - 1), [1] * (amount - 1)
    while spare > 0:
        free = [i for i in range(amount - 1) if counts[i] < reach]
        pool, remaining = sum([weights[i] for i in free]), spare
        for i in free:
            extra = min(reach - counts[i], max(1, remaining * weights[i] // pool), spare)
            counts[i] = counts[i] + extra
            spare = spare - extra
    return np.array([reach] + counts)


def uneven_parts(rng, amount, total, most, lean):
    if amount == 2:
        one = jax.random.randint(rng, (), max(1, total - most), min(most, total - 1) + 1)
        return jnp.stack([one, total - one])
    tallies = jnp.asarray(length_profile(amount, total, most, lean), jnp.int32)
    twos = (amount - 1) // 2
    donor, taker = tallies[1:1 + 2 * twos:2], tallies[2:2 + 2 * twos:2]
    margin = jnp.minimum(donor - 1, most - taker)
    moved = jax.random.randint(jax.random.fold_in(rng, 1), (twos,), 0, 1 << 20) % (margin + 1)
    tallies = tallies.at[1:1 + 2 * twos:2].set(donor - moved).at[2:2 + 2 * twos:2].set(taker + moved)
    return tallies[jax.random.permutation(jax.random.fold_in(rng, 2), amount)]


def normal_values(rng, extent, deviation, most, pieces=(), kind=jnp.bfloat16):
    level = levels(rng, extent, pieces, -0.22, 0.18) if pieces else 1.0
    values = jax.random.normal(rng, extent, jnp.float32) * deviation * level
    return jnp.minimum(jnp.maximum(values, -most), most).astype(kind)


def setup_inputs(seed: int = 0) -> dict:
    seeds = jax.random.split(jax.random.key(seed), 22)
    return {
        "history": draw_history(jax.random.fold_in(seeds[21], 71), 0),
        "cotangent": draw_cotangent(jax.random.fold_in(seeds[21], 71), 0),
        "segments": jax.vmap(lambda own: jnp.searchsorted(jnp.cumsum(uneven_parts(own, max(8, SEQ // 64), SEQ, SEQ // 4, 1)), jnp.arange(SEQ), side="right"))(jax.random.split(seeds[2], SEQS)).reshape((SEQS, SEQ)).astype(jnp.int32),
        "w_attend": normal_values(seeds[3], (3, D, D), D ** -0.5, 0.21875, ((1, 8), (2, 4)), jnp.float32),
        "m_attend": normal_values(seeds[4], (3, D, D), (0.22 * TOKENS ** 0.5), 160.0, ((1, 8), (2, 4)), jnp.float32),
        "v_attend": jnp.clip(jnp.exp(math.log(13107.2) - 1.3862944 * jax.random.uniform(seeds[5], (3, D, D), jnp.float32) ** levels(seeds[5], (3, D, D), ((1, 8), (2, 4)), -0.2, 0.2)), 3276.8, 13107.2),
        "w_output": normal_values(seeds[6], (D, D), (D // 32) ** -0.5, 1.25, ((0, 4), (1, 8)), jnp.float32),
        "m_output": normal_values(seeds[7], (D, D), (0.066 * TOKENS ** 0.5), 48.0, ((0, 4), (1, 8)), jnp.float32),
        "v_output": jnp.clip(jnp.exp(math.log(1245.184) - 1.3862944 * jax.random.uniform(seeds[8], (D, D), jnp.float32) ** levels(seeds[8], (D, D), ((0, 4), (1, 8)), -0.2, 0.2)), 311.296, 1245.184),
        "w_expand": normal_values(seeds[9], (D, FF), D ** -0.5, 0.21875, ((0, 8), (1, 4)), jnp.float32),
        "m_expand": normal_values(seeds[10], (D, FF), (0.13 * TOKENS ** 0.5), 96.0, ((0, 8), (1, 4)), jnp.float32),
        "v_expand": jnp.clip(jnp.exp(math.log(4915.2) - 1.3730492 * jax.random.uniform(seeds[11], (D, FF), jnp.float32) ** levels(seeds[11], (D, FF), ((0, 8), (1, 4)), -0.2, 0.2)), 1245.184, 4915.2),
        "w_reduce": normal_values(seeds[12], (FF, D), (FF // 4) ** -0.5, 0.21875, ((0, 4), (1, 8)), jnp.float32),
        "m_reduce": normal_values(seeds[13], (FF, D), (0.15 * TOKENS ** 0.5), 112.0, ((0, 4), (1, 8)), jnp.float32),
        "v_reduce": jnp.clip(jnp.exp(math.log(6225.92) - 1.335001 * jax.random.uniform(seeds[14], (FF, D), jnp.float32) ** levels(seeds[14], (FF, D), ((0, 4), (1, 8)), -0.2, 0.2)), 1638.4, 6225.92),
        "gains": jnp.clip(1.0 + 0.1 * jax.random.normal(seeds[15], (2, D), jnp.float32), 0.5, 1.5),
        "m_gains": normal_values(seeds[16], (2, D), (0.22 * TOKENS ** 0.5), 160.0, ((1, 4),), jnp.float32),
        "v_gains": jnp.clip(jnp.exp(math.log(13107.2) - 1.3862944 * jax.random.uniform(seeds[17], (2, D), jnp.float32) ** levels(seeds[17], (2, D), ((1, 4),), -0.2, 0.2)), 3276.8, 13107.2),
        "mix": normal_values(seeds[18], (HIST,), 0.3, 4.0, (), jnp.float32),
        "m_mix": normal_values(seeds[19], (HIST,), (0.55 * (TOKENS * D) ** 0.5), 12288.0, (), jnp.float32),
        "v_mix": jnp.clip(jnp.exp(jax.random.uniform(seeds[20], (HIST,), jnp.float32, math.log(16357786), math.log(66689432))), 16357786, 66689432),
    }


@jax.custom_vjp
def low(v):
    return lax.optimization_barrier(v.astype(jnp.bfloat16)).astype(jnp.float32)

@jax.custom_vjp
def low_back(v):
    return v

def low_keep(v):
    return (low(v), None)

def low_pass(kept, grad):
    return (grad,)

def back_keep(v):
    return (v, None)

def back_low(kept, grad):
    return (low(grad),)
low.defvjp(low_keep, low_pass)
low_back.defvjp(back_keep, back_low)
EPS_NORM = 1e-05
EPS_ADAM = 1e-08
BETA_ONE = 0.9
BETA_TWO = 0.95
RATE_MATRIX = 0.02
RATE_OUTPUT = 0.12
RATE_GAIN = 0.4
RATE_MIX = 0.05
DECAY = 0.1
MASKED = -1e+30
HIGHEST = lax.Precision.HIGHEST

def norm_rows(stream, gain):
    centre = lax.optimization_barrier(jnp.mean(stream, -1, keepdims=True))
    spread = lax.optimization_barrier(jnp.mean(stream * stream, -1, keepdims=True)) - centre * centre
    return gain * ((stream - centre) * lax.rsqrt(spread + EPS_NORM))

def rotary(heads_in, cosine, sine):
    halfway = heads_in.shape[-1] // 2
    leading = heads_in[..., :halfway]
    trailing = heads_in[..., halfway:]
    return jnp.concatenate([leading * cosine - trailing * sine, trailing * cosine + leading * sine], -1)

def angles(segments):
    row_length = segments.shape[-1]
    places = jnp.arange(row_length, dtype=jnp.int32)
    changed = jnp.concatenate([jnp.ones_like(segments[:, :1]), (segments[:, 1:] != segments[:, :-1]).astype(jnp.int32)], 1)
    doc_starts = lax.cummax(changed * places[None, :], axis=1)
    position = (places[None, :] - doc_starts).astype(jnp.float32)
    halfway = HEAD // 2
    frequency = jnp.exp(jnp.arange(halfway, dtype=jnp.float32) * (-2.0 * math.log(10000.0) / HEAD))
    turned = position[:, :, None] * frequency[None, None, :]
    return (jnp.cos(turned)[:, :, None, :], jnp.sin(turned)[:, :, None, :])

def allowed_pairs(segment_row):
    places = jnp.arange(segment_row.shape[0], dtype=jnp.int32)
    return (segment_row[:, None] == segment_row[None, :]) & (places[None, :] <= places[:, None])

def attend(entry):
    queries, key_heads, value_heads, segment_row = entry
    scores = jnp.einsum('qhd,khd->hqk', queries, key_heads, precision=HIGHEST) * HEAD ** (-0.5)
    scores = low_back(scores)
    scores = jnp.where(allowed_pairs(segment_row)[None], scores, MASKED)
    weights = jax.nn.softmax(scores, axis=-1)
    return jnp.einsum('hqk,khd->qhd', low(weights), value_heads, precision=HIGHEST)

def forward(params, history_part, segment_rows):
    w_attend, w_output, w_expand, w_reduce, gains, mix = params
    row_count = segment_rows.shape[0]
    stream = jnp.einsum('j,jtc->tc', mix, history_part, precision=HIGHEST)
    normed_one = low(norm_rows(stream, gains[0]))
    projected = low_back(jnp.einsum('td,kde->kte', normed_one, low(w_attend), precision=HIGHEST))
    projected = projected.reshape(3, row_count, SEQ, HEADS, HEAD)
    cosine, sine = angles(segment_rows)
    queries = low(rotary(projected[0], cosine, sine))
    key_heads = low(rotary(projected[1], cosine, sine))
    value_heads = low(projected[2])
    attended = lax.map(jax.checkpoint(attend), (queries, key_heads, value_heads, segment_rows))
    attended = low(low_back(attended)).reshape(row_count * SEQ, D)
    attn_out = low_back(jnp.dot(attended, low(w_output), precision=HIGHEST))
    middle = stream + attn_out
    normed_two = low(norm_rows(middle, gains[1]))
    hidden_in = low_back(jnp.dot(normed_two, low(w_expand), precision=HIGHEST))
    hidden = low(jax.nn.gelu(hidden_in))
    return middle + jnp.dot(hidden, low(w_reduce), precision=HIGHEST)

def optimize(weight, gradient, first_moment, second_moment, rate, decay):
    first_moment = BETA_ONE * first_moment + (1.0 - BETA_ONE) * gradient
    second_moment = BETA_TWO * second_moment + (1.0 - BETA_TWO) * gradient * gradient
    first_fixed = first_moment / (1.0 - BETA_ONE ** STEP)
    second_fixed = second_moment / (1.0 - BETA_TWO ** STEP)
    weight = weight - rate * (first_fixed / (jnp.sqrt(second_fixed) + EPS_ADAM) + decay * weight)
    return (weight, first_moment, second_moment)

def reference(history, cotangent, segments, w_attend, m_attend, v_attend, w_output, m_output, v_output, w_expand, m_expand, v_expand, w_reduce, m_reduce, v_reduce, gains, m_gains, v_gains, mix, m_mix, v_mix):
    params = (w_attend, w_output, w_expand, w_reduce, gains, mix)
    row_group = math.gcd(SEQS, max(1, 4096 // SEQ))
    group_tokens = row_group * SEQ
    group_count = SEQS // row_group

    def scan_body(totals, block_index):
        first_token = block_index * group_tokens
        history_part = jnp.transpose(lax.dynamic_slice_in_dim(history, first_token, group_tokens, 2).astype(jnp.float32), (0, 2, 1))
        cot_part = jnp.transpose(lax.dynamic_slice_in_dim(cotangent, first_token, group_tokens, 1).astype(jnp.float32))
        segment_rows = lax.dynamic_slice_in_dim(segments, block_index * row_group, row_group, 0)
        output, pullback = jax.vjp(lambda weights, past: forward(weights, past, segment_rows), params, history_part)
        gradients, past_grad = pullback(cot_part)
        totals = jax.tree.map(jnp.add, totals, gradients)
        return (totals, (output.astype(jnp.bfloat16), past_grad.astype(jnp.bfloat16)))
    initial = jax.tree.map(jnp.zeros_like, params)
    gradients, (outputs, past_grads) = lax.scan(scan_body, initial, jnp.arange(group_count, dtype=jnp.int32))
    block_output = jnp.transpose(outputs.reshape(TOKENS, D))
    history_grad = jnp.transpose(past_grads, (1, 3, 0, 2)).reshape(HIST, D, TOKENS)
    g_attend, g_output, g_expand, g_reduce, g_gains, g_mix = gradients
    w_attend_new, m_attend_new, v_attend_new = optimize(w_attend, g_attend, m_attend, v_attend, RATE_MATRIX, DECAY)
    w_output_new, m_output_new, v_output_new = optimize(w_output, g_output, m_output, v_output, RATE_OUTPUT, DECAY)
    w_expand_new, m_expand_new, v_expand_new = optimize(w_expand, g_expand, m_expand, v_expand, RATE_MATRIX, DECAY)
    w_reduce_new, m_reduce_new, v_reduce_new = optimize(w_reduce, g_reduce, m_reduce, v_reduce, RATE_MATRIX, DECAY)
    gains_new, m_gains_new, v_gains_new = optimize(gains, g_gains, m_gains, v_gains, RATE_GAIN, 0.0)
    mix_new, m_mix_new, v_mix_new = optimize(mix, g_mix, m_mix, v_mix, RATE_MIX, 0.0)
    return (block_output, history_grad, w_attend_new, m_attend_new, v_attend_new, w_output_new, m_output_new, v_output_new, w_expand_new, m_expand_new, v_expand_new, w_reduce_new, m_reduce_new, v_reduce_new, gains_new, m_gains_new, v_gains_new, mix_new, m_mix_new, v_mix_new)
```

```python
import functools
import math
from types import SimpleNamespace

import jax
import jax.numpy as jnp
from jax import lax
from jax.experimental import pallas as pl
from jax.experimental.pallas import tpu as pltpu
from jax.sharding import PartitionSpec as P

D = 768
HEAD = 64
STEP = 10
HALO = 256
LANES = 128


EPS_NORM = 1e-05
EPS_ADAM = 1e-08
BETA_ONE = 0.9
BETA_TWO = 0.95
RATE_MATRIX = 0.02
RATE_OUTPUT = 0.12
RATE_GAIN = 0.4
RATE_MIX = 0.05
DECAY = 0.1
MASKED = -1e30

MESH = pl.DeviceIdType.MESH
F32 = jnp.float32
BF16 = jnp.bfloat16
MIB = 1 << 20


def optimize(weight, gradient, first_moment, second_moment, rate, decay):
    first_moment = BETA_ONE * first_moment + (1.0 - BETA_ONE) * gradient
    second_moment = BETA_TWO * second_moment + (1.0 - BETA_TWO) * gradient * gradient
    first_fixed = first_moment / (1.0 - BETA_ONE**STEP)
    second_fixed = second_moment / (1.0 - BETA_TWO**STEP)
    weight = weight - rate * (first_fixed / (jnp.sqrt(second_fixed) + EPS_ADAM) + decay * weight)
    return (weight, first_moment, second_moment)


def flip(index, bit):
    return index + bit - 2 * bit * ((index // bit) % 2)


def flips(index, bits):
    for bit in bits:
        index = flip(index, bit)
    return index


def subsets(bits):
    found = [()]
    for bit in bits:
        found = found + [one + (bit,) for one in found]
    return found


def row_bits(rows):
    digits = [1 << place for place in range(rows.bit_length() - 1)]
    return digits[0], digits[1:]


def tiles(count, body):
    def step(at, carry):
        body(at)
        return carry

    lax.fori_loop(0, count, step, 0)


def lane_tile(at, size=LANES, base=0):
    return pl.ds(pl.multiple_of(base + at * size, LANES), size)


def dot(a, b):
    return jnp.dot(a, b, preferred_element_type=F32)


def dot_rows(a, b):
    return lax.dot_general(a, b, (((1,), (1,)), ((), ())), preferred_element_type=F32)


def dot_cols(a, b):
    return lax.dot_general(a, b, (((0,), (0,)), ((), ())), preferred_element_type=F32)


def greet(z, r, width, bits):
    bar = pltpu.get_barrier_semaphore()
    places = [(r, lax.rem(z + k, width)) for k in range(1, width)] + [(flip(r, b), z) for b in bits]
    for place in places:
        pl.semaphore_signal(bar, inc=1, device_id=place, device_id_type=MESH)
    pl.semaphore_wait(bar, len(places))


class Sends:
    def __init__(self, send, recv):
        self.send, self.recv, self.used = send, recv, 0

    def make(self, src, dst, place):
        at = self.used
        self.used += 1
        return pltpu.make_async_remote_copy(
            src_ref=src, dst_ref=dst, send_sem=self.send.at[at], recv_sem=self.recv.at[at],
            device_id=place, device_id_type=MESH,
        )


class Gather:
    def __init__(self, sends, own, full, z, r, width, rows):
        self.core, self.bits = row_bits(rows)
        shard = own.shape[0]
        self.full, self.own, self.z, self.r, self.shard = full, own, z, r, shard

        def block(index):
            return pl.ds(pl.multiple_of(index * shard, 16), shard)

        self.block = block
        self.over_width = [
            sends.make(own, full.at[z, block(r)], (r, lax.rem(z + k, width))) for k in range(1, width)
        ]
        half = width // 2
        self.steps = []
        for step in range(len(self.bits)):
            here = []
            for start, order in ((0, self.bits), (half, self.bits[::-1])):
                for sub in subsets(order[:step]):
                    part = full.at[pl.ds(start, half), block(flips(r, sub))]
                    here.append(sends.make(part, part, (flip(r, order[step]), z)))
            self.steps.append(here)
        last = []
        for sub in subsets(self.bits):
            part = full.at[:, block(flips(r, sub))]
            last.append(sends.make(part, part, (flip(r, self.core), z)))
        self.steps.append(last)

    def start(self):
        for copy in self.over_width:
            copy.start()
        self.full[self.z, self.block(self.r), :] = self.own[...]

    def advance(self, step):
        for copy in self.over_width if step == 0 else self.steps[step - 1]:
            copy.wait_recv()
        if step < len(self.steps):
            for copy in self.steps[step]:
                copy.start()

    def end(self):
        for copy in self.over_width + [one for step in self.steps for one in step]:
            copy.wait_send()

    @staticmethod
    def copies(width, rows):
        bits = rows.bit_length() - 2
        return width - 1 + sum(2 * 2**step for step in range(bits)) + 2**bits


class Scatter:
    def __init__(self, sends, grads, boxes, last_box, final, total, z, r, width, rows):
        self.core, self.bits = row_bits(rows)
        shard = total.shape[0]
        self.grads, self.boxes, self.last_box, self.final, self.total = grads, boxes, last_box, final, total
        self.z, self.width, self.shard = z, width, shard
        half = width // 2
        self.half = half

        def block(index):
            return pl.ds(pl.multiple_of(index * shard, 16), shard)

        self.block = block
        self.r = r
        other = flip(r, self.core)
        self.places = subsets(self.bits)
        self.steps = [
            [
                sends.make(grads.at[:, block(flips(other, sub))], boxes[0].at[at], (other, z))
                for at, sub in enumerate(self.places)
            ]
        ]
        self.where = [{(h, sub): boxes[0].at[at, pl.ds(h * half, half)] for at, sub in enumerate(self.places) for h in (0, 1)}]
        self.box_refs = [None]
        self.orders = (self.bits, self.bits[::-1])
        for step in range(len(self.bits)):
            here, kept, plan = [], {}, []
            for h, order in enumerate(self.orders):
                bit = order[step]
                for at, sub in enumerate(subsets(order[step + 1 :])):
                    far = tuple(sorted(sub + (bit,)))
                    near = tuple(sorted(sub))
                    slot = boxes[step + 1].at[h, at]
                    here.append(sends.make(self.where[step][(h, far)], slot, (flip(r, bit), z)))
                    plan.append((slot, self.where[step][(h, near)], h))
                    kept[(h, near)] = slot
            self.steps.append(here)
            self.where.append(kept)
            self.box_refs.append(plan)
        self.over_width = [
            sends.make(final.at[lax.rem(z + k, width)], last_box.at[k - 1], (r, lax.rem(z + k, width)))
            for k in range(1, width)
        ]

    def start(self):
        for copy in self.steps[0]:
            copy.start()

    def advance(self, step):
        for copy in self.steps[step]:
            copy.wait_recv()
        if step == 0:
            for at, sub in enumerate(self.places):
                rows = self.block(flips(self.r, sub))

                def add(w, at=at, rows=rows):
                    box = self.boxes[0].at[at, w]
                    box[...] = (box[...].astype(F32) + self.grads[w, rows, :].astype(F32)).astype(BF16)

                tiles(self.width, add)
        else:
            is_last = step == len(self.bits)
            for slot, kept, h in self.box_refs[step]:
                for w in range(self.half):
                    value = slot[w].astype(F32) + kept[w].astype(F32)
                    if is_last:
                        self.final[h * self.half + w] = value.astype(BF16)
                    else:
                        slot[w] = value.astype(BF16)
        following = self.over_width if step == len(self.bits) else self.steps[step + 1]
        for copy in following:
            copy.start()

    def finish(self):
        for copy in self.over_width:
            copy.wait_recv()
        value = self.final[self.z].astype(F32)
        for k in range(self.width - 1):
            value = value + self.last_box[k].astype(F32)
        self.total[...] = value

    def end(self):
        for copy in self.over_width + [one for step in self.steps for one in step]:
            copy.wait_send()

    @staticmethod
    def copies(width, rows):
        bits = rows.bit_length() - 2
        return width - 1 + sum(2 * 2 ** (bits - 1 - step) for step in range(bits)) + 2**bits

    @staticmethod
    def box_shapes(width, rows, shard):
        bits = rows.bit_length() - 2
        shapes = [(2**bits, width, shard, D)]
        for step in range(bits):
            shapes.append((2, 2 ** (bits - 1 - step), width // 2, shard, D))
        return shapes


def mix_stream(mix_ref, pair_ref, out_ref, base, layers):
    features, size = pair_ref.shape[1], pair_ref.shape[2]
    strip = 16

    def body(at):
        rows = pl.ds(pl.multiple_of(at * strip, strip), strip)
        total = mix_ref[0] * pair_ref[0, rows, :].astype(F32)
        for j in range(1, layers):
            total = total + mix_ref[j] * pair_ref[j, rows, :].astype(F32)
        out_ref[rows, base] = total.astype(BF16)

    tiles(features // strip, body)


def spread_gains(box_ref, gain_ref, width, piece):
    for w in range(width):
        for i in range(2):
            row = box_ref[w, pl.ds(i, 1), :]
            full = jnp.transpose(jnp.broadcast_to(row, (LANES, row.shape[1])))
            gain_ref[i, pl.ds(w * piece, piece), :] = full[:piece]


def norm_forward(x_ref, x_base, gain_ref, i, out_ref, stat_ref, count):
    def body(at):
        cols = lane_tile(at)
        x = x_ref[:, lane_tile(at, base=x_base)].astype(F32)
        centre = jnp.sum(x, 0, keepdims=True) / D
        spread = jnp.sum(x * x, 0, keepdims=True) / D - centre * centre
        scaling = lax.rsqrt(spread + EPS_NORM)
        out_ref[:, cols] = (gain_ref[i] * ((x - centre) * scaling)).astype(BF16)
        stat_ref[0:1, cols] = centre
        stat_ref[1:2, cols] = scaling

    tiles(count // LANES, body)


def norm_back(u_ref, u_base, x_ref, x_base, stat_ref, stat_base, gain_ref, i, residual, write, gain_acc, count):
    gain_acc[...] = jnp.zeros_like(gain_acc)

    def body(at):
        u = u_ref[:, lane_tile(at, base=u_base)].astype(F32)
        x = x_ref[:, lane_tile(at, base=x_base)].astype(F32)
        cols = lane_tile(at, base=stat_base)
        scaling = stat_ref[1:2, cols]
        centred = (x - stat_ref[0:1, cols]) * scaling
        gain_acc[...] += u * centred
        s = u * gain_ref[i]
        mean_s = jnp.sum(s, 0, keepdims=True) / D
        mean_c = jnp.sum(s * centred, 0, keepdims=True) / D
        write(lane_tile(at), residual(lane_tile(at)) + scaling * (s - mean_s - centred * mean_c))

    tiles(count // LANES, body)


def document_starts(seg_ref, start_ref, trig_ref, row, own_at, own):
    seg = seg_ref[pl.ds(row, 1), :]
    length = seg.shape[1]
    place = lax.broadcasted_iota(jnp.int32, (8, length), 1)
    seg = jnp.broadcast_to(seg, (8, length))
    before = pltpu.roll(seg, 1, 1)
    start = jnp.where((place > 0) & (seg == before), 0, place)
    step = 1
    while step < length:
        moved = pltpu.roll(start, step, 1)
        start = jnp.maximum(start, jnp.where(place >= step, moved, 0))
        step *= 2
    position = (place - start).astype(F32)
    scratch = start_ref.at[0:8]
    ext = HALO + own
    scratch[:, pl.ds(0, HALO)] = jnp.zeros((8, HALO), F32)
    scratch[:, pl.ds(HALO, length)] = position
    window = scratch[:, pl.ds(pl.multiple_of(own_at, LANES), ext)][0:1]
    half = HEAD // 2
    freq = jnp.exp(
        lax.broadcasted_iota(jnp.int32, (half, ext), 0).astype(F32) * (-2.0 * math.log(10000.0) / HEAD)
    )
    angle = freq * window
    trig_ref[0] = jnp.cos(angle)
    trig_ref[1] = jnp.sin(angle)
    scratch[:, pl.ds(HALO, length)] = start.astype(F32)
    kept = scratch[:, pl.ds(pl.multiple_of(own_at, LANES), ext)]
    scratch[:, pl.ds(0, ext)] = kept - (own_at - HALO).astype(F32)


def rotated(heads, cosine, sine):
    half = HEAD // 2
    a, b = heads[:half], heads[half:]
    return jnp.concatenate([a * cosine - b * sine, b * cosine + a * sine], 0)


def project(x_ref, wa_ref, trig_ref, q_ref, k_ref, v_ref, wo_ref, width, per, own):
    ext = HALO + own
    group = per * HEAD
    scale = HEAD**-0.5

    def body(w):
        turned = jnp.transpose(wa_ref[w])
        wo_ref[w] = turned[3 * group :]
        queries = dot(turned[:group], x_ref[:, HALO:])
        cosine, sine = trig_ref[0], trig_ref[1]
        for i in range(per):
            rows = queries[i * HEAD : (i + 1) * HEAD]
            q_ref[w * per + i] = (rotated(rows, cosine[:, HALO:], sine[:, HALO:]).astype(BF16) * scale).astype(BF16)
        keys = dot(turned[group : 2 * group], x_ref[...])
        for i in range(per):
            rows = keys[i * HEAD : (i + 1) * HEAD]
            k_ref[w * per + i] = rotated(rows, cosine, sine).astype(BF16)
        values = dot(turned[2 * group : 3 * group], x_ref[...])
        for i in range(per):
            v_ref[w * per + i] = values[i * HEAD : (i + 1) * HEAD].astype(BF16)

    tiles(width, body)


def attend(q_ref, k_ref, v_ref, start_ref, bias_ref, p_ref, ao_ref, width, per, own):
    blocks = own // HALO
    for b in range(blocks):
        key_at = lax.broadcasted_iota(jnp.int32, (2 * HALO, HALO), 0).astype(F32) + float(b * HALO)
        query_at = lax.broadcasted_iota(jnp.int32, (2 * HALO, HALO), 1).astype(F32) + float((b + 1) * HALO)
        first = start_ref[0:1, (b + 1) * HALO : (b + 2) * HALO]
        bias_ref[b] = jnp.where((key_at >= first) & (key_at <= query_at), 0.0, MASKED)

    def body(w):
        ao_ref[w, 0:HEAD, :] = jnp.zeros((HEAD, own), BF16)
        for i in range(per):
            h = w * per + i
            for b in range(blocks):
                keys = k_ref[h, :, b * HALO : (b + 2) * HALO]
                scores = dot_cols(keys, q_ref[h, :, b * HALO : (b + 1) * HALO]) + bias_ref[b]
                top = jnp.max(scores, 0, keepdims=True)
                raised = jnp.exp(scores - top)
                total = jnp.sum(raised, 0, keepdims=True)
                p_ref[h, b] = (raised * (1.0 / total)).astype(BF16)
                out = dot(v_ref[h, :, b * HALO : (b + 2) * HALO], p_ref[h, b])
                ao_ref[w, (i + 1) * HEAD : (i + 2) * HEAD, b * HALO : (b + 1) * HALO] = out.astype(BF16)

    tiles(width, body)


def out_project(st_ref, wa_ref, ao_ref, mid_ref, width, per):
    group = 3 * per * HEAD - HEAD
    mid_ref[...] = st_ref[:, HALO:].astype(F32)

    def body(w):
        mid_ref[...] += dot(wa_ref[w, :, group:], ao_ref[w])

    tiles(width, body)


def feed_forward(x_ref, ct_ref, wb_ref, wc_ref, gb_ref, gc_ref, acc_ref, u_ref, xt_ref, ctt_ref, pre_ref, gh_ref, hid_ref, gi_ref, width):
    own = x_ref.shape[1]
    xt_ref[...] = jnp.transpose(x_ref[...])
    ctt_ref[...] = jnp.transpose(ct_ref[...])
    u_ref[...] = jnp.zeros_like(u_ref)
    strip = 32

    def body(w):
        pre_ref[...] = dot(xt_ref[...], wb_ref[w])
        gh_ref[...] = dot(ctt_ref[...], wc_ref[w])

        def gelu(at):
            rows = pl.ds(pl.multiple_of(at * strip, strip), strip)
            x = pre_ref[rows, :]
            root = math.sqrt(2.0 / math.pi)
            square = x * x
            bent = jnp.tanh(root * (x + 0.044715 * (square * x)))
            hid_ref[rows, :] = (0.5 * x * (1.0 + bent)).astype(BF16)
            slope = 0.5 * (1.0 + bent) + (0.5 * root) * x * (1.0 - bent * bent) * (1.0 + (3 * 0.044715) * square)
            gi_ref[rows, :] = (gh_ref[rows, :] * slope).astype(BF16)

        tiles(own // strip, gelu)
        acc_ref[...] += dot_rows(wc_ref[w], hid_ref[...])
        gc_ref[w] = dot(ct_ref[...], hid_ref[...]).astype(BF16)
        u_ref[...] += dot_rows(wb_ref[w], gi_ref[...])
        gb_ref[w] = dot(x_ref[...], gi_ref[...]).astype(BF16)

    tiles(width, body)


def attend_back(low_ref, wo_ref, p_ref, q_ref, k_ref, v_ref, trig_ref, gp_ref, width, per, own):
    ext = HALO + own
    group = per * HEAD
    blocks = own // HALO
    scale = HEAD**-0.5

    def body(w):
        gp_ref[w, 3 * group :, :] = jnp.zeros((group, ext), BF16)
        gp_ref[w, :group, :HALO] = jnp.zeros((group, HALO), BF16)
        upstream = dot(wo_ref[w], low_ref[...]).astype(BF16)
        for i in range(per):
            h = w * per + i
            grad_keys, grad_values = [None] * (blocks + 1), [None] * (blocks + 1)
            for b in range(blocks):
                q = q_ref[h, :, b * HALO : (b + 1) * HALO]
                k = k_ref[h, :, b * HALO : (b + 2) * HALO]
                v = v_ref[h, :, b * HALO : (b + 2) * HALO]
                up = upstream[i * HEAD : (i + 1) * HEAD, b * HALO : (b + 1) * HALO]
                weights = p_ref[h, b]
                wide = weights.astype(F32)
                grad_weights = dot_cols(v, up)
                inner = jnp.sum(wide * grad_weights, 0, keepdims=True)
                grad_scores = (wide * (grad_weights - inner)).astype(BF16)
                gv = dot_rows(up, weights)
                gk = dot_rows(q, grad_scores)
                gq = dot(k, grad_scores) * scale
                cols = slice((b + 1) * HALO, (b + 2) * HALO)
                gp_ref[w, i * HEAD : (i + 1) * HEAD, cols] = rotated(gq, trig_ref[0, :, cols], -trig_ref[1, :, cols]).astype(BF16)
                for part in range(2):
                    piece = slice(part * HALO, (part + 1) * HALO)
                    at = b + part
                    grad_keys[at] = gk[:, piece] if grad_keys[at] is None else grad_keys[at] + gk[:, piece]
                    grad_values[at] = gv[:, piece] if grad_values[at] is None else grad_values[at] + gv[:, piece]
            for at in range(blocks + 1):
                cols = slice(at * HALO, (at + 1) * HALO)
                gp_ref[w, group + i * HEAD : group + (i + 1) * HEAD, cols] = rotated(
                    grad_keys[at], trig_ref[0, :, cols], -trig_ref[1, :, cols]
                ).astype(BF16)
                gp_ref[w, 2 * group + i * HEAD : 2 * group + (i + 1) * HEAD, cols] = grad_values[at].astype(BF16)

    tiles(width, body)


def project_back(x_ref, low_ref, ao_ref, wa_ref, gp_ref, ga_ref, u_ref, width, per):
    group = 3 * per * HEAD - HEAD
    u_ref[...] = jnp.zeros_like(u_ref)

    def body(w):
        u_ref[...] += dot(wa_ref[w], gp_ref[w])
        ga_ref[w, :, :group] = dot_rows(x_ref[...], gp_ref[w, :group, :]).astype(BF16)
        ga_ref[w, :, group:] = (
            dot_rows(x_ref[...], gp_ref[w, group:, :]) + dot_rows(low_ref[...], ao_ref[w])
        ).astype(BF16)

    tiles(width, body)


def bring_kernel(width, rows, mix_ref, hist_ref, cot_ref, own_ref, box_ref, st_ref, ct_ref, full_ref, boxes_ref,
                 pair, mixed, load_sem, here_sem, send_sem, recv_sem):
    r, z = lax.axis_index("rows"), lax.axis_index("width")
    layers, piece, tokens = hist_ref.shape
    own = tokens // width
    _, bits = row_bits(rows)
    greet(z, r, width, [1] + bits)
    sends = Sends(send_sem, recv_sem)
    gathers = []
    if own_ref is not None:
        gathers = [Gather(sends, own_ref.at[x], full_ref.at[x], z, r, width, rows) for x in range(3)]
    first = 1 - z // 2
    chunks = []
    for at in range(width):
        low = flip(first, 1) if at // 2 else first
        chunks.append(2 * low + at % 2)
    loads = []
    for at in range(width):
        cols = pl.ds(pl.multiple_of(chunks[at] * own, LANES), own)
        load = pltpu.make_async_copy(hist_ref.at[:, :, cols], pair.at[at], load_sem.at[at])
        load.start()
        loads.append(load)
    if gathers:
        gathers[0].start()
    mine = pl.ds(pl.multiple_of(z * piece, 16), piece)
    st_even = st_ref.at[mine, pl.ds(HALO, own)]
    st_odd = st_ref.at[mine, :]
    gain_sends = [sends.make(box_ref, boxes_ref.at[z], (r, lax.rem(z + k, width))) for k in range(1, width)]
    for copy in gain_sends:
        copy.start()
    boxes_ref[z] = box_ref[...]
    base = sends.used
    sends.used += width - 1

    def stream_copy(k, target, odd, start):
        if odd:
            src = mixed.at[:, pl.ds(pl.multiple_of(start - HALO, LANES), HALO + own)]
            dst = st_odd
        else:
            src = mixed.at[:, pl.ds(pl.multiple_of(start, LANES), own)]
            dst = st_even
        return pltpu.make_async_remote_copy(
            src_ref=src, dst_ref=dst, send_sem=send_sem.at[base + k - 1], recv_sem=recv_sem.at[base + k - 1],
            device_id=(r, target), device_id_type=MESH,
        )

    for at in range(width):
        target = chunks[at]
        start = pl.multiple_of(target * own, LANES)
        loads[at].wait()
        mix_stream(mix_ref, pair.at[at], mixed, pl.ds(start, own), layers)
        odd = at % 2 == 1
        for k in range(1, width):
            @pl.when(lax.rem(z + k, width) == target)
            def _(k=k, target=target, odd=odd, start=start):
                stream_copy(k, target, odd, start).start()

        @pl.when(target == z)
        def _(odd=odd, start=start):
            if odd:
                st_odd[...] = mixed[:, pl.ds(pl.multiple_of(start - HALO, LANES), HALO + own)]
            else:
                st_even[...] = mixed[:, pl.ds(start, own)]
                st_ref[:, 0:HALO] = jnp.zeros((D, HALO), BF16)

    for gather in gathers[1:]:
        gather.start()
    cot_sends = []
    for k in range(1, width):
        target = lax.rem(z + k, width)
        cols = pl.ds(pl.multiple_of(target * own, LANES), own)
        cot_sends.append(sends.make(cot_ref.at[:, cols], ct_ref.at[mine, :], (r, target)))
    for copy in cot_sends:
        copy.start()
    cot_here = pltpu.make_async_copy(
        cot_ref.at[:, pl.ds(pl.multiple_of(z * own, LANES), own)], ct_ref.at[mine, :], here_sem
    )
    cot_here.start()
    for step in range(len(bits) + 2):
        for gather in gathers:
            gather.advance(step)
    for k in range(1, width):
        for odd in (False, True):
            @pl.when(lax.rem(z, 2) == int(odd))
            def _(k=k, odd=odd):
                stream_copy(k, lax.rem(z + k, width), odd, HALO if odd else 0).wait_recv()

            @pl.when(lax.rem(z + k, 2) == int(odd))
            def _(k=k, odd=odd):
                stream_copy(k, lax.rem(z + k, width), odd, HALO if odd else 0).wait_send()
    cot_here.wait()
    for copy in gain_sends + cot_sends:
        copy.wait()
    for gather in gathers:
        gather.end()


def middle_kernel(width, per, seg_ref, st_ref, ct_ref, full_ref, boxes_ref,
                  blk_ref, gmid_ref, u_ref, ga_ref, gb_ref, gc_ref, gain_ref, gacc_ref, stat_ref,
                  x_ref, start_ref, trig, q_ref, k_ref, v_ref, wo_ref, bias, prob, ao, mid, stat_two, u_two, low):
    z = lax.axis_index("width")
    own = ct_ref.shape[1]
    per_row = seg_ref.shape[1] // own
    spread_gains(boxes_ref, gain_ref, width, D // width)
    document_starts(seg_ref, start_ref, trig, z // per_row, lax.rem(z, per_row) * own, own)
    norm_forward(st_ref, 0, gain_ref, 0, x_ref, stat_ref, HALO + own)
    project(x_ref, full_ref.at[0], trig, q_ref, k_ref, v_ref, wo_ref, width, per, own)
    attend(q_ref, k_ref, v_ref, start_ref, bias, prob, ao, width, per, own)
    out_project(st_ref, full_ref.at[0], ao, mid, width, per)
    gmid_ref[...] = mid[...]

    def inner(x_two, xt, ctt, pre, gh, hid, gi):
        norm_forward(mid, 0, gain_ref, 1, x_two, stat_two, own)
        feed_forward(x_two, ct_ref, full_ref.at[1], full_ref.at[2], gb_ref, gc_ref, gmid_ref, u_two, xt, ctt, pre, gh, hid, gi, width)

    pl.run_scoped(
        inner, pltpu.VMEM((D, own), BF16), pltpu.VMEM((own, D), BF16), pltpu.VMEM((own, D), BF16), pltpu.VMEM((own, D), F32),
        pltpu.VMEM((own, D), F32), pltpu.VMEM((own, D), BF16), pltpu.VMEM((own, D), BF16),
    )
    blk_ref[...] = gmid_ref[...].astype(BF16)

    def write(cols, value):
        gmid_ref[:, cols] = value
        low[:, cols] = value.astype(BF16)

    norm_back(u_two, 0, mid, 0, stat_two, 0, gain_ref, 1, lambda cols: ct_ref[:, cols].astype(F32), write, gacc_ref, own)

    def last(gp):
        attend_back(low, wo_ref, prob, q_ref, k_ref, v_ref, trig, gp, width, per, own)
        project_back(x_ref, low, ao, full_ref.at[0], gp, ga_ref, u_ref, width, per)

    pl.run_scoped(last, pltpu.VMEM((width, 4 * per * HEAD, HALO + own), BF16))


def return_kernel(width, rows, mix_ref, hist_ref, u_ref, gmid_ref, st_ref, stat_ref, gain_ref, gtwo_ref, blk_ref,
                  ga_ref, gb_ref, gc_ref, hgrad_ref, bout_ref, total_ref, small_ref,
                  pair, uh, halo_out, halo_in, gs, gcol, gone, macc, small_out, small_in, small_step,
                  final, last_box, boxes, load_sem, store_sem, here_sem, send_sem, recv_sem):
    r, z = lax.axis_index("rows"), lax.axis_index("width")
    layers, piece, tokens = hist_ref.shape
    own = tokens // width
    core, bits = row_bits(rows)
    greet(z, r, width, [1] + bits)
    sends = Sends(send_sem, recv_sem)
    loads, order = [], []
    for k in range(width):
        chunk = lax.rem(z + width - k, width)
        cols = pl.ds(pl.multiple_of(chunk * own, LANES), own)
        load = pltpu.make_async_copy(hist_ref.at[:, :, cols], pair.at[k], load_sem.at[k])
        load.start()
        loads.append(load)
        order.append(cols)
    scatters = []
    if total_ref is not None:
        scatters = [
            Scatter(sends, grads, [box.at[x] for box in boxes], last_box.at[x], final.at[x], total_ref.at[x], z, r, width, rows)
            for x, grads in ((2, gc_ref), (1, gb_ref), (0, ga_ref))
        ]
    odd = lax.rem(z, 2) == 1
    halo = sends.make(halo_out, halo_in, (r, flip(z, 1)))

    @pl.when(odd)
    def _():
        halo_out[...] = u_ref[:, 0:HALO].astype(BF16)
        halo.start()

    for scatter in scatters:
        scatter.start()
    uh[...] = u_ref[:, HALO:]

    @pl.when(jnp.logical_not(odd))
    def _():
        halo.wait_recv()
        uh[:, own - HALO : own] += halo_in[...].astype(F32)

    def write(cols, value):
        gs[:, cols] = value.astype(BF16)

    norm_back(uh, 0, st_ref, HALO, stat_ref, HALO, gain_ref, 0, lambda cols: gmid_ref[:, cols], write, gone, own)
    gs_sends, blk_sends = [], []
    mine = pl.ds(pl.multiple_of(z * own, LANES), own)
    for k in range(1, width):
        target = lax.rem(z + k, width)
        part = pl.ds(pl.multiple_of(target * piece, 16), piece)
        gs_sends.append(sends.make(gs.at[part, :], gcol.at[k], (r, target)))
        blk_sends.append(sends.make(blk_ref.at[part, :], bout_ref.at[:, mine], (r, target)))
    for copy in gs_sends + blk_sends:
        copy.start()
    part = pl.ds(pl.multiple_of(z * piece, 16), piece)
    bout_ref[:, mine] = blk_ref[part, :]
    gcol[0] = gs[part, :]
    macc[...] = jnp.zeros_like(macc)
    strip = 16
    stores = []
    for k in range(width):
        if k:
            gs_sends[k - 1].wait_recv()
        loads[k].wait()

        def body(at, k=k):
            cut = pl.ds(pl.multiple_of(at * strip, strip), strip)
            g = gcol[k, cut, :].astype(F32)
            for j in range(layers):
                crossed = pair[k, j, cut, :].astype(F32) * g
                folded = crossed[:8] + crossed[8:]
                part = folded[:, :LANES]
                for lane in range(1, own // LANES):
                    part = part + folded[:, lane * LANES : (lane + 1) * LANES]
                macc[j] += part
                pair[k, j, cut, :] = (mix_ref[j] * g).astype(BF16)

        tiles(piece // strip, body)
        store = pltpu.make_async_copy(pair.at[k], hgrad_ref.at[:, :, order[k]], store_sem.at[k])
        store.start()
        stores.append(store)
        if k <= len(bits):
            for scatter in scatters:
                scatter.advance(k)
    for step in range(width, len(bits) + 1):
        for scatter in scatters:
            scatter.advance(step)
    small_out[...] = jnp.zeros_like(small_out)
    first = jnp.sum(jnp.transpose(gone[...]), 0, keepdims=True)
    second = jnp.sum(jnp.transpose(gtwo_ref[...]), 0, keepdims=True)
    summed = jnp.sum(macc[...], 1)
    depth = jnp.sum(jnp.transpose(summed), 0, keepdims=True)
    for w in range(width):
        small_out[w, 0:1, 0:piece] = first[:, w * piece : (w + 1) * piece]
        small_out[w, 1:2, 0:piece] = second[:, w * piece : (w + 1) * piece]
        small_out[w, 2:3, 0 : depth.shape[1]] = depth
    small_sends = [
        sends.make(small_out.at[lax.rem(z + k, width)], small_in.at[k - 1], (r, lax.rem(z + k, width))) for k in range(1, width)
    ]
    for copy in small_sends:
        copy.start()
    current = small_out[z]
    for k in range(1, width):
        small_sends[k - 1].wait_recv()
        current = current + small_in[k - 1]
    for at, bit in enumerate([core] + bits):
        small_step[at, 0] = current
        copy = sends.make(small_step.at[at, 0], small_step.at[at, 1], (flip(r, bit), z))
        copy.start()
        copy.wait_recv()
        current = current + small_step[at, 1]
        small_sends.append(copy)
    small_ref[...] = current
    for scatter in scatters:
        scatter.finish()
    for copy in blk_sends:
        copy.wait_recv()
    for copy in gs_sends + blk_sends + small_sends:
        copy.wait_send()

    @pl.when(odd)
    def _():
        halo.wait_send()

    for scatter in scatters:
        scatter.end()
    for store in stores:
        store.wait()


def vmem(count):
    return [pl.BlockSpec(memory_space=pltpu.VMEM)] * count


def shape(*sizes, dtype=F32):
    return jax.ShapeDtypeStruct(sizes, dtype)


def bring(width, rows, mix, history, cotangent, own_three, box):
    layers, piece, tokens = history.shape
    own = tokens // width
    inside = own_three.shape[1] % 16 == 0
    count = (width - 1) * 3 + 3 * Gather.copies(width, rows) + 4
    any_space = pl.BlockSpec(memory_space=pl.ANY)
    outs = [shape(D, HALO + own, dtype=BF16), shape(D, own, dtype=BF16), shape(width, 8, 2 * LANES)]
    if inside:
        outs.append(shape(3, width, D, D, dtype=BF16))

    def kernel(mix_ref, hist_ref, cot_ref, own_ref, box_ref, st, ct, boxes, *rest):
        full, rest = (rest[0], rest[1:]) if inside else (None, rest)
        bring_kernel(width, rows, mix_ref, hist_ref, cot_ref, own_ref if inside else None, box_ref, st, ct, full, boxes, *rest)

    found = pl.pallas_call(
        kernel,
        out_shape=outs,
        in_specs=[pl.BlockSpec(memory_space=pltpu.SMEM), any_space] + vmem(3),
        out_specs=vmem(len(outs)),
        scratch_shapes=[
            pltpu.VMEM((width, layers, piece, own), BF16),
            pltpu.VMEM((piece, tokens), BF16),
            pltpu.SemaphoreType.DMA((width,)),
            pltpu.SemaphoreType.DMA,
            pltpu.SemaphoreType.DMA((count,)),
            pltpu.SemaphoreType.DMA((count,)),
        ],
        compiler_params=pltpu.CompilerParams(collective_id=0, has_side_effects=True, vmem_limit_bytes=60 * MIB),
    )(mix, history, cotangent, own_three, box)
    if inside:
        return found
    full = lax.all_gather(lax.all_gather(own_three, "rows", axis=1, tiled=True), "width", axis=1)
    return (*found, full)


def middle(width, segments, st, ct, boxes, full):
    own = ct.shape[1]
    ext = HALO + own
    heads = D // HEAD
    per = heads // width
    group = per * HEAD
    blocks = own // HALO
    outs = [
        shape(D, own, dtype=BF16), shape(D, own), shape(D, ext),
        shape(width, D, D, dtype=BF16), shape(width, D, D, dtype=BF16), shape(width, D, D, dtype=BF16),
        shape(2, D, LANES), shape(D, LANES), shape(8, ext),
    ]
    scratch = [
        pltpu.VMEM((D, ext), BF16), pltpu.VMEM((8, HALO + segments.shape[1]), F32), pltpu.VMEM((2, HEAD // 2, ext), F32),
        pltpu.VMEM((heads, HEAD, own), BF16), pltpu.VMEM((heads, HEAD, ext), BF16), pltpu.VMEM((heads, HEAD, ext), BF16),
        pltpu.VMEM((width, group, D), BF16), pltpu.VMEM((blocks, 2 * HALO, HALO), F32),
        pltpu.VMEM((heads, blocks, 2 * HALO, HALO), BF16), pltpu.VMEM((width, HEAD + group, own), BF16),
        pltpu.VMEM((D, own), F32), pltpu.VMEM((8, own), F32), pltpu.VMEM((D, own), F32), pltpu.VMEM((D, own), BF16),
    ]
    return pl.pallas_call(
        functools.partial(middle_kernel, width, per),
        out_shape=outs,
        in_specs=vmem(5),
        out_specs=vmem(len(outs)),
        scratch_shapes=scratch,
        compiler_params=pltpu.CompilerParams(vmem_limit_bytes=62 * MIB),
    )(segments, st, ct, full, boxes)


def give_back(width, rows, shard, mix, history, u, gmid, st, stat, gain, gtwo, blk, ga, gb, gc):
    layers, piece, tokens = history.shape
    own = tokens // width
    inside = shard % 16 == 0
    row_digits = rows.bit_length() - 1
    count = 3 * Scatter.copies(width, rows) + 1 + 3 * (width - 1) + row_digits
    any_space = pl.BlockSpec(memory_space=pl.ANY)
    outs = [shape(*history.shape, dtype=BF16), shape(piece, tokens, dtype=BF16), shape(8, 2 * LANES)]
    specs = [any_space] + vmem(2)
    box_shapes = []
    if inside:
        outs.append(shape(3, shard, D))
        specs += vmem(1)
        box_shapes = Scatter.box_shapes(width, rows, shard)
    ins = [mix, history, u, gmid, st, stat, gain, gtwo, blk] + ([ga, gb, gc] if inside else [])

    def kernel(*refs):
        given, rest = refs[: len(ins)], refs[len(ins) :]
        hgrad, bout, small = rest[:3]
        rest = rest[3:]
        total, grads = None, (None, None, None)
        final, last_box, boxes = None, None, ()
        if inside:
            total, rest = rest[0], rest[1:]
            grads = given[9:]
        common, rest = rest[:11], rest[11:]
        if inside:
            final, last_box = rest[:2]
            boxes = rest[2 : 2 + len(box_shapes)]
            rest = rest[2 + len(box_shapes) :]
        return_kernel(width, rows, *given[:9], *grads, hgrad, bout, total, small, *common, final, last_box, boxes, *rest)

    scratch = [
        pltpu.VMEM((width, layers, piece, own), BF16),
        pltpu.VMEM((D, own), F32),
        pltpu.VMEM((D, HALO), BF16),
        pltpu.VMEM((D, HALO), BF16),
        pltpu.VMEM((D, own), BF16),
        pltpu.VMEM((width, piece, own), BF16),
        pltpu.VMEM((D, LANES), F32),
        pltpu.VMEM((layers, 8, LANES), F32),
        pltpu.VMEM((width, 8, 2 * LANES), F32),
        pltpu.VMEM((width - 1, 8, 2 * LANES), F32),
    ]
    scratch.append(pltpu.VMEM((row_digits, 2, 8, 2 * LANES), F32))
    if inside:
        scratch += [pltpu.VMEM((3, width, shard, D), BF16), pltpu.VMEM((3, width - 1, shard, D), BF16)]
        scratch += [pltpu.VMEM((3, *one), BF16) for one in box_shapes]
    scratch += [
        pltpu.SemaphoreType.DMA((width,)), pltpu.SemaphoreType.DMA((width,)), pltpu.SemaphoreType.DMA,
        pltpu.SemaphoreType.DMA((count,)), pltpu.SemaphoreType.DMA((count,)),
    ]
    found = pl.pallas_call(
        kernel,
        out_shape=outs,
        in_specs=[pl.BlockSpec(memory_space=pltpu.SMEM), any_space] + vmem(len(ins) - 2),
        out_specs=specs,
        scratch_shapes=scratch,
        compiler_params=pltpu.CompilerParams(collective_id=1, has_side_effects=True, vmem_limit_bytes=63 * MIB),
    )(*ins)
    if inside:
        return found
    total = lax.psum_scatter(jnp.stack([ga, gb, gc], 1), "width", scatter_dimension=0)
    return (*found, lax.psum_scatter(total, "rows", scatter_dimension=1, tiled=True).astype(F32))


def on_device(
    width, rows, history, cotangent, segments, w_attend, m_attend, v_attend, w_output, m_output, v_output,
    w_expand, m_expand, v_expand, w_reduce, m_reduce, v_reduce, gains, m_gains, v_gains, mix, m_mix, v_mix,
):
    layers, piece, _ = history.shape
    own_three = jnp.stack([
        jnp.concatenate([w_attend[0], w_attend[1], w_attend[2], jnp.transpose(w_output)], 1),
        w_expand,
        jnp.transpose(w_reduce),
    ]).astype(BF16)
    shard = own_three.shape[1]
    box = jnp.pad(gains, ((0, 8 - gains.shape[0]), (0, 2 * LANES - piece)))
    st, ct, boxes, full = bring(width, rows, mix, history, cotangent, own_three, box)
    blk, gmid, u, ga, gb, gc, gain, gtwo, stat = middle(width, segments, st, ct, boxes, full)
    history_grad, block_output, small, total = give_back(
        width, rows, shard, mix, history, u, gmid, st, stat, gain, gtwo, blk, ga, gb, gc
    )
    first = total[0]
    sum_attend = jnp.stack([first[:, k * piece : (k + 1) * piece] for k in range(3)])
    sum_output = jnp.transpose(first[:, 3 * piece :])
    new_attend = optimize(w_attend, sum_attend, m_attend, v_attend, RATE_MATRIX, DECAY)
    new_output = optimize(w_output, sum_output, m_output, v_output, RATE_OUTPUT, DECAY)
    new_expand = optimize(w_expand, total[1], m_expand, v_expand, RATE_MATRIX, DECAY)
    new_reduce = optimize(w_reduce, jnp.transpose(total[2]), m_reduce, v_reduce, RATE_MATRIX, DECAY)
    new_gains = optimize(gains, small[0:2, :piece], m_gains, v_gains, RATE_GAIN, 0.0)
    new_mix = optimize(mix, small[2, :layers], m_mix, v_mix, RATE_MIX, 0.0)
    return (block_output, history_grad, *new_attend, *new_output, *new_expand, *new_reduce, *new_gains, *new_mix)


def solution(mesh):
    square, tall, wide = P(None, "rows", "width"), P("width", "rows"), P("rows", "width")
    weights = (square,) * 3 + (tall,) * 3 + (wide,) * 3 + (tall,) * 3 + (P(None, "width"),) * 3 + (P(),) * 3
    return jax.shard_map(
        functools.partial(on_device, mesh.shape["width"], mesh.shape["rows"]),
        mesh=mesh,
        in_specs=(P(None, "width", "rows"), P("width", "rows"), P("rows", None)) + weights,
        out_specs=(P("width", "rows"), P(None, "width", "rows")) + weights,
        check_vma=False,
    )
```

```python
import functools
import math
from types import SimpleNamespace

import jax
import jax.numpy as jnp
from jax import lax
from jax.experimental import pallas as pl
from jax.experimental.pallas import tpu as pltpu
from jax.sharding import PartitionSpec as P

D = 768
HEAD = 64
STEP = 10
HALO = 256
LANES = 128


EPS_NORM = 1e-05
EPS_ADAM = 1e-08
BETA_ONE = 0.9
BETA_TWO = 0.95
RATE_MATRIX = 0.02
RATE_OUTPUT = 0.12
RATE_GAIN = 0.4
RATE_MIX = 0.05
DECAY = 0.1
MASKED = -1e30

MESH = pl.DeviceIdType.MESH
F32 = jnp.float32
BF16 = jnp.bfloat16
MIB = 1 << 20


def optimize(weight, gradient, first_moment, second_moment, rate, decay):
    first_moment = BETA_ONE * first_moment + (1.0 - BETA_ONE) * gradient
    second_moment = BETA_TWO * second_moment + (1.0 - BETA_TWO) * gradient * gradient
    first_fixed = first_moment / (1.0 - BETA_ONE**STEP)
    second_fixed = second_moment / (1.0 - BETA_TWO**STEP)
    weight = weight - rate * (first_fixed / (jnp.sqrt(second_fixed) + EPS_ADAM) + decay * weight)
    return (weight, first_moment, second_moment)


def flip(index, bit):
    return index + bit - 2 * bit * ((index // bit) % 2)


def flips(index, bits):
    for bit in bits:
        index = flip(index, bit)
    return index


def subsets(bits):
    found = [()]
    for bit in bits:
        found = found + [one + (bit,) for one in found]
    return found


def row_bits(rows):
    digits = [1 << place for place in range(rows.bit_length() - 1)]
    return digits[0], digits[1:]


def tiles(count, body):
    def step(at, carry):
        body(at)
        return carry

    lax.fori_loop(0, count, step, 0)


def lane_tile(at, size=LANES, base=0):
    return pl.ds(pl.multiple_of(base + at * size, LANES), size)


def dot(a, b):
    return jnp.dot(a, b, preferred_element_type=F32)


def dot_rows(a, b):
    return lax.dot_general(a, b, (((1,), (1,)), ((), ())), preferred_element_type=F32)


def dot_cols(a, b):
    return lax.dot_general(a, b, (((0,), (0,)), ((), ())), preferred_element_type=F32)


def greet(z, r, width, bits):
    bar = pltpu.get_barrier_semaphore()
    places = [(r, lax.rem(z + k, width)) for k in range(1, width)] + [(flip(r, b), z) for b in bits]
    for place in places:
        pl.semaphore_signal(bar, inc=1, device_id=place, device_id_type=MESH)
    pl.semaphore_wait(bar, len(places))


def at_steps(table):
    def hook(step):
        for at, actions in table.items():
            @pl.when(step == at)
            def _(actions=actions):
                for action in actions:
                    action()

    return hook


class Sends:
    def __init__(self, send, recv):
        self.send, self.recv, self.used = send, recv, 0

    def make(self, src, dst, place):
        at = self.used
        self.used += 1
        return pltpu.make_async_remote_copy(
            src_ref=src, dst_ref=dst, send_sem=self.send.at[at], recv_sem=self.recv.at[at],
            device_id=place, device_id_type=MESH,
        )


class Gather:
    def __init__(self, sends, own, full, z, r, width, rows):
        self.core, self.bits = row_bits(rows)
        shard = own.shape[0]
        self.full, self.own, self.z, self.r, self.shard = full, own, z, r, shard

        def block(index):
            return pl.ds(pl.multiple_of(index * shard, 16), shard)

        self.block = block
        self.over_width = [
            sends.make(own, full.at[z, block(r)], (r, lax.rem(z + k, width))) for k in range(1, width)
        ]
        half = width // 2
        self.steps = []
        for step in range(len(self.bits)):
            here = []
            for start, order in ((0, self.bits), (half, self.bits[::-1])):
                for sub in subsets(order[:step]):
                    part = full.at[pl.ds(start, half), block(flips(r, sub))]
                    here.append(sends.make(part, part, (flip(r, order[step]), z)))
            self.steps.append(here)
        last = []
        for sub in subsets(self.bits):
            part = full.at[:, block(flips(r, sub))]
            last.append(sends.make(part, part, (flip(r, self.core), z)))
        self.steps.append(last)

    def start(self):
        for copy in self.over_width:
            copy.start()
        self.full[self.z, self.block(self.r), :] = self.own[...]

    def advance(self, step):
        for copy in self.over_width if step == 0 else self.steps[step - 1]:
            copy.wait_recv()
        if step < len(self.steps):
            for copy in self.steps[step]:
                copy.start()

    def end(self):
        for copy in self.over_width + [one for step in self.steps for one in step]:
            copy.wait_send()

    @staticmethod
    def copies(width, rows):
        bits = rows.bit_length() - 2
        return width - 1 + sum(2 * 2**step for step in range(bits)) + 2**bits


class Scatter:
    def __init__(self, sends, grads, boxes, last_box, final, total, z, r, width, rows):
        self.core, self.bits = row_bits(rows)
        shard = total.shape[0]
        self.grads, self.boxes, self.last_box, self.final, self.total = grads, boxes, last_box, final, total
        self.z, self.width, self.shard = z, width, shard
        half = width // 2
        self.half = half

        def block(index):
            return pl.ds(pl.multiple_of(index * shard, 16), shard)

        self.block = block
        self.r = r
        other = flip(r, self.core)
        self.places = subsets(self.bits)
        self.steps = [
            [
                sends.make(grads.at[:, block(flips(other, sub))], boxes[0].at[at], (other, z))
                for at, sub in enumerate(self.places)
            ]
        ]
        self.where = [{(h, sub): boxes[0].at[at, pl.ds(h * half, half)] for at, sub in enumerate(self.places) for h in (0, 1)}]
        self.box_refs = [None]
        self.orders = (self.bits, self.bits[::-1])
        for step in range(len(self.bits)):
            here, kept, plan = [], {}, []
            for h, order in enumerate(self.orders):
                bit = order[step]
                for at, sub in enumerate(subsets(order[step + 1 :])):
                    far = tuple(sorted(sub + (bit,)))
                    near = tuple(sorted(sub))
                    slot = boxes[step + 1].at[h, at]
                    here.append(sends.make(self.where[step][(h, far)], slot, (flip(r, bit), z)))
                    plan.append((slot, self.where[step][(h, near)], h))
                    kept[(h, near)] = slot
            self.steps.append(here)
            self.where.append(kept)
            self.box_refs.append(plan)
        self.over_width = [
            sends.make(final.at[lax.rem(z + k, width)], last_box.at[k - 1], (r, lax.rem(z + k, width)))
            for k in range(1, width)
        ]

    def start(self):
        for copy in self.steps[0]:
            copy.start()

    def advance(self, step):
        for copy in self.steps[step]:
            copy.wait_recv()
        if step == 0:
            for at, sub in enumerate(self.places):
                rows = self.block(flips(self.r, sub))

                def add(w, at=at, rows=rows):
                    box = self.boxes[0].at[at, w]
                    box[...] = (box[...].astype(F32) + self.grads[w, rows, :].astype(F32)).astype(BF16)

                tiles(self.width, add)
        else:
            is_last = step == len(self.bits)
            for slot, kept, h in self.box_refs[step]:
                for w in range(self.half):
                    value = slot[w].astype(F32) + kept[w].astype(F32)
                    if is_last:
                        self.final[h * self.half + w] = value.astype(BF16)
                    else:
                        slot[w] = value.astype(BF16)
        following = self.over_width if step == len(self.bits) else self.steps[step + 1]
        for copy in following:
            copy.start()

    def finish(self):
        for copy in self.over_width:
            copy.wait_recv()
        value = self.final[self.z].astype(F32)
        for k in range(self.width - 1):
            value = value + self.last_box[k].astype(F32)
        self.total[...] = value

    def end(self):
        for copy in self.over_width + [one for step in self.steps for one in step]:
            copy.wait_send()

    @staticmethod
    def copies(width, rows):
        bits = rows.bit_length() - 2
        return width - 1 + sum(2 * 2 ** (bits - 1 - step) for step in range(bits)) + 2**bits

    @staticmethod
    def box_shapes(width, rows, shard):
        bits = rows.bit_length() - 2
        shapes = [(2**bits, width, shard, D)]
        for step in range(bits):
            shapes.append((2, 2 ** (bits - 1 - step), width // 2, shard, D))
        return shapes


def mix_stream(mix_ref, pair_ref, out_ref, base, layers):
    features, size = pair_ref.shape[1], pair_ref.shape[2]
    strip = 16

    def body(at):
        rows = pl.ds(pl.multiple_of(at * strip, strip), strip)
        total = mix_ref[0] * pair_ref[0, rows, :].astype(F32)
        for j in range(1, layers):
            total = total + mix_ref[j] * pair_ref[j, rows, :].astype(F32)
        out_ref[rows, base] = total.astype(BF16)

    tiles(features // strip, body)


def spread_gains(box_ref, gain_ref, width, piece):
    for w in range(width):
        for i in range(2):
            row = box_ref[w, pl.ds(i, 1), :]
            full = jnp.transpose(jnp.broadcast_to(row, (LANES, row.shape[1])))
            gain_ref[i, pl.ds(w * piece, piece), :] = full[:piece]


def norm_forward(x_ref, x_base, gain_ref, i, out_ref, stat_ref, count):
    def body(at):
        cols = lane_tile(at)
        x = x_ref[:, lane_tile(at, base=x_base)].astype(F32)
        centre = jnp.sum(x, 0, keepdims=True) / D
        spread = jnp.sum(x * x, 0, keepdims=True) / D - centre * centre
        scaling = lax.rsqrt(spread + EPS_NORM)
        out_ref[:, cols] = (gain_ref[i] * ((x - centre) * scaling)).astype(BF16)
        stat_ref[0:1, cols] = centre
        stat_ref[1:2, cols] = scaling

    tiles(count // LANES, body)


def norm_back(u_ref, u_base, x_ref, x_base, stat_ref, stat_base, gain_ref, i, residual, write, gain_acc, count):
    gain_acc[...] = jnp.zeros_like(gain_acc)

    def body(at):
        u = u_ref[:, lane_tile(at, base=u_base)].astype(F32)
        x = x_ref[:, lane_tile(at, base=x_base)].astype(F32)
        cols = lane_tile(at, base=stat_base)
        scaling = stat_ref[1:2, cols]
        centred = (x - stat_ref[0:1, cols]) * scaling
        gain_acc[...] += u * centred
        s = u * gain_ref[i]
        mean_s = jnp.sum(s, 0, keepdims=True) / D
        mean_c = jnp.sum(s * centred, 0, keepdims=True) / D
        write(lane_tile(at), residual(lane_tile(at)) + scaling * (s - mean_s - centred * mean_c))

    tiles(count // LANES, body)


def document_starts(seg_ref, start_ref, trig_ref, row, own_at, own):
    seg = seg_ref[pl.ds(row, 1), :]
    length = seg.shape[1]
    place = lax.broadcasted_iota(jnp.int32, (8, length), 1)
    seg = jnp.broadcast_to(seg, (8, length))
    before = pltpu.roll(seg, 1, 1)
    start = jnp.where((place > 0) & (seg == before), 0, place)
    step = 1
    while step < length:
        moved = pltpu.roll(start, step, 1)
        start = jnp.maximum(start, jnp.where(place >= step, moved, 0))
        step *= 2
    position = (place - start).astype(F32)
    scratch = start_ref.at[0:8]
    ext = HALO + own
    scratch[:, pl.ds(0, HALO)] = jnp.zeros((8, HALO), F32)
    scratch[:, pl.ds(HALO, length)] = position
    window = scratch[:, pl.ds(pl.multiple_of(own_at, LANES), ext)][0:1]
    half = HEAD // 2
    freq = jnp.exp(
        lax.broadcasted_iota(jnp.int32, (half, ext), 0).astype(F32) * (-2.0 * math.log(10000.0) / HEAD)
    )
    angle = freq * window
    trig_ref[0] = jnp.cos(angle)
    trig_ref[1] = jnp.sin(angle)
    scratch[:, pl.ds(HALO, length)] = start.astype(F32)
    kept = scratch[:, pl.ds(pl.multiple_of(own_at, LANES), ext)]
    scratch[:, pl.ds(0, ext)] = kept - (own_at - HALO).astype(F32)


def rotated(heads, cosine, sine):
    half = HEAD // 2
    a, b = heads[:half], heads[half:]
    return jnp.concatenate([a * cosine - b * sine, b * cosine + a * sine], 0)


def project(x_ref, wa_ref, trig_ref, q_ref, k_ref, v_ref, wo_ref, width, per, own, hook):
    ext = HALO + own
    group = per * HEAD
    scale = HEAD**-0.5

    def body(w):
        hook(w)
        turned = jnp.transpose(wa_ref[w])
        wo_ref[w] = turned[3 * group :]
        queries = dot(turned[:group], x_ref[:, HALO:])
        cosine, sine = trig_ref[0], trig_ref[1]
        for i in range(per):
            rows = queries[i * HEAD : (i + 1) * HEAD]
            q_ref[w * per + i] = (rotated(rows, cosine[:, HALO:], sine[:, HALO:]).astype(BF16) * scale).astype(BF16)
        keys = dot(turned[group : 2 * group], x_ref[...])
        for i in range(per):
            rows = keys[i * HEAD : (i + 1) * HEAD]
            k_ref[w * per + i] = rotated(rows, cosine, sine).astype(BF16)
        values = dot(turned[2 * group : 3 * group], x_ref[...])
        for i in range(per):
            v_ref[w * per + i] = values[i * HEAD : (i + 1) * HEAD].astype(BF16)

    tiles(width, body)


def attend(q_ref, k_ref, v_ref, start_ref, bias_ref, p_ref, ao_ref, width, per, own, hook):
    blocks = own // HALO
    for b in range(blocks):
        key_at = lax.broadcasted_iota(jnp.int32, (2 * HALO, HALO), 0).astype(F32) + float(b * HALO)
        query_at = lax.broadcasted_iota(jnp.int32, (2 * HALO, HALO), 1).astype(F32) + float((b + 1) * HALO)
        first = start_ref[0:1, (b + 1) * HALO : (b + 2) * HALO]
        bias_ref[b] = jnp.where((key_at >= first) & (key_at <= query_at), 0.0, MASKED)

    def body(w):
        hook(w)
        ao_ref[w, 0:HEAD, :] = jnp.zeros((HEAD, own), BF16)
        for i in range(per):
            h = w * per + i
            for b in range(blocks):
                keys = k_ref[h, :, b * HALO : (b + 2) * HALO]
                scores = dot_cols(keys, q_ref[h, :, b * HALO : (b + 1) * HALO]) + bias_ref[b]
                top = jnp.max(scores, 0, keepdims=True)
                raised = jnp.exp(scores - top)
                total = jnp.sum(raised, 0, keepdims=True)
                p_ref[h, b] = (raised * (1.0 / total)).astype(BF16)
                out = dot(v_ref[h, :, b * HALO : (b + 2) * HALO], p_ref[h, b])
                ao_ref[w, (i + 1) * HEAD : (i + 2) * HEAD, b * HALO : (b + 1) * HALO] = out.astype(BF16)

    tiles(width, body)


def out_project(st_ref, wa_ref, ao_ref, mid_ref, width, per):
    group = 3 * per * HEAD - HEAD
    mid_ref[...] = st_ref[:, HALO:].astype(F32)

    def body(w):
        mid_ref[...] += dot(wa_ref[w, :, group:], ao_ref[w])

    tiles(width, body)


def feed_forward(x_ref, ct_ref, wb_ref, wc_ref, gb_ref, gc_ref, acc_ref, u_ref, xt_ref, ctt_ref, pre_ref, gh_ref, hid_ref, gi_ref, width, hook):
    own = x_ref.shape[1]
    xt_ref[...] = jnp.transpose(x_ref[...])
    ctt_ref[...] = jnp.transpose(ct_ref[...])
    u_ref[...] = jnp.zeros_like(u_ref)
    strip = 32

    def body(w):
        hook(w)
        pre_ref[...] = dot(xt_ref[...], wb_ref[w])
        gh_ref[...] = dot(ctt_ref[...], wc_ref[w])

        def gelu(at):
            rows = pl.ds(pl.multiple_of(at * strip, strip), strip)
            x = pre_ref[rows, :]
            root = math.sqrt(2.0 / math.pi)
            square = x * x
            bent = jnp.tanh(root * (x + 0.044715 * (square * x)))
            hid_ref[rows, :] = (0.5 * x * (1.0 + bent)).astype(BF16)
            slope = 0.5 * (1.0 + bent) + (0.5 * root) * x * (1.0 - bent * bent) * (1.0 + (3 * 0.044715) * square)
            gi_ref[rows, :] = (gh_ref[rows, :] * slope).astype(BF16)

        tiles(own // strip, gelu)
        acc_ref[...] += dot_rows(wc_ref[w], hid_ref[...])
        gc_ref[w] = dot(ct_ref[...], hid_ref[...]).astype(BF16)
        u_ref[...] += dot_rows(wb_ref[w], gi_ref[...])
        gb_ref[w] = dot(x_ref[...], gi_ref[...]).astype(BF16)

    tiles(width, body)


def attend_back(low_ref, wo_ref, p_ref, q_ref, k_ref, v_ref, trig_ref, gp_ref, width, per, own, hook):
    ext = HALO + own
    group = per * HEAD
    blocks = own // HALO
    scale = HEAD**-0.5

    def body(w):
        hook(w)
        gp_ref[w, 3 * group :, :] = jnp.zeros((group, ext), BF16)
        gp_ref[w, :group, :HALO] = jnp.zeros((group, HALO), BF16)
        upstream = dot(wo_ref[w], low_ref[...]).astype(BF16)
        for i in range(per):
            h = w * per + i
            grad_keys, grad_values = [None] * (blocks + 1), [None] * (blocks + 1)
            for b in range(blocks):
                q = q_ref[h, :, b * HALO : (b + 1) * HALO]
                k = k_ref[h, :, b * HALO : (b + 2) * HALO]
                v = v_ref[h, :, b * HALO : (b + 2) * HALO]
                up = upstream[i * HEAD : (i + 1) * HEAD, b * HALO : (b + 1) * HALO]
                weights = p_ref[h, b]
                wide = weights.astype(F32)
                grad_weights = dot_cols(v, up)
                inner = jnp.sum(wide * grad_weights, 0, keepdims=True)
                grad_scores = (wide * (grad_weights - inner)).astype(BF16)
                gv = dot_rows(up, weights)
                gk = dot_rows(q, grad_scores)
                gq = dot(k, grad_scores) * scale
                cols = slice((b + 1) * HALO, (b + 2) * HALO)
                gp_ref[w, i * HEAD : (i + 1) * HEAD, cols] = rotated(gq, trig_ref[0, :, cols], -trig_ref[1, :, cols]).astype(BF16)
                for part in range(2):
                    piece = slice(part * HALO, (part + 1) * HALO)
                    at = b + part
                    grad_keys[at] = gk[:, piece] if grad_keys[at] is None else grad_keys[at] + gk[:, piece]
                    grad_values[at] = gv[:, piece] if grad_values[at] is None else grad_values[at] + gv[:, piece]
            for at in range(blocks + 1):
                cols = slice(at * HALO, (at + 1) * HALO)
                gp_ref[w, group + i * HEAD : group + (i + 1) * HEAD, cols] = rotated(
                    grad_keys[at], trig_ref[0, :, cols], -trig_ref[1, :, cols]
                ).astype(BF16)
                gp_ref[w, 2 * group + i * HEAD : 2 * group + (i + 1) * HEAD, cols] = grad_values[at].astype(BF16)

    tiles(width, body)


def project_back(x_ref, low_ref, ao_ref, wa_ref, gp_ref, ga_ref, u_ref, width, per, hook):
    group = 3 * per * HEAD - HEAD
    u_ref[...] = jnp.zeros_like(u_ref)

    def body(w):
        hook(w)
        u_ref[...] += dot(wa_ref[w], gp_ref[w])
        ga_ref[w, :, :group] = dot_rows(x_ref[...], gp_ref[w, :group, :]).astype(BF16)
        ga_ref[w, :, group:] = (
            dot_rows(x_ref[...], gp_ref[w, group:, :]) + dot_rows(low_ref[...], ao_ref[w])
        ).astype(BF16)

    tiles(width, body)


def block_kernel(width, rows, per, mix_ref, hist_ref, cot_ref, seg_ref, box_ref, own_ref, given_ref,
                 gcol_ref, bout_ref, small_ref, total_ref, left_ref,
                 full, st, ct, boxes_in, gain, x_one, stat_one, starts, trig, q, k, v, wo, ao, prob, mid, stat_two, gmid, low, blk,
                 gacc_one, gacc_two, halo_out, halo_in, macc, small_out, small_in, small_step,
                 final, last_box, boxes, load_sem, here_sem, send_sem, recv_sem):
    r, z = lax.axis_index("rows"), lax.axis_index("width")
    layers, piece, tokens = hist_ref.shape
    own = tokens // width
    ext = HALO + own
    per_row = seg_ref.shape[1] // own
    core, bits = row_bits(rows)
    hops = len(bits)
    cut = own // 2
    greet(z, r, width, [core] + bits)
    sends = Sends(send_sem, recv_sem)
    inside = own_ref is not None
    gathers = []
    if inside:
        gathers = [Gather(sends, own_ref.at[at], full.at[at], z, r, width, rows) for at in range(3)]
        first, second, third = gathers
    odd = lax.rem(z, 2) == 1
    mine = pl.ds(pl.multiple_of(z * piece, 16), piece)

    far = 1 - z // 2
    chunks = []
    for at in range(width):
        low_half = flip(far, 1) if at // 2 else far
        chunks.append(2 * low_half + at % 2)
    st_even = st.at[mine, pl.ds(HALO, own)]
    st_odd = st.at[mine, :]
    gain_sends = [sends.make(box_ref, boxes_in.at[z], (r, lax.rem(z + step, width))) for step in range(1, width)]
    base = sends.used
    sends.used += width - 1

    def scoped_stream(pair, mixed):
        def load(at):
            cols = pl.ds(pl.multiple_of(chunks[at // 2] * own + (at % 2) * cut, LANES), cut)
            return pltpu.make_async_copy(hist_ref.at[:, :, cols], pair.at[at % 3], load_sem.at[at % 3])

        def stream_copy(step, target, is_odd):
            start = pl.multiple_of(target * own, LANES)
            if is_odd:
                src, dst = mixed.at[:, pl.ds(pl.multiple_of(start - HALO, LANES), ext)], st_odd
            else:
                src, dst = mixed.at[:, pl.ds(start, own)], st_even
            return pltpu.make_async_remote_copy(
                src_ref=src, dst_ref=dst, send_sem=send_sem.at[base + step - 1], recv_sem=recv_sem.at[base + step - 1],
                device_id=(r, target), device_id_type=MESH,
            )

        for at in range(3):
            load(at).start()
        if inside:
            first.start()
        for copy in gain_sends:
            copy.start()
        boxes_in[z] = box_ref[...]
        for at in range(2 * width):
            load(at).wait()
            target = chunks[at // 2]
            start = pl.multiple_of(target * own + (at % 2) * cut, LANES)
            mix_stream(mix_ref, pair.at[at % 3], mixed, pl.ds(start, cut), layers)
            if at + 3 < 2 * width:
                load(at + 3).start()
            if at % 2 == 0:
                continue
            is_odd = at // 2 % 2 == 1
            for step in range(1, width):
                @pl.when(lax.rem(z + step, width) == target)
                def _(step=step, target=target, is_odd=is_odd):
                    stream_copy(step, target, is_odd).start()

            @pl.when(target == z)
            def _(is_odd=is_odd, target=target):
                start = pl.multiple_of(target * own, LANES)
                if is_odd:
                    st_odd[...] = mixed[:, pl.ds(pl.multiple_of(start - HALO, LANES), ext)]
                else:
                    st_even[...] = mixed[:, pl.ds(start, own)]
                    st[:, 0:HALO] = jnp.zeros((D, HALO), BF16)

        for gather in gathers[1:]:
            gather.start()
        for copy in cot_sends:
            copy.start()
        cot_here.start()
        for copy in gain_sends:
            copy.wait()
        spread_gains(boxes_in, gain, width, piece)
        document_starts(seg_ref, starts, trig, z // per_row, lax.rem(z, per_row) * own, own)
        if inside:
            first.advance(0)
            first.advance(1)
        for step in range(1, width):
            for is_odd in (False, True):
                @pl.when(lax.rem(z, 2) == int(is_odd))
                def _(step=step, is_odd=is_odd):
                    stream_copy(step, z, is_odd).wait_recv()

                @pl.when(lax.rem(z + step, 2) == int(is_odd))
                def _(step=step, is_odd=is_odd):
                    stream_copy(step, lax.rem(z + step, width), is_odd).wait_send()

    cot_sends = []
    for step in range(1, width):
        target = lax.rem(z + step, width)
        cols = pl.ds(pl.multiple_of(target * own, LANES), own)
        cot_sends.append(sends.make(cot_ref.at[:, cols], ct.at[mine, :], (r, target)))
    cot_here = pltpu.make_async_copy(
        cot_ref.at[:, pl.ds(pl.multiple_of(z * own, LANES), own)], ct.at[mine, :], here_sem
    )
    if not inside:
        given = pltpu.make_async_copy(given_ref, full, load_sem.at[3])
        given.start()
    pl.run_scoped(scoped_stream, pltpu.VMEM((3, layers, piece, cut), BF16), pltpu.VMEM((piece, tokens), BF16))

    norm_forward(st, 0, gain, 0, x_one, stat_one, ext)
    if inside:
        for step in range(2, hops + 2):
            first.advance(step)
    else:
        given.wait()
    project(x_one, full.at[0], trig, q, k, v, wo, width, per, own, at_steps({}))
    when_attend = at_steps({2: [lambda: second.advance(0)]}) if inside else at_steps({})
    pl.run_scoped(
        lambda bias: attend(q, k, v, starts, bias, prob, ao, width, per, own, when_attend),
        pltpu.VMEM((own // HALO, 2 * HALO, HALO), F32),
    )
    if inside:
        second.advance(1)
        third.advance(0)
    out_project(st, full.at[0], ao, mid, width, per)
    gmid[...] = mid[...]
    if inside:
        for step in range(1, hops + 1):
            second.advance(step + 1)
            third.advance(step)
        third.advance(hops + 1)
        for gather in gathers:
            gather.end()

    scatters = []
    if inside:
        scatters = [
            Scatter(sends, full.at[at], [box.at[at] for box in boxes], last_box.at[at], final.at[at], total_ref.at[at], z, r, width, rows)
            for at in (2, 1, 0)
        ]
    for copy in cot_sends:
        copy.wait()
    cot_here.wait()

    def scoped_feed(x_two, xt, ctt, pre, gh, hid, gi, u_two):
        norm_forward(mid, 0, gain, 1, x_two, stat_two, own)
        feed_forward(x_two, ct, full.at[1], full.at[2], full.at[1], full.at[2], gmid, u_two, xt, ctt, pre, gh, hid, gi, width, at_steps({}))
        blk[...] = gmid[...].astype(BF16)

        def write(cols, value):
            gmid[:, cols] = value
            low[:, cols] = value.astype(BF16)

        norm_back(u_two, 0, mid, 0, stat_two, 0, gain, 1, lambda cols: ct[:, cols].astype(F32), write, gacc_two, own)

    pl.run_scoped(
        scoped_feed, pltpu.VMEM((D, own), BF16), pltpu.VMEM((own, D), BF16), pltpu.VMEM((own, D), BF16), pltpu.VMEM((own, D), F32),
        pltpu.VMEM((own, D), F32), pltpu.VMEM((own, D), BF16), pltpu.VMEM((own, D), BF16), pltpu.VMEM((D, own), F32),
    )
    for scatter in scatters[:2]:
        scatter.start()
    blk_sends, gs_sends = [], []
    here = pl.ds(pl.multiple_of(z * own, LANES), own)
    for step in range(1, width):
        target = lax.rem(z + step, width)
        part = pl.ds(pl.multiple_of(target * piece, 16), piece)
        blk_sends.append(sends.make(blk.at[part, :], bout_ref.at[:, here], (r, target)))
    for copy in blk_sends:
        copy.start()
    bout_ref[:, here] = blk[mine, :]

    halo = sends.make(halo_out, halo_in, (r, flip(z, 1)))

    def scoped_back(gp, u):
        when_attend, when_project = at_steps({}), at_steps({})
        if inside:
            when_attend = at_steps({1: [lambda: scatters[0].advance(0), lambda: scatters[1].advance(0)]})
            when_project = at_steps({1: [lambda: scatters[0].advance(1)]})
        attend_back(low, wo, prob, q, k, v, trig, gp, width, per, own, when_attend)
        project_back(x_one, low, ao, full.at[0], gp, full.at[0], u, width, per, when_project)

        @pl.when(odd)
        def _():
            halo_out[...] = u[:, 0:HALO].astype(BF16)
            halo.start()

        if inside:
            scatters[2].start()
            scatters[0].advance(2)

        @pl.when(jnp.logical_not(odd))
        def _():
            halo.wait_recv()
            u[:, own : own + HALO] += halo_in[...].astype(F32)

        def write(cols, value):
            blk[:, cols] = value.astype(BF16)

        for copy in blk_sends:
            copy.wait_send()
        norm_back(u, HALO, st, HALO, stat_one, HALO, gain, 0, lambda cols: gmid[:, cols], write, gacc_one, own)

    pl.run_scoped(scoped_back, pltpu.VMEM((width, 4 * per * HEAD, ext), BF16), pltpu.VMEM((D, ext), F32))

    for step in range(1, width):
        target = lax.rem(z + step, width)
        part = pl.ds(pl.multiple_of(target * piece, 16), piece)
        gs_sends.append(sends.make(blk.at[part, :], gcol_ref.at[:, here], (r, target)))
    for copy in gs_sends:
        copy.start()
    gcol_ref[:, here] = blk[mine, :]
    macc[...] = jnp.zeros_like(macc)
    strip = 16

    def scoped_mix(pair):
        def place(at):
            chunk = lax.rem(z + width - at // 2, width)
            return pl.ds(pl.multiple_of(chunk * own + (at % 2) * cut, LANES), cut)

        def load(at):
            return pltpu.make_async_copy(hist_ref.at[:, :, place(at)], pair.at[at % 3], load_sem.at[at % 3])

        for at in range(3):
            load(at).start()
        for at in range(2 * width):
            if at % 2 == 0 and at:
                gs_sends[at // 2 - 1].wait_recv()
            load(at).wait()
            cols = place(at)

            def body(row, at=at, cols=cols):
                part = pl.ds(pl.multiple_of(row * strip, strip), strip)
                g = gcol_ref[part, cols].astype(F32)
                for j in range(layers):
                    crossed = pair[at % 3, j, part, :].astype(F32) * g
                    folded = crossed[:8] + crossed[8:]
                    total = folded[:, :LANES]
                    for lane in range(1, cut // LANES):
                        total = total + folded[:, lane * LANES : (lane + 1) * LANES]
                    macc[j] += total

            tiles(piece // strip, body)
            if at + 3 < 2 * width:
                load(at + 3).start()
            if inside:
                if at == 0:
                    scatters[1].advance(1)
                    scatters[2].advance(0)
                if at == 1:
                    scatters[1].advance(2)
                    scatters[2].advance(1)

    pl.run_scoped(scoped_mix, pltpu.VMEM((3, layers, piece, cut), BF16))

    small_out[...] = jnp.zeros_like(small_out)
    gain_one = jnp.sum(jnp.transpose(gacc_one[...]), 0, keepdims=True)
    gain_two = jnp.sum(jnp.transpose(gacc_two[...]), 0, keepdims=True)
    depth = jnp.sum(jnp.transpose(jnp.sum(macc[...], 1)), 0, keepdims=True)
    for w in range(width):
        small_out[w, 0:1, 0:piece] = gain_one[:, w * piece : (w + 1) * piece]
        small_out[w, 1:2, 0:piece] = gain_two[:, w * piece : (w + 1) * piece]
        small_out[w, 2:3, 0 : depth.shape[1]] = depth
    small_sends = [
        sends.make(small_out.at[lax.rem(z + step, width)], small_in.at[step - 1], (r, lax.rem(z + step, width)))
        for step in range(1, width)
    ]
    for copy in small_sends:
        copy.start()
    current = small_out[z]
    for step in range(1, width):
        small_sends[step - 1].wait_recv()
        current = current + small_in[step - 1]
    for at, bit in enumerate([core] + bits):
        small_step[at, 0] = current
        copy = sends.make(small_step.at[at, 0], small_step.at[at, 1], (flip(r, bit), z))
        copy.start()
        copy.wait_recv()
        current = current + small_step[at, 1]
        small_sends.append(copy)
    small_ref[...] = current
    if inside:
        scatters[2].advance(2)
    for scatter in scatters:
        scatter.finish()
    for copy in blk_sends:
        copy.wait_recv()
    for copy in gs_sends + small_sends:
        copy.wait_send()

    @pl.when(odd)
    def _():
        halo.wait_send()

    for scatter in scatters:
        scatter.end()
    if not inside:
        leave = pltpu.make_async_copy(full, left_ref, load_sem.at[3])
        leave.start()
        leave.wait()


def vmem(count):
    return [pl.BlockSpec(memory_space=pltpu.VMEM)] * count


def shape(*sizes, dtype=F32):
    return jax.ShapeDtypeStruct(sizes, dtype)


def block(width, rows, mix, history, cotangent, segments, box, own_three):
    layers, piece, tokens = history.shape
    shard = own_three.shape[1]
    own = tokens // width
    ext = HALO + own
    heads = D // HEAD
    per = heads // width
    group = per * HEAD
    blocks = own // HALO
    digits = rows.bit_length() - 1
    inside = shard % 16 == 0
    any_space = pl.BlockSpec(memory_space=pl.ANY)
    ins = [mix, history, cotangent, segments, box]
    specs = [pl.BlockSpec(memory_space=pltpu.SMEM), any_space, any_space] + vmem(2)
    outs = [shape(piece, tokens, dtype=BF16), shape(piece, tokens, dtype=BF16), shape(8, 2 * LANES)]
    out_specs = vmem(3)
    box_shapes = []
    if inside:
        ins, specs = ins + [own_three], specs + vmem(1)
        outs, out_specs = outs + [shape(3, shard, D)], out_specs + vmem(1)
        box_shapes = Scatter.box_shapes(width, rows, shard)
    else:
        gathered = lax.all_gather(lax.all_gather(own_three, "rows", axis=1, tiled=True), "width", axis=1)
        ins, specs = ins + [gathered], specs + [any_space]
        outs, out_specs = outs + [shape(3, width, D, D, dtype=BF16)], out_specs + [any_space]
    low = lambda *sizes: pltpu.VMEM(sizes, BF16)
    full = lambda *sizes: pltpu.VMEM(sizes, F32)
    scratch = [
        low(3, width, D, D), low(D, ext), low(D, own), full(width, 8, 2 * LANES), full(2, D, LANES), low(D, ext), full(8, ext),
        full(8, HALO + segments.shape[1]), full(2, HEAD // 2, ext), low(heads, HEAD, own), low(heads, HEAD, ext), low(heads, HEAD, ext),
        low(width, group, D), low(width, HEAD + group, own), low(heads, blocks, 2 * HALO, HALO), full(D, own), full(8, own),
        full(D, own), low(D, own), low(D, own), full(D, LANES), full(D, LANES), low(D, HALO), low(D, HALO), full(layers, 8, LANES),
        full(width, 8, 2 * LANES), full(width - 1, 8, 2 * LANES), full(digits, 2, 8, 2 * LANES),
    ]
    common = len(scratch)
    if inside:
        scratch += [low(3, width, shard, D), low(3, width - 1, shard, D)] + [low(3, *one) for one in box_shapes]
    count = 5 * (width - 1) + 1 + (width - 1) + digits
    count += 3 * Gather.copies(width, rows) + 3 * Scatter.copies(width, rows)
    scratch += [
        pltpu.SemaphoreType.DMA((4,)), pltpu.SemaphoreType.DMA, pltpu.SemaphoreType.DMA((count,)), pltpu.SemaphoreType.DMA((count,)),
    ]

    def kernel(*refs):
        given, found, rest = refs[:6], refs[6:10], refs[10:]
        weights = (given[5], None) if inside else (None, given[5])
        results = (found[3], None) if inside else (None, found[3])
        kept, rest = rest[:common], rest[common:]
        final, last_box, boxes = None, None, ()
        if inside:
            final, last_box, boxes, rest = rest[0], rest[1], rest[2 : 2 + len(box_shapes)], rest[2 + len(box_shapes) :]
        block_kernel(width, rows, per, *given[:5], *weights, *found[:3], *results, *kept, final, last_box, boxes, *rest)

    found = pl.pallas_call(
        kernel,
        out_shape=outs,
        in_specs=specs,
        out_specs=out_specs,
        scratch_shapes=scratch,
        compiler_params=pltpu.CompilerParams(collective_id=0, has_side_effects=True, vmem_limit_bytes=64 * MIB - 128 * 1024),
    )(*ins)
    if inside:
        return found
    total = lax.psum_scatter(found[3], "width", scatter_dimension=1)
    return (*found[:3], lax.psum_scatter(total, "rows", scatter_dimension=1, tiled=True).astype(F32))


def on_device(
    width, rows, history, cotangent, segments, w_attend, m_attend, v_attend, w_output, m_output, v_output,
    w_expand, m_expand, v_expand, w_reduce, m_reduce, v_reduce, gains, m_gains, v_gains, mix, m_mix, v_mix,
):
    layers, piece, _ = history.shape
    own_three = jnp.stack([
        jnp.concatenate([w_attend[0], w_attend[1], w_attend[2], jnp.transpose(w_output)], 1),
        w_expand,
        jnp.transpose(w_reduce),
    ]).astype(BF16)
    box = jnp.pad(gains, ((0, 8 - gains.shape[0]), (0, 2 * LANES - piece)))
    grad_stream, block_output, small, total = block(width, rows, mix, history, cotangent, segments, box, own_three)
    history_grad = (mix[:, None, None] * grad_stream[None].astype(F32)).astype(BF16)
    first = total[0]
    sum_attend = jnp.stack([first[:, k * piece : (k + 1) * piece] for k in range(3)])
    sum_output = jnp.transpose(first[:, 3 * piece :])
    new_attend = optimize(w_attend, sum_attend, m_attend, v_attend, RATE_MATRIX, DECAY)
    new_output = optimize(w_output, sum_output, m_output, v_output, RATE_OUTPUT, DECAY)
    new_expand = optimize(w_expand, total[1], m_expand, v_expand, RATE_MATRIX, DECAY)
    new_reduce = optimize(w_reduce, jnp.transpose(total[2]), m_reduce, v_reduce, RATE_MATRIX, DECAY)
    new_gains = optimize(gains, small[0:2, :piece], m_gains, v_gains, RATE_GAIN, 0.0)
    new_mix = optimize(mix, small[2, :layers], m_mix, v_mix, RATE_MIX, 0.0)
    return (block_output, history_grad, *new_attend, *new_output, *new_expand, *new_reduce, *new_gains, *new_mix)


def solution(mesh):
    square, tall, wide = P(None, "rows", "width"), P("width", "rows"), P("rows", "width")
    weights = (square,) * 3 + (tall,) * 3 + (wide,) * 3 + (tall,) * 3 + (P(None, "width"),) * 3 + (P(),) * 3
    return jax.shard_map(
        functools.partial(on_device, mesh.shape["width"], mesh.shape["rows"]),
        mesh=mesh,
        in_specs=(P(None, "width", "rows"), P("width", "rows"), P("rows", None)) + weights,
        out_specs=(P("width", "rows"), P(None, "width", "rows")) + weights,
        check_vma=False,
    )
```

```python
import functools
import math
from types import SimpleNamespace

import jax
import jax.numpy as jnp
from jax import lax
from jax.experimental import pallas as pl
from jax.experimental.pallas import tpu as pltpu
from jax.sharding import PartitionSpec as P

D = 768
HEAD = 64
STEP = 10
HALO = 256
LANES = 128


EPS_NORM = 1e-05
EPS_ADAM = 1e-08
BETA_ONE = 0.9
BETA_TWO = 0.95
RATE_MATRIX = 0.02
RATE_OUTPUT = 0.12
RATE_GAIN = 0.4
RATE_MIX = 0.05
DECAY = 0.1
MASKED = -1e30

MESH = pl.DeviceIdType.MESH
F32 = jnp.float32
BF16 = jnp.bfloat16
MIB = 1 << 20


def optimize(weight, gradient, first_moment, second_moment, rate, decay):
    first_moment = BETA_ONE * first_moment + (1.0 - BETA_ONE) * gradient
    second_moment = BETA_TWO * second_moment + (1.0 - BETA_TWO) * gradient * gradient
    first_fixed = first_moment / (1.0 - BETA_ONE**STEP)
    second_fixed = second_moment / (1.0 - BETA_TWO**STEP)
    weight = weight - rate * (first_fixed / (jnp.sqrt(second_fixed) + EPS_ADAM) + decay * weight)
    return (weight, first_moment, second_moment)


def flip(index, bit):
    return index + bit - 2 * bit * lax.rem(lax.div(index, jnp.int32(bit)), 2)


def flips(index, bits):
    for bit in bits:
        index = flip(index, bit)
    return index


def subsets(bits):
    found = [()]
    for bit in bits:
        found = found + [one + (bit,) for one in found]
    return found


def row_bits(rows):
    digits = [1 << place for place in range(rows.bit_length() - 1)]
    return digits[0], digits[1:]


def tiles(count, body):
    def step(at, carry):
        body(at)
        return carry

    lax.fori_loop(0, count, step, 0)


def lane_tile(at, size=LANES, base=0):
    return pl.ds(pl.multiple_of(base + at * size, LANES), size)


def dot(a, b):
    return jnp.dot(a, b, preferred_element_type=F32)


def dot_rows(a, b):
    return lax.dot_general(a, b, (((1,), (1,)), ((), ())), preferred_element_type=F32)


def dot_cols(a, b):
    return lax.dot_general(a, b, (((0,), (0,)), ((), ())), preferred_element_type=F32)


def greet(z, r, width, bits):
    bar = pltpu.get_barrier_semaphore()
    places = [(r, lax.rem(z + k, width)) for k in range(1, width)] + [(flip(r, b), z) for b in bits]
    for place in places:
        pl.semaphore_signal(bar, inc=1, device_id=place, device_id_type=MESH)
    pl.semaphore_wait(bar, len(places))


def at_steps(table):
    def hook(step):
        for at, actions in table.items():
            @pl.when(step == at)
            def _(actions=actions):
                for action in actions:
                    action()

    return hook


class Sends:
    def __init__(self, send, recv):
        self.send, self.recv, self.used = send, recv, 0

    def reserve(self, count):
        at = self.used
        self.used += count
        return at

    def copy(self, at, src, dst, place):
        return pltpu.make_async_remote_copy(
            src_ref=src, dst_ref=dst, send_sem=self.send.at[at], recv_sem=self.recv.at[at],
            device_id=place, device_id_type=MESH,
        )

    def make(self, src, dst, place):
        return self.copy(self.reserve(1), src, dst, place)


def arrival(z, at, width):
    found = 0
    for own in range(width):
        order = sorted(range(width), key=lambda w, own=own: (abs(w - own), w))
        for place, w in enumerate(order):
            if w:
                found = found + w * jnp.where((z == own) & (at == place), 1, 0)
    return found


class Plane:
    def __init__(self, chunk, z, r, width, rows, shard):
        self.core, self.bits = row_bits(rows)
        self.chunk, self.z, self.r, self.width, self.shard = chunk, z, r, width, shard
        self.hops = len(self.bits)
        self.per_slab = 2 ** (self.hops + 1) - 1

    def rows(self, index):
        return pl.ds(pl.multiple_of(index * self.shard, 16), self.shard)

    def bit(self, w, at):
        one, other = self.bits[at], self.bits[::-1][at]
        return one + (other - one) * lax.rem(w + self.chunk, 2)

    def place(self, index, w, code):
        for at in range(self.hops):
            if code >> at & 1:
                index = flip(index, self.bit(w, at))
        return index


class Gather(Plane):
    def __init__(self, sends, chunk, own, full, z, r, width, rows):
        super().__init__(chunk, z, r, width, rows, own.shape[0])
        self.sends, self.own, self.full = sends, own, full
        self.line_base = sends.reserve(2 * (width - 1))
        self.slab_base = sends.reserve(width * self.per_slab)

    @staticmethod
    def copies(width, rows):
        return 2 * (width - 1) + width * (rows // 2 * 2 - 1)

    def line(self, w, up, distance, target):
        part = self.full.at[w, self.rows(self.r)]
        at = self.line_base + (1 - up) * (self.width - 1) + distance
        return self.sends.copy(at, part, part, (self.r, target))

    def start(self):
        self.full[self.z, self.rows(self.r), :] = self.own[...]
        for up, there, target in ((1, self.z + 1 < self.width, self.z + 1), (0, self.z > 0, self.z - 1)):
            @pl.when(there)
            def _(up=up, target=target):
                self.line(self.z, up, 0, target).start()

        self.spread(self.z)

    def hop(self, w):
        up = jnp.where(w < self.z, 1, 0)
        distance = (self.z - w) * (2 * up - 1)
        self.line(w, up, distance - 1, self.z).wait_recv()
        self.spread(w)

    def onward(self, w):
        up = jnp.where(w < self.z, 1, 0)
        distance = (self.z - w) * (2 * up - 1)
        target = self.z + 2 * up - 1
        return (target >= 0) & (target < self.width), self.line(w, up, distance, target)

    def forward(self, w):
        there, copy = self.onward(w)

        @pl.when(there)
        def _():
            copy.start()

    def step(self, w, at):
        peer = flip(self.r, self.bit(w, at) if at < self.hops else self.core)
        found = []
        for code in range(2**at):
            part = self.full.at[w, self.rows(self.place(self.r, w, code))]
            found.append(self.sends.copy(self.slab_base + w * self.per_slab + 2**at - 1 + code, part, part, (peer, self.z)))
        return found

    def spread(self, w):
        for copy in self.step(w, 0):
            copy.start()

    def pass_on(self, w, at):
        for copy in self.step(w, at - 1):
            copy.wait_recv()
        for copy in self.step(w, at):
            copy.start()

    def to_chips(self, w):
        for at in range(1, self.hops):
            self.pass_on(w, at)

    def to_core(self, w):
        if self.hops:
            self.pass_on(w, self.hops)

    def take(self, w):
        for copy in self.step(w, self.hops):
            copy.wait_recv()

    def clear(self, w):
        for at in range(self.hops + 1):
            for copy in self.step(w, at):
                copy.wait_send()

        @pl.when(w == self.z)
        def _():
            for up, there, target in ((1, self.z + 1 < self.width, self.z + 1), (0, self.z > 0, self.z - 1)):
                @pl.when(there)
                def _(up=up, target=target):
                    self.line(self.z, up, 0, target).wait_send()

        there, onward = self.onward(w)

        @pl.when((w != self.z) & there)
        def _():
            onward.wait_send()


class Scatter(Plane):
    def __init__(self, sends, chunk, grads, boxes, last_box, total, z, r, width, rows):
        super().__init__(chunk, z, r, width, rows, total.shape[0])
        self.sends, self.grads, self.boxes, self.last_box, self.total = sends, grads, boxes, last_box, total
        self.other = flip(r, self.core)
        self.slab_base = sends.reserve(width * self.per_slab)
        self.width_base = sends.reserve(width - 1)

    @staticmethod
    def copies(width, rows):
        return width - 1 + width * (rows // 2 * 2 - 1)

    @staticmethod
    def box_shapes(width, rows, shard):
        hops = rows.bit_length() - 2
        return [(2 ** (hops - at), width, shard, D) for at in range(hops + 1)]

    def step(self, w, at):
        base = self.slab_base + w * self.per_slab
        if at == 0:
            return [
                self.sends.copy(base + code, self.grads.at[w, self.rows(self.place(self.other, w, code))], self.boxes[0].at[code, w], (self.other, self.z))
                for code in range(2**self.hops)
            ]
        base += sum(2 ** (self.hops - one) for one in range(at))
        peer = flip(self.r, self.bit(w, at - 1))
        return [
            self.sends.copy(base + code, self.boxes[at - 1].at[2 * code + 1, w], self.boxes[at].at[code, w], (peer, self.z))
            for code in range(2 ** (self.hops - at))
        ]

    def over_width(self, w):
        ahead = lax.rem(w - self.z + self.width, self.width)
        return self.sends.copy(
            self.width_base + ahead - 1, self.boxes[self.hops].at[0, w], self.last_box.at[ahead - 1], (self.r, w)
        )

    def begin(self, w):
        for copy in self.step(w, 0):
            copy.start()

    def take(self, w, at):
        for copy in self.step(w, at):
            copy.wait_recv()
        for code in range(2 ** (self.hops - at)):
            box = self.boxes[at].at[code, w]
            if at == 0:
                kept = self.grads.at[w, self.rows(self.place(self.r, w, code))]
            else:
                kept = self.boxes[at - 1].at[2 * code, w]
            box[...] = (box[...].astype(F32) + kept[...].astype(F32)).astype(BF16)
        if at < self.hops:
            for copy in self.step(w, at + 1):
                copy.start()
        else:
            @pl.when(w != self.z)
            def _():
                self.over_width(w).start()

    def take_core(self, w):
        self.take(w, 0)

    def take_chips(self, w):
        for at in range(1, self.hops):
            self.take(w, at)

    def take_last(self, w):
        if self.hops:
            self.take(w, self.hops)

    def finish(self):
        for ahead in range(1, self.width):
            self.over_width(lax.rem(self.z + ahead, self.width)).wait_recv()
        value = self.boxes[self.hops][0, self.z].astype(F32)
        for ahead in range(1, self.width):
            value = value + self.last_box[ahead - 1].astype(F32)
        self.total[...] = value

    def end(self):
        def one(w):
            for at in range(self.hops + 1):
                for copy in self.step(w, at):
                    copy.wait_send()

            @pl.when(w != self.z)
            def _():
                self.over_width(w).wait_send()

        tiles(self.width, one)


def mix_stream(mix_ref, pair_ref, out_ref, base, layers):
    features, size = pair_ref.shape[1], pair_ref.shape[2]
    strip = 16

    def body(at):
        rows = pl.ds(pl.multiple_of(at * strip, strip), strip)
        total = mix_ref[0] * pair_ref[0, rows, :].astype(F32)
        for j in range(1, layers):
            total = total + mix_ref[j] * pair_ref[j, rows, :].astype(F32)
        out_ref[rows, base] = total.astype(BF16)

    tiles(features // strip, body)


def spread_gains(box_ref, gain_ref, width, piece):
    for w in range(width):
        for i in range(2):
            row = box_ref[w, pl.ds(i, 1), :]
            full = jnp.transpose(jnp.broadcast_to(row, (LANES, row.shape[1])))
            gain_ref[i, pl.ds(w * piece, piece), :] = full[:piece]


def norm_forward(x_ref, x_base, gain_ref, i, out_ref, stat_ref, count):
    def body(at):
        cols = lane_tile(at)
        x = x_ref[:, lane_tile(at, base=x_base)].astype(F32)
        centre = jnp.sum(x, 0, keepdims=True) / D
        spread = jnp.sum(x * x, 0, keepdims=True) / D - centre * centre
        scaling = lax.rsqrt(spread + EPS_NORM)
        out_ref[:, cols] = (gain_ref[i] * ((x - centre) * scaling)).astype(BF16)
        stat_ref[0:1, cols] = centre
        stat_ref[1:2, cols] = scaling

    tiles(count // LANES, body)


def norm_back(u_ref, u_base, x_ref, x_base, stat_ref, stat_base, gain_ref, i, residual, write, gain_acc, start, count):
    def body(step):
        at = step + start // LANES
        u = u_ref[:, lane_tile(at, base=u_base)].astype(F32)
        x = x_ref[:, lane_tile(at, base=x_base)].astype(F32)
        cols = lane_tile(at, base=stat_base)
        scaling = stat_ref[1:2, cols]
        centred = (x - stat_ref[0:1, cols]) * scaling
        gain_acc[...] += u * centred
        s = u * gain_ref[i]
        mean_s = jnp.sum(s, 0, keepdims=True) / D
        mean_c = jnp.sum(s * centred, 0, keepdims=True) / D
        write(lane_tile(at), residual(lane_tile(at)) + scaling * (s - mean_s - centred * mean_c))

    tiles(count // LANES, body)


def document_starts(seg_ref, start_ref, trig_ref, row, own_at, own):
    seg = seg_ref[pl.ds(row, 1), :]
    length = seg.shape[1]
    place = lax.broadcasted_iota(jnp.int32, (8, length), 1)
    seg = jnp.broadcast_to(seg, (8, length))
    before = pltpu.roll(seg, 1, 1)
    start = jnp.where((place > 0) & (seg == before), 0, place)
    step = 1
    while step < length:
        moved = pltpu.roll(start, step, 1)
        start = jnp.maximum(start, jnp.where(place >= step, moved, 0))
        step *= 2
    position = (place - start).astype(F32)
    scratch = start_ref.at[0:8]
    ext = HALO + own
    scratch[:, pl.ds(0, HALO)] = jnp.zeros((8, HALO), F32)
    scratch[:, pl.ds(HALO, length)] = position
    window = scratch[:, pl.ds(pl.multiple_of(own_at, LANES), ext)][0:1]
    half = HEAD // 2
    freq = jnp.exp(
        lax.broadcasted_iota(jnp.int32, (half, ext), 0).astype(F32) * (-2.0 * math.log(10000.0) / HEAD)
    )
    angle = freq * window
    trig_ref[0] = jnp.cos(angle)
    trig_ref[1] = jnp.sin(angle)
    scratch[:, pl.ds(HALO, length)] = start.astype(F32)
    kept = scratch[:, pl.ds(pl.multiple_of(own_at, LANES), ext)]
    scratch[:, pl.ds(0, ext)] = kept - (own_at - HALO).astype(F32)


def rotated(heads, cosine, sine):
    half = HEAD // 2
    a, b = heads[:half], heads[half:]
    return jnp.concatenate([a * cosine - b * sine, b * cosine + a * sine], 0)


def project(x_ref, wa_ref, trig_ref, q_ref, k_ref, v_ref, wo_ref, w, per):
    group = per * HEAD
    scale = HEAD**-0.5
    turned = jnp.transpose(wa_ref[w])
    wo_ref[w] = turned[3 * group :]
    queries = dot(turned[:group], x_ref[:, HALO:])
    cosine, sine = trig_ref[0], trig_ref[1]
    for i in range(per):
        rows = queries[i * HEAD : (i + 1) * HEAD]
        q_ref[w * per + i] = (rotated(rows, cosine[:, HALO:], sine[:, HALO:]).astype(BF16) * scale).astype(BF16)
    keys = dot(turned[group : 2 * group], x_ref[...])
    for i in range(per):
        rows = keys[i * HEAD : (i + 1) * HEAD]
        k_ref[w * per + i] = rotated(rows, cosine, sine).astype(BF16)
    values = dot(turned[2 * group : 3 * group], x_ref[...])
    for i in range(per):
        v_ref[w * per + i] = values[i * HEAD : (i + 1) * HEAD].astype(BF16)


def attend_bias(start_ref, bias_ref):
    for b in range(bias_ref.shape[0]):
        key_at = lax.broadcasted_iota(jnp.int32, (2 * HALO, HALO), 0).astype(F32) + float(b * HALO)
        query_at = lax.broadcasted_iota(jnp.int32, (2 * HALO, HALO), 1).astype(F32) + float((b + 1) * HALO)
        first = start_ref[0:1, (b + 1) * HALO : (b + 2) * HALO]
        bias_ref[b] = jnp.where((key_at >= first) & (key_at <= query_at), 0.0, MASKED)


def attend(q_ref, k_ref, v_ref, bias_ref, p_ref, ao_ref, w, per):
    ao_ref[w, 0:HEAD, :] = jnp.zeros((HEAD, ao_ref.shape[2]), BF16)
    for i in range(per):
        h = w * per + i
        for b in range(bias_ref.shape[0]):
            keys = k_ref[h, :, b * HALO : (b + 2) * HALO]
            scores = dot_cols(keys, q_ref[h, :, b * HALO : (b + 1) * HALO]) + bias_ref[b]
            top = jnp.max(scores, 0, keepdims=True)
            raised = jnp.exp(scores - top)
            total = jnp.sum(raised, 0, keepdims=True)
            p_ref[h, b] = (raised * (1.0 / total)).astype(BF16)
            out = dot(v_ref[h, :, b * HALO : (b + 2) * HALO], p_ref[h, b])
            ao_ref[w, (i + 1) * HEAD : (i + 2) * HEAD, b * HALO : (b + 1) * HALO] = out.astype(BF16)


def out_project(st_ref, wa_ref, ao_ref, mid_ref, width, per):
    group = 3 * per * HEAD - HEAD
    mid_ref[...] = st_ref[:, HALO:].astype(F32)

    def body(w):
        mid_ref[...] += dot(wa_ref[w, :, group:], ao_ref[w])

    tiles(width, body)


def feed_forward(xt_ref, wb_ref, wc_ref, acc_ref, pre_ref, hid_ref, slope_ref, width, slab, before):
    own = xt_ref.shape[0]
    strip = 32

    def body(at):
        w = slab(at)
        before(at, w)
        pre_ref[...] = dot(xt_ref[...], wb_ref[w])

        def gelu(part):
            rows = pl.ds(pl.multiple_of(part * strip, strip), strip)
            x = pre_ref[rows, :]
            root = math.sqrt(2.0 / math.pi)
            square = x * x
            bent = jnp.tanh(root * (x + 0.044715 * (square * x)))
            hid_ref[w, rows, :] = (0.5 * x * (1.0 + bent)).astype(BF16)
            slope = 0.5 * (1.0 + bent) + (0.5 * root) * x * (1.0 - bent * bent) * (1.0 + (3 * 0.044715) * square)
            slope_ref[w, rows, :] = slope.astype(BF16)

        tiles(own // strip, gelu)
        acc_ref[...] += dot_rows(wc_ref[w], hid_ref[w])

    tiles(width, body)


def feed_back(x_ref, ct_ref, ctt_ref, wb_ref, wc_ref, gb_ref, gc_ref, u_ref, gh_ref, hid_ref, slope_ref, width, slab, between, after):
    own = x_ref.shape[1]
    strip = 32
    u_ref[...] = jnp.zeros_like(u_ref)

    def body(at):
        w = slab(at)
        gh_ref[...] = dot(ctt_ref[...], wc_ref[w])
        between(at, w)

        def multiply(part):
            rows = pl.ds(pl.multiple_of(part * strip, strip), strip)
            slope_ref[w, rows, :] = (gh_ref[rows, :] * slope_ref[w, rows, :].astype(F32)).astype(BF16)

        tiles(own // strip, multiply)
        gc_ref[w] = dot(ct_ref[...], hid_ref[w]).astype(BF16)
        u_ref[...] += dot_rows(wb_ref[w], slope_ref[w])
        gb_ref[w] = dot(x_ref[...], slope_ref[w]).astype(BF16)
        after(at, w)

    tiles(width, body)


def attend_back(low_ref, wo_ref, p_ref, q_ref, k_ref, v_ref, trig_ref, gp_ref, width, per, own, hook):
    ext = HALO + own
    group = per * HEAD
    blocks = own // HALO
    scale = HEAD**-0.5

    def body(w):
        hook(w)
        gp_ref[w, 3 * group :, :] = jnp.zeros((group, ext), BF16)
        gp_ref[w, :group, :HALO] = jnp.zeros((group, HALO), BF16)
        upstream = dot(wo_ref[w], low_ref[...]).astype(BF16)
        for i in range(per):
            h = w * per + i
            grad_keys, grad_values = [None] * (blocks + 1), [None] * (blocks + 1)
            for b in range(blocks):
                q = q_ref[h, :, b * HALO : (b + 1) * HALO]
                k = k_ref[h, :, b * HALO : (b + 2) * HALO]
                v = v_ref[h, :, b * HALO : (b + 2) * HALO]
                up = upstream[i * HEAD : (i + 1) * HEAD, b * HALO : (b + 1) * HALO]
                weights = p_ref[h, b]
                wide = weights.astype(F32)
                grad_weights = dot_cols(v, up)
                inner = jnp.sum(wide * grad_weights, 0, keepdims=True)
                grad_scores = (wide * (grad_weights - inner)).astype(BF16)
                gv = dot_rows(up, weights)
                gk = dot_rows(q, grad_scores)
                gq = dot(k, grad_scores) * scale
                cols = slice((b + 1) * HALO, (b + 2) * HALO)
                gp_ref[w, i * HEAD : (i + 1) * HEAD, cols] = rotated(gq, trig_ref[0, :, cols], -trig_ref[1, :, cols]).astype(BF16)
                for part in range(2):
                    piece = slice(part * HALO, (part + 1) * HALO)
                    at = b + part
                    grad_keys[at] = gk[:, piece] if grad_keys[at] is None else grad_keys[at] + gk[:, piece]
                    grad_values[at] = gv[:, piece] if grad_values[at] is None else grad_values[at] + gv[:, piece]
            for at in range(blocks + 1):
                cols = slice(at * HALO, (at + 1) * HALO)
                gp_ref[w, group + i * HEAD : group + (i + 1) * HEAD, cols] = rotated(
                    grad_keys[at], trig_ref[0, :, cols], -trig_ref[1, :, cols]
                ).astype(BF16)
                gp_ref[w, 2 * group + i * HEAD : 2 * group + (i + 1) * HEAD, cols] = grad_values[at].astype(BF16)

    tiles(width, body)


def stream_back(wa_ref, gp_ref, u_ref, start, size, width):
    cols = slice(start, start + size)
    u_ref[:, cols] = dot(wa_ref[0], gp_ref[0, :, cols])

    def body(at):
        u_ref[:, cols] += dot(wa_ref[at + 1], gp_ref[at + 1, :, cols])

    tiles(width - 1, body)


def project_back(x_ref, low_ref, ao_ref, gp_ref, ga_ref, width, per, slab, before, after):
    group = 3 * per * HEAD - HEAD

    def body(at):
        w = slab(at)
        before(at, w)
        ga_ref[w, :, :group] = dot_rows(x_ref[...], gp_ref[w, :group, :]).astype(BF16)
        ga_ref[w, :, group:] = (
            dot_rows(x_ref[...], gp_ref[w, group:, :]) + dot_rows(low_ref[...], ao_ref[w])
        ).astype(BF16)
        after(at, w)

    tiles(width, body)


def block_kernel(width, rows, per, mix_ref, hist_ref, cot_ref, seg_ref, box_ref, own_ref, given_ref,
                 gcol_ref, bout_ref, small_ref, total_ref, left_ref,
                 full, st, ct, boxes_in, gain, x_one, stat_one, starts, trig, q, k, v, wo, ao, prob, mid, stat_two, gmid, low, blk,
                 gacc_one, gacc_two, halo_out, halo_in, macc, small_out, small_in, small_step,
                 last_box, boxes, load_sem, here_sem, send_sem, recv_sem):
    r, z = lax.axis_index("rows"), lax.axis_index("width")
    layers, piece, tokens = hist_ref.shape
    own = tokens // width
    ext = HALO + own
    per_row = seg_ref.shape[1] // own
    core, bits = row_bits(rows)
    hops = len(bits)
    cut = own // 2
    greet(z, r, width, [core] + bits)
    sends = Sends(send_sem, recv_sem)
    inside = own_ref is not None
    gathers = []
    if inside:
        gathers = [Gather(sends, at, own_ref.at[at], full.at[at], z, r, width, rows) for at in range(3)]
        first, second, third = gathers
    slab = functools.partial(arrival, z, width=width)

    def each(*actions):
        for method, chosen, distances in actions:
            for away in distances:
                if away == 0:
                    for one in chosen:
                        getattr(one, method)(z)
                    continue
                for w, there in ((z - away, z >= away), (z + away, z + away < width)):
                    @pl.when(there)
                    def _(w=w, method=method, chosen=chosen):
                        for one in chosen:
                            getattr(one, method)(w)
    odd = lax.rem(z, 2) == 1
    mine = pl.ds(pl.multiple_of(z * piece, 16), piece)

    far = 1 - z // 2
    chunks = []
    for at in range(width):
        low_half = flip(far, 1) if at // 2 else far
        chunks.append(2 * low_half + at % 2)
    st_even = st.at[mine, pl.ds(HALO, own)]
    st_odd = st.at[mine, :]
    gain_sends = [sends.make(box_ref, boxes_in.at[z], (r, lax.rem(z + step, width))) for step in range(1, width)]
    base = sends.used
    sends.used += width - 1

    def scoped_stream(pair, mixed):
        def load(at):
            cols = pl.ds(pl.multiple_of(chunks[at // 2] * own + (at % 2) * cut, LANES), cut)
            return pltpu.make_async_copy(hist_ref.at[:, :, cols], pair.at[at % 3], load_sem.at[at % 3])

        def stream_copy(step, target, is_odd):
            start = pl.multiple_of(target * own, LANES)
            if is_odd:
                src, dst = mixed.at[:, pl.ds(pl.multiple_of(start - HALO, LANES), ext)], st_odd
            else:
                src, dst = mixed.at[:, pl.ds(start, own)], st_even
            return pltpu.make_async_remote_copy(
                src_ref=src, dst_ref=dst, send_sem=send_sem.at[base + step - 1], recv_sem=recv_sem.at[base + step - 1],
                device_id=(r, target), device_id_type=MESH,
            )

        for at in range(3):
            load(at).start()
        for gather in gathers:
            gather.start()
        for copy in gain_sends:
            copy.start()
        boxes_in[z] = box_ref[...]
        for at in range(2 * width):
            load(at).wait()
            target = chunks[at // 2]
            start = pl.multiple_of(target * own + (at % 2) * cut, LANES)
            mix_stream(mix_ref, pair.at[at % 3], mixed, pl.ds(start, cut), layers)
            if at + 3 < 2 * width:
                load(at + 3).start()
            if at % 2 == 0:
                continue
            is_odd = at // 2 % 2 == 1
            for step in range(1, width):
                @pl.when(lax.rem(z + step, width) == target)
                def _(step=step, target=target, is_odd=is_odd):
                    stream_copy(step, target, is_odd).start()

            @pl.when(target == z)
            def _(is_odd=is_odd, target=target):
                start = pl.multiple_of(target * own, LANES)
                if is_odd:
                    st_odd[...] = mixed[:, pl.ds(pl.multiple_of(start - HALO, LANES), ext)]
                else:
                    st_even[...] = mixed[:, pl.ds(start, own)]
                    st[:, 0:HALO] = jnp.zeros((D, HALO), BF16)

        if inside:
            each(("hop", gathers, [1]), ("forward", gathers, [1]), ("to_chips", gathers, [0]))
        for copy in gain_sends:
            copy.wait()
        spread_gains(boxes_in, gain, width, piece)
        document_starts(seg_ref, starts, trig, z // per_row, lax.rem(z, per_row) * own, own)
        if inside:
            each(
                ("to_chips", gathers, [1]), ("to_core", gathers, [0]), ("hop", gathers, [2]), ("forward", gathers, [2]),
                ("to_core", gathers, [1]), ("to_chips", gathers, [2]),
            )
        for step in range(1, width):
            for is_odd in (False, True):
                @pl.when(lax.rem(z, 2) == int(is_odd))
                def _(step=step, is_odd=is_odd):
                    stream_copy(step, z, is_odd).wait_recv()

                @pl.when(lax.rem(z + step, 2) == int(is_odd))
                def _(step=step, is_odd=is_odd):
                    stream_copy(step, lax.rem(z + step, width), is_odd).wait_send()

        cot_here.start()

    cot_sends = []
    for step in range(1, width):
        target = lax.rem(z + step, width)
        cols = pl.ds(pl.multiple_of(target * own, LANES), own)
        cot_sends.append(sends.make(cot_ref.at[:, cols], ct.at[mine, :], (r, target)))
    cot_here = pltpu.make_async_copy(
        cot_ref.at[:, pl.ds(pl.multiple_of(z * own, LANES), own)], ct.at[mine, :], here_sem
    )
    if not inside:
        given = pltpu.make_async_copy(given_ref, full, load_sem.at[3])
        given.start()
    pl.run_scoped(scoped_stream, pltpu.VMEM((3, layers, piece, cut), BF16), pltpu.VMEM((piece, tokens), BF16))

    norm_forward(st, 0, gain, 0, x_one, stat_one, ext)
    if not inside:
        given.wait()

    def send_cotangent():
        for copy in cot_sends:
            copy.start()

    def scoped_attend(bias):
        attend_bias(starts, bias)
        serve = at_steps({0: [send_cotangent]})
        if inside:
            serve = at_steps({
                0: [lambda: each(("hop", gathers, [3]), ("to_core", gathers, [2])), send_cotangent],
                1: [lambda: each(("to_chips", gathers, [3]))],
                2: [lambda: each(("to_core", gathers, [3]))],
            })

        def body(at):
            w = slab(at)
            serve(at)
            if inside:
                first.take(w)
            project(x_one, full.at[0], trig, q, k, v, wo, w, per)
            attend(q, k, v, bias, prob, ao, w, per)

        tiles(width, body)

    pl.run_scoped(scoped_attend, pltpu.VMEM((own // HALO, 2 * HALO, HALO), F32))
    out_project(st, full.at[0], ao, mid, width, per)
    gmid[...] = mid[...]
    if inside:
        tiles(width, first.clear)

    scatters = []
    if inside:
        scatters = [
            Scatter(sends, at, full.at[at], [box.at[at] for box in boxes], last_box.at[at], total_ref.at[at], z, r, width, rows)
            for at in range(3)
        ]
    attending, pair_back = scatters[:1], scatters[1:]

    def back(method, chosen, at):
        for one in chosen:
            getattr(one, method)(turned(at))

    def later(method, chosen, at):
        return lambda: back(method, chosen, at)

    def turned(at):
        return slab(width - 1 - at)


    def feed_before(at, w):
        if inside:
            second.take(w)
            third.take(w)

    def feed_between(at, w):
        if inside:
            second.clear(w)
            third.clear(w)

        feed_service(at)

    feed_service = at_steps({
        1: [later("take_core", pair_back, 0)],
        3: [later("take_chips", pair_back, 0), later("take_core", pair_back, 1)],
    })

    def feed_after(at, w):
        for scatter in pair_back:
            scatter.begin(w)

    blk_sends, gs_sends = [], []
    here = pl.ds(pl.multiple_of(z * own, LANES), own)
    for step in range(1, width):
        target = lax.rem(z + step, width)
        part = pl.ds(pl.multiple_of(target * piece, 16), piece)
        blk_sends.append(sends.make(blk.at[part, :], bout_ref.at[:, here], (r, target)))

    blk_here = pltpu.make_async_copy(blk.at[mine, :], bout_ref.at[:, here], load_sem.at[3])

    def scoped_feed(x_two, turn, pre, hid, slope, u_two):
        norm_forward(mid, 0, gain, 1, x_two, stat_two, own)
        turn[...] = jnp.transpose(x_two[...])
        feed_forward(turn, full.at[1], full.at[2], gmid, pre, hid, slope, width, slab, feed_before)
        blk[...] = gmid[...].astype(BF16)
        for copy in blk_sends:
            copy.start()
        blk_here.start()
        for copy in cot_sends:
            copy.wait()
        cot_here.wait()
        turn[...] = jnp.transpose(ct[...])
        feed_back(
            x_two, ct, turn, full.at[1], full.at[2], full.at[1], full.at[2], u_two, pre, hid, slope, width, turned, feed_between, feed_after
        )

        def write(cols, value):
            gmid[:, cols] = value
            low[:, cols] = value.astype(BF16)

        gacc_two[...] = jnp.zeros_like(gacc_two)
        norm_back(u_two, 0, mid, 0, stat_two, 0, gain, 1, lambda cols: ct[:, cols].astype(F32), write, gacc_two, 0, own)

    pl.run_scoped(
        scoped_feed, pltpu.VMEM((D, own), BF16), pltpu.VMEM((own, D), BF16), pltpu.VMEM((own, D), F32),
        pltpu.VMEM((width, own, D), BF16), pltpu.VMEM((width, own, D), BF16), pltpu.VMEM((D, own), F32),
    )

    when_attend = at_steps({
        2: [later("take_chips", pair_back, 1), later("take_core", pair_back, 2), later("take_last", pair_back, 0)],
    })
    when_mix = {
        3: [
            later("take_chips", attending, 0), later("take_chips", attending, 1), later("take_core", attending, 2),
            later("take_core", attending, 3), later("take_last", pair_back, 3),
        ],
        7: [
            later("take_chips", attending, 2), later("take_chips", attending, 3), later("take_last", attending, 0),
            later("take_last", attending, 1),
        ],
    }
    halo = sends.make(halo_out, halo_in, (r, flip(z, 1)))
    half = own // 2
    for part in range(2):
        columns = pl.ds(pl.multiple_of(z * own + part * half, LANES), half)
        for step in range(1, width):
            target = lax.rem(z + step, width)
            features = pl.ds(pl.multiple_of(target * piece, 16), piece)
            gs_sends.append(
                sends.make(blk.at[features, pl.ds(part * half, half)], gcol_ref.at[:, columns], (r, target))
            )

    def scoped_back(gp, u):
        def send_stream(part):
            def write(cols, value):
                blk[:, cols] = value.astype(BF16)

            norm_back(
                u, HALO, st, HALO, stat_one, HALO, gain, 0, lambda cols: gmid[:, cols], write, gacc_one, part * half, half
            )
            for copy in gs_sends[part * (width - 1) : (part + 1) * (width - 1)]:
                copy.start()
            columns = pl.ds(pl.multiple_of(z * own + part * half, LANES), half)
            gcol_ref[:, columns] = blk[mine, pl.ds(part * half, half)]

        attend_back(low, wo, prob, q, k, v, trig, gp, width, per, own, when_attend)
        stream_back(full.at[0], gp, u, 0, HALO, width)

        @pl.when(odd)
        def _():
            halo_out[...] = u[:, 0:HALO].astype(BF16)
            halo.start()

        stream_back(full.at[0], gp, u, HALO, own, width)
        gacc_one[...] = jnp.zeros_like(gacc_one)
        for copy in blk_sends:
            copy.wait_send()
        blk_here.wait()
        send_stream(0)
        back("take_chips", pair_back, 2)
        back("take_core", pair_back, 3)
        back("take_last", pair_back, 1)

        def after_project(at, w):
            for scatter in attending:
                scatter.begin(w)

        project_back(x_one, low, ao, gp, full.at[0], width, per, turned, lambda at, w: None, after_project)

        @pl.when(jnp.logical_not(odd))
        def _():
            halo.wait_recv()
            u[:, own : own + HALO] += halo_in[...].astype(F32)

        send_stream(1)
        back("take_chips", pair_back, 3)
        back("take_core", attending, 0)
        back("take_core", attending, 1)
        back("take_last", pair_back, 2)

    pl.run_scoped(scoped_back, pltpu.VMEM((width, 4 * per * HEAD, ext), BF16), pltpu.VMEM((D, ext), F32))

    macc[...] = jnp.zeros_like(macc)
    strip = 16

    def scoped_mix(pair):
        def place(at):
            chunk = lax.rem(z + width - at % width, width)
            return pl.ds(pl.multiple_of(chunk * own + (at // width) * half, LANES), half)

        def load(at):
            return pltpu.make_async_copy(hist_ref.at[:, :, place(at)], pair.at[at % 3], load_sem.at[at % 3])

        for at in range(3):
            load(at).start()
        for at in range(2 * width):
            if at % width:
                gs_sends[at // width * (width - 1) + at % width - 1].wait_recv()
            load(at).wait()
            cols = place(at)

            def body(row, at=at, cols=cols):
                part = pl.ds(pl.multiple_of(row * strip, strip), strip)
                g = gcol_ref[part, cols].astype(F32)
                for j in range(layers):
                    crossed = pair[at % 3, j, part, :].astype(F32) * g
                    folded = crossed[:8] + crossed[8:]
                    total = folded[:, :LANES]
                    for lane in range(1, cut // LANES):
                        total = total + folded[:, lane * LANES : (lane + 1) * LANES]
                    macc[j] += total

            tiles(piece // strip, body)
            if at + 3 < 2 * width:
                load(at + 3).start()
            for action in when_mix.get(at, ()):
                action()

    pl.run_scoped(scoped_mix, pltpu.VMEM((3, layers, piece, cut), BF16))

    small_out[...] = jnp.zeros_like(small_out)
    gain_one = jnp.sum(jnp.transpose(gacc_one[...]), 0, keepdims=True)
    gain_two = jnp.sum(jnp.transpose(gacc_two[...]), 0, keepdims=True)
    depth = jnp.sum(jnp.transpose(jnp.sum(macc[...], 1)), 0, keepdims=True)
    for w in range(width):
        small_out[w, 0:1, 0:piece] = gain_one[:, w * piece : (w + 1) * piece]
        small_out[w, 1:2, 0:piece] = gain_two[:, w * piece : (w + 1) * piece]
        small_out[w, 2:3, 0 : depth.shape[1]] = depth
    small_sends = [
        sends.make(small_out.at[lax.rem(z + step, width)], small_in.at[step - 1], (r, lax.rem(z + step, width)))
        for step in range(1, width)
    ]
    for copy in small_sends:
        copy.start()
    current = small_out[z]
    for step in range(1, width):
        small_sends[step - 1].wait_recv()
        current = current + small_in[step - 1]
    for at, bit in enumerate([core] + bits):
        small_step[at, 0] = current
        copy = sends.make(small_step.at[at, 0], small_step.at[at, 1], (flip(r, bit), z))
        copy.start()
        copy.wait_recv()
        current = current + small_step[at, 1]
        small_sends.append(copy)
    small_ref[...] = current
    back("take_last", attending, 2)
    back("take_last", attending, 3)
    for scatter in scatters:
        scatter.finish()
    for copy in blk_sends:
        copy.wait_recv()
    for copy in gs_sends + small_sends:
        copy.wait_send()

    @pl.when(odd)
    def _():
        halo.wait_send()

    for scatter in scatters:
        scatter.end()
    if not inside:
        leave = pltpu.make_async_copy(full, left_ref, load_sem.at[3])
        leave.start()
        leave.wait()


def vmem(count):
    return [pl.BlockSpec(memory_space=pltpu.VMEM)] * count


def shape(*sizes, dtype=F32):
    return jax.ShapeDtypeStruct(sizes, dtype)


def block(width, rows, mix, history, cotangent, segments, box, own_three):
    layers, piece, tokens = history.shape
    shard = own_three.shape[1]
    own = tokens // width
    ext = HALO + own
    heads = D // HEAD
    per = heads // width
    group = per * HEAD
    blocks = own // HALO
    digits = rows.bit_length() - 1
    inside = shard % 16 == 0
    any_space = pl.BlockSpec(memory_space=pl.ANY)
    ins = [mix, history, cotangent, segments, box]
    specs = [pl.BlockSpec(memory_space=pltpu.SMEM), any_space, any_space] + vmem(2)
    outs = [shape(piece, tokens, dtype=BF16), shape(piece, tokens, dtype=BF16), shape(8, 2 * LANES)]
    out_specs = vmem(1) + [any_space] + vmem(1)
    box_shapes = []
    if inside:
        ins, specs = ins + [own_three], specs + vmem(1)
        outs, out_specs = outs + [shape(3, shard, D)], out_specs + vmem(1)
        box_shapes = Scatter.box_shapes(width, rows, shard)
    else:
        gathered = lax.all_gather(lax.all_gather(own_three, "rows", axis=1, tiled=True), "width", axis=1)
        ins, specs = ins + [gathered], specs + [any_space]
        outs, out_specs = outs + [shape(3, width, D, D, dtype=BF16)], out_specs + [any_space]
    low = lambda *sizes: pltpu.VMEM(sizes, BF16)
    full = lambda *sizes: pltpu.VMEM(sizes, F32)
    scratch = [
        low(3, width, D, D), low(D, ext), low(D, own), full(width, 8, 2 * LANES), full(2, D, LANES), low(D, ext), full(8, ext),
        full(8, HALO + segments.shape[1]), full(2, HEAD // 2, ext), low(heads, HEAD, own), low(heads, HEAD, ext), low(heads, HEAD, ext),
        low(width, group, D), low(width, HEAD + group, own), low(heads, blocks, 2 * HALO, HALO), full(D, own), full(8, own),
        full(D, own), low(D, own), low(D, own), full(D, LANES), full(D, LANES), low(D, HALO), low(D, HALO), full(layers, 8, LANES),
        full(width, 8, 2 * LANES), full(width - 1, 8, 2 * LANES), full(digits, 2, 8, 2 * LANES),
    ]
    common = len(scratch)
    if inside:
        scratch += [low(3, width - 1, shard, D)] + [low(3, *one) for one in box_shapes]
    count = 6 * (width - 1) + 1 + (width - 1) + digits
    count += 3 * Gather.copies(width, rows) + 3 * Scatter.copies(width, rows)
    scratch += [
        pltpu.SemaphoreType.DMA((4,)), pltpu.SemaphoreType.DMA, pltpu.SemaphoreType.DMA((count,)), pltpu.SemaphoreType.DMA((count,)),
    ]

    def kernel(*refs):
        given, found, rest = refs[:6], refs[6:10], refs[10:]
        weights = (given[5], None) if inside else (None, given[5])
        results = (found[3], None) if inside else (None, found[3])
        kept, rest = rest[:common], rest[common:]
        last_box, boxes = None, ()
        if inside:
            last_box, boxes, rest = rest[0], rest[1 : 1 + len(box_shapes)], rest[1 + len(box_shapes) :]
        block_kernel(width, rows, per, *given[:5], *weights, *found[:3], *results, *kept, last_box, boxes, *rest)

    found = pl.pallas_call(
        kernel,
        out_shape=outs,
        in_specs=specs,
        out_specs=out_specs,
        scratch_shapes=scratch,
        compiler_params=pltpu.CompilerParams(collective_id=0, has_side_effects=True, vmem_limit_bytes=64 * MIB - 128 * 1024),
    )(*ins)
    if inside:
        return found
    total = lax.psum_scatter(found[3], "width", scatter_dimension=1)
    return (*found[:3], lax.psum_scatter(total, "rows", scatter_dimension=1, tiled=True).astype(F32))


def prepare_kernel(attend_ref, output_ref, expand_ref, reduce_ref, gains_ref, own_ref, box_ref):
    parts = [attend_ref[k] for k in range(3)] + [jnp.transpose(output_ref[...])]
    own_ref[0] = jnp.concatenate(parts, 1).astype(BF16)
    own_ref[1] = expand_ref[...].astype(BF16)
    own_ref[2] = reduce_ref[...].astype(BF16)
    box_ref[...] = jnp.zeros_like(box_ref)
    box_ref[0:2, 0 : gains_ref.shape[1]] = gains_ref[...]


def prepare(w_attend, w_output, w_expand, w_reduce, gains):
    shard, piece = w_expand.shape[0], gains.shape[1]
    if shard % 16 == 0:
        return pl.pallas_call(
            prepare_kernel,
            out_shape=[shape(3, shard, D, dtype=BF16), shape(8, 2 * LANES)],
            in_specs=vmem(5),
            out_specs=vmem(2),
            compiler_params=pltpu.CompilerParams(vmem_limit_bytes=60 * MIB),
        )(w_attend, w_output, w_expand, jnp.transpose(w_reduce), gains)
    first = jnp.concatenate([w_attend[0], w_attend[1], w_attend[2], jnp.transpose(w_output)], 1)
    own_three = jnp.stack([first, w_expand, jnp.transpose(w_reduce)]).astype(BF16)
    return own_three, jnp.pad(gains, ((0, 8 - gains.shape[0]), (0, 2 * LANES - piece)))


def finish_kernel(per_step, mix_ref, grad_ref, total_ref, out_ref, *refs):
    weights, (hist_ref, block_ref, *news) = refs[:12], refs[12:]
    at = pl.program_id(0)
    piece = grad_ref.shape[0]
    strip = 16

    def body(row):
        rows = pl.ds(pl.multiple_of(row * strip, strip), strip)
        g = grad_ref[rows, :].astype(F32)
        for j in range(per_step):
            hist_ref[j, rows, :] = (mix_ref[at * per_step + j] * g).astype(BF16)

    tiles(piece // strip, body)

    def update(which, gradient, rate):
        found = optimize(weights[3 * which][...], gradient, weights[3 * which + 1][...], weights[3 * which + 2][...], rate, DECAY)
        for ref, value in zip(news[3 * which : 3 * which + 3], found):
            ref[...] = value

    @pl.when(at == 0)
    def _():
        for k in range(3):
            gradient = total_ref[0, :, k * piece : (k + 1) * piece]
            found = optimize(weights[0][k], gradient, weights[1][k], weights[2][k], RATE_MATRIX, DECAY)
            for ref, value in zip(news[:3], found):
                ref[k] = value

    @pl.when(at == 1)
    def _():
        update(1, jnp.transpose(total_ref[0, :, 3 * piece :]), RATE_OUTPUT)

    @pl.when(at == 2)
    def _():
        update(2, total_ref[1], RATE_MATRIX)

    @pl.when(at == 3)
    def _():
        update(3, total_ref[2], RATE_MATRIX)
        block_ref[...] = out_ref[...]


def finish(mix, grad_stream, total, block_output, layers, weights):
    shard = total.shape[1]
    piece, tokens = grad_stream.shape
    if shard % 16 == 0 and layers % 5 == 0:
        weights = [jnp.transpose(one) if at // 3 == 3 else one for at, one in enumerate(weights)]
        held = [shape(*one.shape) for one in weights]
        per_step = layers // 5
        history_grad, block_output, *news = pl.pallas_call(
            functools.partial(finish_kernel, per_step),
            grid=(5,),
            out_shape=[shape(layers, piece, tokens, dtype=BF16), shape(piece, tokens, dtype=BF16)] + held,
            in_specs=[pl.BlockSpec(memory_space=pltpu.SMEM)] + vmem(3 + len(weights)),
            out_specs=[pl.BlockSpec((per_step, piece, tokens), lambda at: (at, 0, 0))] + vmem(1 + len(weights)),
            compiler_params=pltpu.CompilerParams(vmem_limit_bytes=60 * MIB),
        )(mix, grad_stream, total, block_output, *weights)
        return (history_grad, block_output, *[jnp.transpose(one) if at // 3 == 3 else one for at, one in enumerate(news)])
    history_grad = (mix[:, None, None] * grad_stream[None].astype(F32)).astype(BF16)
    first = total[0]
    gradients = (
        jnp.stack([first[:, k * piece : (k + 1) * piece] for k in range(3)]),
        jnp.transpose(first[:, 3 * piece :]), total[1], jnp.transpose(total[2]),
    )
    news = []
    for at, rate in enumerate((RATE_MATRIX, RATE_OUTPUT, RATE_MATRIX, RATE_MATRIX)):
        w, m, v = weights[3 * at : 3 * at + 3]
        news += optimize(w, gradients[at], m, v, rate, DECAY)
    return (history_grad, block_output, *news)


def on_device(
    width, rows, history, cotangent, segments, w_attend, m_attend, v_attend, w_output, m_output, v_output,
    w_expand, m_expand, v_expand, w_reduce, m_reduce, v_reduce, gains, m_gains, v_gains, mix, m_mix, v_mix,
):
    layers, piece, _ = history.shape
    own_three, box = prepare(w_attend, w_output, w_expand, w_reduce, gains)
    grad_stream, block_output, small, total = block(width, rows, mix, history, cotangent, segments, box, own_three)
    weights = (
        w_attend, m_attend, v_attend, w_output, m_output, v_output, w_expand, m_expand, v_expand, w_reduce, m_reduce, v_reduce,
    )
    history_grad, block_output, *news = finish(mix, grad_stream, total, block_output, layers, weights)
    new_gains = optimize(gains, small[0:2, :piece], m_gains, v_gains, RATE_GAIN, 0.0)
    new_mix = optimize(mix, small[2, :layers], m_mix, v_mix, RATE_MIX, 0.0)
    return (block_output, history_grad, *news, *new_gains, *new_mix)


def solution(mesh):
    square, tall, wide = P(None, "rows", "width"), P("width", "rows"), P("rows", "width")
    weights = (square,) * 3 + (tall,) * 3 + (wide,) * 3 + (tall,) * 3 + (P(None, "width"),) * 3 + (P(),) * 3
    return jax.shard_map(
        functools.partial(on_device, mesh.shape["width"], mesh.shape["rows"]),
        mesh=mesh,
        in_specs=(P(None, "width", "rows"), P("width", "rows"), P("rows", None)) + weights,
        out_specs=(P("width", "rows"), P(None, "width", "rows")) + weights,
        check_vma=False,
    )
```

```python
import functools
import math
from types import SimpleNamespace

import jax
import jax.numpy as jnp
from jax import lax
from jax.experimental import pallas as pl
from jax.experimental.pallas import tpu as pltpu
from jax.sharding import PartitionSpec as P

D = 768
HEAD = 64
STEP = 10
HALO = 256
LANES = 128


EPS_NORM = 1e-05
EPS_ADAM = 1e-08
BETA_ONE = 0.9
BETA_TWO = 0.95
RATE_MATRIX = 0.02
RATE_OUTPUT = 0.12
RATE_GAIN = 0.4
RATE_MIX = 0.05
DECAY = 0.1
MASKED = -1e30

MESH = pl.DeviceIdType.MESH
F32 = jnp.float32
BF16 = jnp.bfloat16
MIB = 1 << 20


def optimize(weight, gradient, first_moment, second_moment, rate, decay):
    first_moment = BETA_ONE * first_moment + (1.0 - BETA_ONE) * gradient
    second_moment = BETA_TWO * second_moment + (1.0 - BETA_TWO) * gradient * gradient
    first_fixed = first_moment / (1.0 - BETA_ONE**STEP)
    second_fixed = second_moment / (1.0 - BETA_TWO**STEP)
    weight = weight - rate * (first_fixed / (jnp.sqrt(second_fixed) + EPS_ADAM) + decay * weight)
    return (weight, first_moment, second_moment)


def flip(index, bit):
    return index + bit - 2 * bit * lax.rem(lax.div(index, jnp.int32(bit)), 2)


def flips(index, bits):
    for bit in bits:
        index = flip(index, bit)
    return index


def subsets(bits):
    found = [()]
    for bit in bits:
        found = found + [one + (bit,) for one in found]
    return found


def row_bits(rows):
    digits = [1 << place for place in range(rows.bit_length() - 1)]
    return digits[0], digits[1:]


def tiles(count, body):
    def step(at, carry):
        body(at)
        return carry

    lax.fori_loop(0, count, step, 0)


def lane_tile(at, size=LANES, base=0):
    return pl.ds(pl.multiple_of(base + at * size, LANES), size)


def dot(a, b):
    return jnp.dot(a, b, preferred_element_type=F32)


def dot_rows(a, b):
    return lax.dot_general(a, b, (((1,), (1,)), ((), ())), preferred_element_type=F32)


def dot_cols(a, b):
    return lax.dot_general(a, b, (((0,), (0,)), ((), ())), preferred_element_type=F32)


def greet(z, r, width, bits):
    bar = pltpu.get_barrier_semaphore()
    places = [(r, lax.rem(z + k, width)) for k in range(1, width)] + [(flip(r, b), z) for b in bits]
    for place in places:
        pl.semaphore_signal(bar, inc=1, device_id=place, device_id_type=MESH)
    pl.semaphore_wait(bar, len(places))


def at_steps(table):
    def hook(step):
        for at, actions in table.items():
            @pl.when(step == at)
            def _(actions=actions):
                for action in actions:
                    action()

    return hook


class Sends:
    def __init__(self, send, recv):
        self.send, self.recv, self.used = send, recv, 0

    def reserve(self, count):
        at = self.used
        self.used += count
        return at

    def copy(self, at, src, dst, place):
        return pltpu.make_async_remote_copy(
            src_ref=src, dst_ref=dst, send_sem=self.send.at[at], recv_sem=self.recv.at[at],
            device_id=place, device_id_type=MESH,
        )

    def make(self, src, dst, place):
        return self.copy(self.reserve(1), src, dst, place)


def arrival(z, at, width):
    found = 0
    for own in range(width):
        order = sorted(range(width), key=lambda w, own=own: (abs(w - own), w))
        for place, w in enumerate(order):
            if w:
                found = found + w * jnp.where((z == own) & (at == place), 1, 0)
    return found


class Plane:
    def __init__(self, chunk, z, r, width, rows, shard):
        self.core, self.bits = row_bits(rows)
        self.chunk, self.z, self.r, self.width, self.shard = chunk, z, r, width, shard
        self.hops = len(self.bits)
        self.per_slab = 2 ** (self.hops + 1) - 1

    def rows(self, index):
        return pl.ds(pl.multiple_of(index * self.shard, 16), self.shard)

    def bit(self, w, at):
        one, other = self.bits[at], self.bits[::-1][at]
        return one + (other - one) * lax.rem(w + self.chunk, 2)

    def place(self, index, w, code):
        for at in range(self.hops):
            if code >> at & 1:
                index = flip(index, self.bit(w, at))
        return index


class Gather(Plane):
    def __init__(self, sends, chunk, own, full, z, r, width, rows):
        super().__init__(chunk, z, r, width, rows, own.shape[0])
        self.sends, self.own, self.full = sends, own, full
        self.line_base = sends.reserve(2 * (width - 1))
        self.slab_base = sends.reserve(width * self.per_slab)

    @staticmethod
    def copies(width, rows):
        return 2 * (width - 1) + width * (rows // 2 * 2 - 1)

    def line(self, w, up, distance, target):
        part = self.full.at[w, self.rows(self.r)]
        at = self.line_base + (1 - up) * (self.width - 1) + distance
        return self.sends.copy(at, part, part, (self.r, target))

    def hold(self):
        self.full[self.z, self.rows(self.r), :] = self.own[...]

    def start(self, w):
        for up, there, target in ((1, self.z + 1 < self.width, self.z + 1), (0, self.z > 0, self.z - 1)):
            @pl.when(there)
            def _(up=up, target=target):
                self.line(self.z, up, 0, target).start()

    def hop(self, w):
        up = jnp.where(w < self.z, 1, 0)
        distance = (self.z - w) * (2 * up - 1)
        self.line(w, up, distance - 1, self.z).wait_recv()
        self.spread(w)

    def onward(self, w):
        up = jnp.where(w < self.z, 1, 0)
        distance = (self.z - w) * (2 * up - 1)
        target = self.z + 2 * up - 1
        return (target >= 0) & (target < self.width), self.line(w, up, distance, target)

    def forward(self, w):
        there, copy = self.onward(w)

        @pl.when(there)
        def _():
            copy.start()

    def step(self, w, at):
        peer = flip(self.r, self.bit(w, at) if at < self.hops else self.core)
        found = []
        for code in range(2**at):
            part = self.full.at[w, self.rows(self.place(self.r, w, code))]
            found.append(self.sends.copy(self.slab_base + w * self.per_slab + 2**at - 1 + code, part, part, (peer, self.z)))
        return found

    def spread(self, w):
        for copy in self.step(w, 0):
            copy.start()

    def pass_on(self, w, at):
        for copy in self.step(w, at - 1):
            copy.wait_recv()
        for copy in self.step(w, at):
            copy.start()

    def to_chips(self, w):
        for at in range(1, self.hops):
            self.pass_on(w, at)

    def to_core(self, w):
        if self.hops:
            self.pass_on(w, self.hops)

    def take(self, w):
        for copy in self.step(w, self.hops):
            copy.wait_recv()

    def clear(self, w):
        for at in range(self.hops + 1):
            for copy in self.step(w, at):
                copy.wait_send()

        @pl.when(w == self.z)
        def _():
            for up, there, target in ((1, self.z + 1 < self.width, self.z + 1), (0, self.z > 0, self.z - 1)):
                @pl.when(there)
                def _(up=up, target=target):
                    self.line(self.z, up, 0, target).wait_send()

        there, onward = self.onward(w)

        @pl.when((w != self.z) & there)
        def _():
            onward.wait_send()


class Scatter(Plane):
    def __init__(self, sends, chunk, along, grads, boxes, last_box, total, z, r, width, rows):
        super().__init__(chunk, z, r, width, rows, total.shape[0])
        self.sends, self.grads, self.boxes, self.last_box, self.total = sends, grads, boxes, last_box, total
        self.along = along
        self.other = flip(r, self.core)
        self.slab_base = sends.reserve(width * self.per_slab)
        self.width_base = sends.reserve(width + 1)

    @staticmethod
    def copies(width, rows):
        return width + 1 + width * (rows // 2 * 2 - 1)

    @staticmethod
    def box_shapes(width, rows, shard):
        hops = rows.bit_length() - 2
        return [(2 ** (hops - at), width, shard, D) for at in range(hops + 1)]

    def step(self, w, at):
        base = self.slab_base + w * self.per_slab
        if at == 0:
            return [
                self.sends.copy(base + code, self.grads.at[w, self.rows(self.place(self.other, w, code))], self.boxes[0].at[code, w], (self.other, self.z))
                for code in range(2**self.hops)
            ]
        base += sum(2 ** (self.hops - one) for one in range(at))
        peer = flip(self.r, self.bit(w, at - 1))
        return [
            self.sends.copy(base + code, self.boxes[at - 1].at[2 * code + 1, w], self.boxes[at].at[code, w], (peer, self.z))
            for code in range(2 ** (self.hops - at))
        ]

    def over_width(self, w):
        if self.along:
            target = self.z + jnp.where(w > self.z, 1, -1)
            slot = jnp.where((target == w) & (w < self.z), self.width, w)
        else:
            target = w
            slot = lax.rem(w - self.z + self.width, self.width) - 1
        return self.sends.copy(self.width_base + slot, self.boxes[self.hops].at[0, w], self.last_box.at[slot], (self.r, target))

    def came(self, slot):
        return self.sends.copy(self.width_base + slot, self.last_box.at[slot], self.last_box.at[slot], (self.r, flip(self.z, 1)))

    def awaited(self, w):
        return jnp.where(w > self.z, self.z, self.width - 1 - self.z) > 0

    def relay(self, w):
        if self.along:
            @pl.when((w != self.z) & self.awaited(w))
            def _():
                self.came(w).wait_recv()
                box = self.boxes[self.hops].at[0, w]
                box[...] = (box[...].astype(F32) + self.last_box[w].astype(F32)).astype(BF16)
                self.over_width(w).start()

    def begin(self, w):
        for copy in self.step(w, 0):
            copy.start()

    def take(self, w, at):
        for copy in self.step(w, at):
            copy.wait_recv()
        for code in range(2 ** (self.hops - at)):
            box = self.boxes[at].at[code, w]
            if at == 0:
                kept = self.grads.at[w, self.rows(self.place(self.r, w, code))]
            else:
                kept = self.boxes[at - 1].at[2 * code, w]
            box[...] = (box[...].astype(F32) + kept[...].astype(F32)).astype(BF16)
        if at < self.hops:
            for copy in self.step(w, at + 1):
                copy.start()
        else:
            @pl.when((w != self.z) & jnp.logical_not(self.awaited(w)) if self.along else w != self.z)
            def _():
                self.over_width(w).start()

    def take_core(self, w):
        self.take(w, 0)

    def take_chips(self, w):
        for at in range(1, self.hops):
            self.take(w, at)

    def take_last(self, w):
        if self.hops:
            self.take(w, self.hops)

    def finish(self):
        self.total[...] = self.boxes[self.hops][0, self.z].astype(F32)
        if self.along:
            arrivals = ((self.z, self.z > 0), (self.width, self.z < self.width - 1))
        else:
            arrivals = [(slot, self.z >= 0) for slot in range(self.width - 1)]
        for slot, there in arrivals:
            @pl.when(there)
            def _(slot=slot):
                self.came(slot).wait_recv()
                self.total[...] += self.last_box[slot].astype(F32)

    def end(self):
        def one(w):
            for at in range(self.hops + 1):
                for copy in self.step(w, at):
                    copy.wait_send()

            @pl.when(w != self.z)
            def _():
                self.over_width(w).wait_send()

        tiles(self.width, one)


def mix_stream(mix_ref, pair_ref, out_ref, base, layers):
    features, size = pair_ref.shape[1], pair_ref.shape[2]
    strip = 16

    def body(at):
        rows = pl.ds(pl.multiple_of(at * strip, strip), strip)
        total = mix_ref[0] * pair_ref[0, rows, :].astype(F32)
        for j in range(1, layers):
            total = total + mix_ref[j] * pair_ref[j, rows, :].astype(F32)
        out_ref[rows, base] = total.astype(BF16)

    tiles(features // strip, body)


def spread_gains(box_ref, gain_ref, width, piece):
    for w in range(width):
        for i in range(2):
            row = box_ref[w, pl.ds(i, 1), :]
            full = jnp.transpose(jnp.broadcast_to(row, (LANES, row.shape[1])))
            gain_ref[i, pl.ds(w * piece, piece), :] = full[:piece]


def norm_forward(x_ref, x_base, gain_ref, i, out_ref, stat_ref, count):
    def body(at):
        cols = lane_tile(at)
        x = x_ref[:, lane_tile(at, base=x_base)].astype(F32)
        centre = jnp.sum(x, 0, keepdims=True) / D
        spread = jnp.sum(x * x, 0, keepdims=True) / D - centre * centre
        scaling = lax.rsqrt(spread + EPS_NORM)
        out_ref[:, cols] = (gain_ref[i] * ((x - centre) * scaling)).astype(BF16)
        stat_ref[0:1, cols] = centre
        stat_ref[1:2, cols] = scaling

    tiles(count // LANES, body)


def norm_back(u_ref, u_base, x_ref, x_base, stat_ref, stat_base, gain_ref, i, residual, write, gain_acc, start, count):
    def body(step):
        at = step + start // LANES
        u = u_ref[:, lane_tile(at, base=u_base)].astype(F32)
        x = x_ref[:, lane_tile(at, base=x_base)].astype(F32)
        cols = lane_tile(at, base=stat_base)
        scaling = stat_ref[1:2, cols]
        centred = (x - stat_ref[0:1, cols]) * scaling
        gain_acc[...] += u * centred
        s = u * gain_ref[i]
        mean_s = jnp.sum(s, 0, keepdims=True) / D
        mean_c = jnp.sum(s * centred, 0, keepdims=True) / D
        write(lane_tile(at), residual(lane_tile(at)) + scaling * (s - mean_s - centred * mean_c))

    tiles(count // LANES, body)


def document_starts(seg_ref, start_ref, trig_ref, row, own_at, own):
    seg = seg_ref[pl.ds(row, 1), :]
    length = seg.shape[1]
    place = lax.broadcasted_iota(jnp.int32, (8, length), 1)
    seg = jnp.broadcast_to(seg, (8, length))
    before = pltpu.roll(seg, 1, 1)
    start = jnp.where((place > 0) & (seg == before), 0, place)
    step = 1
    while step < length:
        moved = pltpu.roll(start, step, 1)
        start = jnp.maximum(start, jnp.where(place >= step, moved, 0))
        step *= 2
    position = (place - start).astype(F32)
    scratch = start_ref.at[0:8]
    ext = HALO + own
    scratch[:, pl.ds(0, HALO)] = jnp.zeros((8, HALO), F32)
    scratch[:, pl.ds(HALO, length)] = position
    window = scratch[:, pl.ds(pl.multiple_of(own_at, LANES), ext)][0:1]
    half = HEAD // 2
    freq = jnp.exp(
        lax.broadcasted_iota(jnp.int32, (half, ext), 0).astype(F32) * (-2.0 * math.log(10000.0) / HEAD)
    )
    angle = freq * window
    trig_ref[0] = jnp.cos(angle)
    trig_ref[1] = jnp.sin(angle)
    scratch[:, pl.ds(HALO, length)] = start.astype(F32)
    kept = scratch[:, pl.ds(pl.multiple_of(own_at, LANES), ext)]
    scratch[:, pl.ds(0, ext)] = kept - (own_at - HALO).astype(F32)


def rotated(heads, cosine, sine):
    half = HEAD // 2
    a, b = heads[:half], heads[half:]
    return jnp.concatenate([a * cosine - b * sine, b * cosine + a * sine], 0)


def project(x_ref, wa_ref, trig_ref, q_ref, k_ref, v_ref, w, per):
    group = per * HEAD
    scale = HEAD**-0.5
    turned = jnp.transpose(wa_ref[w])
    queries = dot(turned[:group], x_ref[:, HALO:])
    cosine, sine = trig_ref[0], trig_ref[1]
    for i in range(per):
        rows = queries[i * HEAD : (i + 1) * HEAD]
        q_ref[w * per + i] = (rotated(rows, cosine[:, HALO:], sine[:, HALO:]).astype(BF16) * scale).astype(BF16)
    keys = dot(turned[group : 2 * group], x_ref[...])
    for i in range(per):
        rows = keys[i * HEAD : (i + 1) * HEAD]
        k_ref[w * per + i] = rotated(rows, cosine, sine).astype(BF16)
    values = dot(turned[2 * group : 3 * group], x_ref[...])
    for i in range(per):
        v_ref[w * per + i] = values[i * HEAD : (i + 1) * HEAD].astype(BF16)


def attend_bias(start_ref, bias_ref):
    for b in range(bias_ref.shape[0]):
        key_at = lax.broadcasted_iota(jnp.int32, (2 * HALO, HALO), 0).astype(F32) + float(b * HALO)
        query_at = lax.broadcasted_iota(jnp.int32, (2 * HALO, HALO), 1).astype(F32) + float((b + 1) * HALO)
        first = start_ref[0:1, (b + 1) * HALO : (b + 2) * HALO]
        bias_ref[b] = jnp.where((key_at >= first) & (key_at <= query_at), 0.0, MASKED)


def attend(q_ref, k_ref, v_ref, bias_ref, p_ref, ao_ref, w, per):
    ao_ref[w, 0:HEAD, :] = jnp.zeros((HEAD, ao_ref.shape[2]), BF16)
    for i in range(per):
        h = w * per + i
        for b in range(bias_ref.shape[0]):
            keys = k_ref[h, :, b * HALO : (b + 2) * HALO]
            scores = dot_cols(keys, q_ref[h, :, b * HALO : (b + 1) * HALO]) + bias_ref[b]
            top = jnp.max(scores, 0, keepdims=True)
            raised = jnp.exp(scores - top)
            total = jnp.sum(raised, 0, keepdims=True)
            p_ref[h, b] = (raised * (1.0 / total)).astype(BF16)
            out = dot(v_ref[h, :, b * HALO : (b + 2) * HALO], p_ref[h, b])
            ao_ref[w, (i + 1) * HEAD : (i + 2) * HEAD, b * HALO : (b + 1) * HALO] = out.astype(BF16)


def out_project(st_ref, wa_ref, ao_ref, mid_ref, width, per):
    group = 3 * per * HEAD - HEAD
    mid_ref[...] = st_ref[:, HALO:].astype(F32)

    def body(w):
        mid_ref[...] += dot(wa_ref[w, :, group:], ao_ref[w])

    tiles(width, body)


def feed_forward(xt_ref, wb_ref, wc_ref, acc_ref, pre_ref, hid_ref, slope_ref, width, slab, before):
    own = xt_ref.shape[0]
    strip = 32

    def body(at):
        w = slab(at)
        before(at, w)
        pre_ref[...] = dot(xt_ref[...], wb_ref[w])

        def gelu(part):
            rows = pl.ds(pl.multiple_of(part * strip, strip), strip)
            x = pre_ref[rows, :]
            root = math.sqrt(2.0 / math.pi)
            square = x * x
            bent = jnp.tanh(root * (x + 0.044715 * (square * x)))
            hid_ref[w, rows, :] = (0.5 * x * (1.0 + bent)).astype(BF16)
            slope = 0.5 * (1.0 + bent) + (0.5 * root) * x * (1.0 - bent * bent) * (1.0 + (3 * 0.044715) * square)
            slope_ref[w, rows, :] = slope.astype(BF16)

        tiles(own // strip, gelu)
        acc_ref[...] += dot_rows(wc_ref[w], hid_ref[w])

    tiles(width, body)


def feed_back(x_ref, ct_ref, ctt_ref, wb_ref, wc_ref, gb_ref, gc_ref, u_ref, gh_ref, hid_ref, slope_ref, width, slab, between, after):
    own = x_ref.shape[1]
    strip = 32
    u_ref[...] = jnp.zeros_like(u_ref)

    def body(at):
        w = slab(at)
        gh_ref[...] = dot(ctt_ref[...], wc_ref[w])
        between(at, w)

        def multiply(part):
            rows = pl.ds(pl.multiple_of(part * strip, strip), strip)
            slope_ref[w, rows, :] = (gh_ref[rows, :] * slope_ref[w, rows, :].astype(F32)).astype(BF16)

        tiles(own // strip, multiply)
        gc_ref[w] = dot(ct_ref[...], hid_ref[w]).astype(BF16)
        u_ref[...] += dot_rows(wb_ref[w], slope_ref[w])
        gb_ref[w] = dot(x_ref[...], slope_ref[w]).astype(BF16)
        after(at, w)

    tiles(width, body)


def attend_back(low_ref, wa_ref, p_ref, q_ref, k_ref, v_ref, trig_ref, gp_ref, width, per, own, hook):
    ext = HALO + own
    group = per * HEAD
    blocks = own // HALO
    scale = HEAD**-0.5

    def body(w):
        hook(w)
        gp_ref[w, 3 * group :, :] = jnp.zeros((group, ext), BF16)
        gp_ref[w, :group, :HALO] = jnp.zeros((group, HALO), BF16)
        turned = jnp.transpose(wa_ref[w, :, 3 * group - HEAD :])
        upstream = dot(turned[HEAD:], low_ref[...]).astype(BF16)
        for i in range(per):
            h = w * per + i
            grad_keys, grad_values = [None] * (blocks + 1), [None] * (blocks + 1)
            for b in range(blocks):
                q = q_ref[h, :, b * HALO : (b + 1) * HALO]
                k = k_ref[h, :, b * HALO : (b + 2) * HALO]
                v = v_ref[h, :, b * HALO : (b + 2) * HALO]
                up = upstream[i * HEAD : (i + 1) * HEAD, b * HALO : (b + 1) * HALO]
                weights = p_ref[h, b]
                wide = weights.astype(F32)
                grad_weights = dot_cols(v, up)
                inner = jnp.sum(wide * grad_weights, 0, keepdims=True)
                grad_scores = (wide * (grad_weights - inner)).astype(BF16)
                gv = dot_rows(up, weights)
                gk = dot_rows(q, grad_scores)
                gq = dot(k, grad_scores) * scale
                cols = slice((b + 1) * HALO, (b + 2) * HALO)
                gp_ref[w, i * HEAD : (i + 1) * HEAD, cols] = rotated(gq, trig_ref[0, :, cols], -trig_ref[1, :, cols]).astype(BF16)
                for part in range(2):
                    piece = slice(part * HALO, (part + 1) * HALO)
                    at = b + part
                    grad_keys[at] = gk[:, piece] if grad_keys[at] is None else grad_keys[at] + gk[:, piece]
                    grad_values[at] = gv[:, piece] if grad_values[at] is None else grad_values[at] + gv[:, piece]
            for at in range(blocks + 1):
                cols = slice(at * HALO, (at + 1) * HALO)
                gp_ref[w, group + i * HEAD : group + (i + 1) * HEAD, cols] = rotated(
                    grad_keys[at], trig_ref[0, :, cols], -trig_ref[1, :, cols]
                ).astype(BF16)
                gp_ref[w, 2 * group + i * HEAD : 2 * group + (i + 1) * HEAD, cols] = grad_values[at].astype(BF16)

    tiles(width, body)


def stream_back(wa_ref, gp_ref, u_ref, start, size, width):
    cols = slice(start, start + size)
    u_ref[:, cols] = dot(wa_ref[0], gp_ref[0, :, cols])

    def body(at):
        u_ref[:, cols] += dot(wa_ref[at + 1], gp_ref[at + 1, :, cols])

    tiles(width - 1, body)


def project_back(x_ref, low_ref, ao_ref, gp_ref, ga_ref, width, per, slab, before, after):
    group = 3 * per * HEAD - HEAD

    def body(at):
        w = slab(at)
        before(at, w)
        ga_ref[w, :, :group] = dot_rows(x_ref[...], gp_ref[w, :group, :]).astype(BF16)
        ga_ref[w, :, group:] = (
            dot_rows(x_ref[...], gp_ref[w, group:, :]) + dot_rows(low_ref[...], ao_ref[w])
        ).astype(BF16)
        after(at, w)

    tiles(width, body)


def block_kernel(width, rows, per, mix_ref, hist_ref, cot_ref, seg_ref, box_ref, own_ref, given_ref,
                 gcol_ref, bout_ref, small_ref, total_ref, left_ref,
                 full, st, ct, boxes_in, gain, x_one, stat_one, starts, trig, q, k, v, ao, prob, mid, stat_two, gmid, low, blk,
                 gacc_one, gacc_two, halo_out, halo_in, macc, small_out, small_in, small_step,
                 last_box, boxes, load_sem, here_sem, send_sem, recv_sem):
    r, z = lax.axis_index("rows"), lax.axis_index("width")
    layers, piece, tokens = hist_ref.shape
    own = tokens // width
    ext = HALO + own
    per_row = seg_ref.shape[1] // own
    core, bits = row_bits(rows)
    hops = len(bits)
    cut = own // 2
    greet(z, r, width, [core] + bits)
    sends = Sends(send_sem, recv_sem)
    inside = own_ref is not None
    gathers = []
    if inside:
        gathers = [Gather(sends, at, own_ref.at[at], full.at[at], z, r, width, rows) for at in range(3)]
        first, second, third = gathers
    others = gathers[1:]
    slab = functools.partial(arrival, z, width=width)

    def each(*actions):
        for method, chosen, distances in actions:
            for away in distances:
                if away == 0:
                    for one in chosen:
                        getattr(one, method)(z)
                    continue
                for w, there in ((z - away, z >= away), (z + away, z + away < width)):
                    @pl.when(there)
                    def _(w=w, method=method, chosen=chosen):
                        for one in chosen:
                            getattr(one, method)(w)
    odd = lax.rem(z, 2) == 1
    mine = pl.ds(pl.multiple_of(z * piece, 16), piece)

    far = 1 - z // 2
    chunks = []
    for at in range(width):
        low_half = flip(far, 1) if at // 2 else far
        chunks.append(2 * low_half + at % 2)
    st_even = st.at[mine, pl.ds(HALO, own)]
    st_odd = st.at[mine, :]
    gain_sends = [sends.make(box_ref, boxes_in.at[z], (r, lax.rem(z + step, width))) for step in range(1, width)]
    base = sends.used
    sends.used += width - 1

    def scoped_stream(pair, mixed):
        def load(at):
            cols = pl.ds(pl.multiple_of(chunks[at // 2] * own + (at % 2) * cut, LANES), cut)
            return pltpu.make_async_copy(hist_ref.at[:, :, cols], pair.at[at % 3], load_sem.at[at % 3])

        def stream_copy(step, target, is_odd):
            start = pl.multiple_of(target * own, LANES)
            if is_odd:
                src, dst = mixed.at[:, pl.ds(pl.multiple_of(start - HALO, LANES), ext)], st_odd
            else:
                src, dst = mixed.at[:, pl.ds(start, own)], st_even
            return pltpu.make_async_remote_copy(
                src_ref=src, dst_ref=dst, send_sem=send_sem.at[base + step - 1], recv_sem=recv_sem.at[base + step - 1],
                device_id=(r, target), device_id_type=MESH,
            )

        for at in range(3):
            load(at).start()
        for copy in gain_sends:
            copy.start()
        boxes_in[z] = box_ref[...]
        when_stream = {}
        if inside:
            for gather in gathers:
                gather.hold()
            first.start(z)
            for gather in gathers:
                gather.spread(z)
            when_stream = {4: [lambda: each(("hop", [first], [1]), ("forward", [first], [1]))]}
        for at in range(2 * width):
            load(at).wait()
            target = chunks[at // 2]
            start = pl.multiple_of(target * own + (at % 2) * cut, LANES)
            mix_stream(mix_ref, pair.at[at % 3], mixed, pl.ds(start, cut), layers)
            if at + 3 < 2 * width:
                load(at + 3).start()
            for action in when_stream.get(at, ()):
                action()

        if inside:
            each(("hop", [first], [2]), ("forward", [first], [2]))
        for at in range(width):
            target, is_odd = chunks[at], at % 2 == 1
            for step in range(1, width):
                @pl.when(lax.rem(z + step, width) == target)
                def _(step=step, target=target, is_odd=is_odd):
                    stream_copy(step, target, is_odd).start()

            @pl.when(target == z)
            def _(is_odd=is_odd, target=target):
                start = pl.multiple_of(target * own, LANES)
                if is_odd:
                    st_odd[...] = mixed[:, pl.ds(pl.multiple_of(start - HALO, LANES), ext)]
                else:
                    st_even[...] = mixed[:, pl.ds(start, own)]
                    st[:, 0:HALO] = jnp.zeros((D, HALO), BF16)

        if inside:
            each(("to_chips", [first], [0]))
        for copy in gain_sends:
            copy.wait()
        spread_gains(boxes_in, gain, width, piece)
        document_starts(seg_ref, starts, trig, z // per_row, lax.rem(z, per_row) * own, own)
        if inside:
            each(
                ("to_chips", [first], [1]), ("to_core", [first], [0]),
                ("to_chips", others, [0]), ("hop", [first], [3]), ("start", others, [0]), ("to_chips", [first], [2]),
                ("to_core", [first], [1]), ("to_core", others, [0]),
            )
        for step in range(1, width):
            for is_odd in (False, True):
                @pl.when(lax.rem(z, 2) == int(is_odd))
                def _(step=step, is_odd=is_odd):
                    stream_copy(step, z, is_odd).wait_recv()

                @pl.when(lax.rem(z + step, 2) == int(is_odd))
                def _(step=step, is_odd=is_odd):
                    stream_copy(step, lax.rem(z + step, width), is_odd).wait_send()

        cot_here.start()

    cot_sends = []
    for step in range(1, width):
        target = lax.rem(z + step, width)
        cols = pl.ds(pl.multiple_of(target * own, LANES), own)
        cot_sends.append(sends.make(cot_ref.at[:, cols], ct.at[mine, :], (r, target)))
    cot_here = pltpu.make_async_copy(
        cot_ref.at[:, pl.ds(pl.multiple_of(z * own, LANES), own)], ct.at[mine, :], here_sem
    )
    if not inside:
        given = pltpu.make_async_copy(given_ref, full, load_sem.at[3])
        given.start()
    pl.run_scoped(scoped_stream, pltpu.VMEM((3, layers, piece, cut), BF16), pltpu.VMEM((piece, tokens), BF16))

    norm_forward(st, 0, gain, 0, x_one, stat_one, ext)
    if not inside:
        given.wait()

    def send_cotangent():
        for copy in cot_sends:
            copy.start()

    def scoped_attend(bias):
        attend_bias(starts, bias)
        if inside:
            serve = at_steps({
                0: [lambda: each(("to_core", [first], [2]))],
                1: [lambda: each(("to_chips", [first], [3]), ("hop", others, [1]), ("forward", others, [1]))],
                2: [lambda: each(("to_core", [first], [3]))],
                3: [lambda: each(("to_chips", others, [1]), ("hop", others, [2]), ("forward", others, [2]))],
            })

        def body(at):
            w = slab(at)
            if inside:
                serve(at)
            if inside:
                first.take(w)
            project(x_one, full.at[0], trig, q, k, v, w, per)
            attend(q, k, v, bias, prob, ao, w, per)

        tiles(width, body)

    pl.run_scoped(scoped_attend, pltpu.VMEM((own // HALO, 2 * HALO, HALO), F32))
    out_project(st, full.at[0], ao, mid, width, per)
    if inside:
        each(("to_core", others, [1]), ("to_chips", others, [2]), ("hop", others, [3]))
    send_cotangent()
    gmid[...] = mid[...]
    if inside:
        tiles(width, first.clear)

    scatters = []
    if inside:
        scatters = [
            Scatter(sends, at, at > 0, full.at[at], [box.at[at] for box in boxes], last_box.at[at], total_ref.at[at], z, r, width, rows)
            for at in range(3)
        ]
    attending, pair_back = scatters[:1], scatters[1:]

    def back(method, chosen, at):
        for one in chosen:
            getattr(one, method)(turned(at))

    def later(method, chosen, at):
        return lambda: back(method, chosen, at)

    def turned(at):
        return slab(width - 1 - at)


    late = at_steps({})
    if inside:
        late = at_steps({
            0: [lambda: each(("to_core", others, [2]))],
            1: [lambda: each(("to_chips", others, [3]))],
            2: [lambda: each(("to_core", others, [3]))],
        })

    def feed_before(at, w):
        late(at)
        if inside:
            second.take(w)
            third.take(w)

    def feed_between(at, w):
        if inside:
            second.clear(w)
            third.clear(w)

        feed_service(at)

    feed_service = at_steps({
        1: [later("take_core", pair_back, 0)],
        3: [later("take_chips", pair_back, 0), later("take_core", pair_back, 1)],
    })

    def feed_after(at, w):
        for scatter in pair_back:
            scatter.begin(w)

    blk_sends, gs_sends = [], []
    here = pl.ds(pl.multiple_of(z * own, LANES), own)
    for step in range(1, width):
        target = lax.rem(z + step, width)
        part = pl.ds(pl.multiple_of(target * piece, 16), piece)
        blk_sends.append(sends.make(blk.at[part, :], bout_ref.at[:, here], (r, target)))

    blk_here = pltpu.make_async_copy(blk.at[mine, :], bout_ref.at[:, here], load_sem.at[3])

    def scoped_feed(x_two, turn, pre, hid, slope, u_two):
        norm_forward(mid, 0, gain, 1, x_two, stat_two, own)
        turn[...] = jnp.transpose(x_two[...])
        feed_forward(turn, full.at[1], full.at[2], gmid, pre, hid, slope, width, slab, feed_before)
        blk[...] = gmid[...].astype(BF16)
        for copy in blk_sends:
            copy.start()
        blk_here.start()
        for copy in cot_sends:
            copy.wait()
        cot_here.wait()
        turn[...] = jnp.transpose(ct[...])
        feed_back(
            x_two, ct, turn, full.at[1], full.at[2], full.at[1], full.at[2], u_two, pre, hid, slope, width, turned, feed_between, feed_after
        )

        def write(cols, value):
            gmid[:, cols] = value
            low[:, cols] = value.astype(BF16)

        gacc_two[...] = jnp.zeros_like(gacc_two)
        norm_back(u_two, 0, mid, 0, stat_two, 0, gain, 1, lambda cols: ct[:, cols].astype(F32), write, gacc_two, 0, own)

    pl.run_scoped(
        scoped_feed, pltpu.VMEM((D, own), BF16), pltpu.VMEM((own, D), BF16), pltpu.VMEM((own, D), F32),
        pltpu.VMEM((width, own, D), BF16), pltpu.VMEM((width, own, D), BF16), pltpu.VMEM((D, own), F32),
    )

    when_attend = at_steps({
        1: [later("take_last", pair_back, 0)],
        2: [later("take_chips", pair_back, 1), later("take_core", pair_back, 2)],
        3: [later("relay", pair_back, 0)],
    })
    when_project = at_steps({3: [later("take_core", attending, 0), later("take_core", attending, 1)]})
    when_mix = {
        0: [later("take_chips", attending, 0), later("take_chips", attending, 1)],
    }
    halo = sends.make(halo_out, halo_in, (r, flip(z, 1)))
    half = own // 2
    for part in range(2):
        columns = pl.ds(pl.multiple_of(z * own + part * half, LANES), half)
        for step in range(1, width):
            target = lax.rem(z + step, width)
            features = pl.ds(pl.multiple_of(target * piece, 16), piece)
            gs_sends.append(
                sends.make(blk.at[features, pl.ds(part * half, half)], gcol_ref.at[:, columns], (r, target))
            )

    def scoped_back(gp, u):
        def send_stream(part):
            def write(cols, value):
                blk[:, cols] = value.astype(BF16)

            norm_back(
                u, HALO, st, HALO, stat_one, HALO, gain, 0, lambda cols: gmid[:, cols], write, gacc_one, part * half, half
            )
            for copy in gs_sends[part * (width - 1) : (part + 1) * (width - 1)]:
                copy.start()
            columns = pl.ds(pl.multiple_of(z * own + part * half, LANES), half)
            gcol_ref[:, columns] = blk[mine, pl.ds(part * half, half)]

        attend_back(low, full.at[0], prob, q, k, v, trig, gp, width, per, own, when_attend)
        stream_back(full.at[0], gp, u, 0, HALO, width)

        @pl.when(odd)
        def _():
            halo_out[...] = u[:, 0:HALO].astype(BF16)
            halo.start()

        back("take_chips", pair_back, 2)
        back("take_core", pair_back, 3)
        stream_back(full.at[0], gp, u, HALO, own, width)
        gacc_one[...] = jnp.zeros_like(gacc_one)
        for copy in blk_sends:
            copy.wait_send()
        blk_here.wait()
        send_stream(0)
        back("take_last", pair_back, 1)

        def after_project(at, w):
            for scatter in attending:
                scatter.begin(w)

        project_back(x_one, low, ao, gp, full.at[0], width, per, turned, lambda at, w: when_project(at), after_project)
        back("relay", pair_back, 1)
        back("take_last", pair_back, 2)
        back("take_chips", pair_back, 3)
        back("take_core", attending, 2)
        back("take_core", attending, 3)

        @pl.when(jnp.logical_not(odd))
        def _():
            halo.wait_recv()
            u[:, own : own + HALO] += halo_in[...].astype(F32)

        send_stream(1)
        back("relay", pair_back, 2)
        back("take_last", pair_back, 3)

    pl.run_scoped(scoped_back, pltpu.VMEM((width, 4 * per * HEAD, ext), BF16), pltpu.VMEM((D, ext), F32))

    macc[...] = jnp.zeros_like(macc)
    strip = 16

    def scoped_mix(pair):
        def place(at):
            chunk = lax.rem(z + width - at % width, width)
            return pl.ds(pl.multiple_of(chunk * own + (at // width) * half, LANES), half)

        def load(at):
            return pltpu.make_async_copy(hist_ref.at[:, :, place(at)], pair.at[at % 3], load_sem.at[at % 3])

        for at in range(3):
            load(at).start()
        for at in range(2 * width):
            if at % width:
                gs_sends[at // width * (width - 1) + at % width - 1].wait_recv()
            load(at).wait()
            cols = place(at)

            def body(row, at=at, cols=cols):
                part = pl.ds(pl.multiple_of(row * strip, strip), strip)
                g = gcol_ref[part, cols].astype(F32)
                for j in range(layers):
                    crossed = pair[at % 3, j, part, :].astype(F32) * g
                    folded = crossed[:8] + crossed[8:]
                    total = folded[:, :LANES]
                    for lane in range(1, cut // LANES):
                        total = total + folded[:, lane * LANES : (lane + 1) * LANES]
                    macc[j] += total

            tiles(piece // strip, body)
            if at + 3 < 2 * width:
                load(at + 3).start()
            for action in when_mix.get(at, ()):
                action()

    pl.run_scoped(scoped_mix, pltpu.VMEM((3, layers, piece, cut), BF16))

    small_out[...] = jnp.zeros_like(small_out)
    gain_one = jnp.sum(jnp.transpose(gacc_one[...]), 0, keepdims=True)
    gain_two = jnp.sum(jnp.transpose(gacc_two[...]), 0, keepdims=True)
    depth = jnp.sum(jnp.transpose(jnp.sum(macc[...], 1)), 0, keepdims=True)
    for w in range(width):
        small_out[w, 0:1, 0:piece] = gain_one[:, w * piece : (w + 1) * piece]
        small_out[w, 1:2, 0:piece] = gain_two[:, w * piece : (w + 1) * piece]
        small_out[w, 2:3, 0 : depth.shape[1]] = depth
    small_sends = [
        sends.make(small_out.at[lax.rem(z + step, width)], small_in.at[step - 1], (r, lax.rem(z + step, width)))
        for step in range(1, width)
    ]
    for copy in small_sends:
        copy.start()
    back("take_last", attending, 0)
    back("take_last", attending, 1)
    current = small_out[z]
    for step in range(1, width):
        small_sends[step - 1].wait_recv()
        current = current + small_in[step - 1]
    for at, bit in enumerate([core] + bits):
        small_step[at, 0] = current
        copy = sends.make(small_step.at[at, 0], small_step.at[at, 1], (flip(r, bit), z))
        copy.start()
        if at == 0:
            back("take_chips", attending, 2)
            back("take_chips", attending, 3)
        copy.wait_recv()
        current = current + small_step[at, 1]
        small_sends.append(copy)
    small_ref[...] = current
    back("take_last", attending, 2)
    back("take_last", attending, 3)
    for scatter in scatters:
        scatter.finish()
    for copy in blk_sends:
        copy.wait_recv()
    for copy in gs_sends + small_sends:
        copy.wait_send()

    @pl.when(odd)
    def _():
        halo.wait_send()

    for scatter in scatters:
        scatter.end()
    if not inside:
        leave = pltpu.make_async_copy(full, left_ref, load_sem.at[3])
        leave.start()
        leave.wait()


def vmem(count):
    return [pl.BlockSpec(memory_space=pltpu.VMEM)] * count


def shape(*sizes, dtype=F32):
    return jax.ShapeDtypeStruct(sizes, dtype)


def block(width, rows, mix, history, cotangent, segments, box, own_three):
    layers, piece, tokens = history.shape
    shard = own_three.shape[1]
    own = tokens // width
    ext = HALO + own
    heads = D // HEAD
    per = heads // width
    group = per * HEAD
    blocks = own // HALO
    digits = rows.bit_length() - 1
    inside = shard % 16 == 0
    any_space = pl.BlockSpec(memory_space=pl.ANY)
    ins = [mix, history, cotangent, segments, box]
    specs = [pl.BlockSpec(memory_space=pltpu.SMEM), any_space, any_space] + vmem(2)
    outs = [shape(piece, tokens, dtype=BF16), shape(piece, tokens, dtype=BF16), shape(8, 2 * LANES)]
    out_specs = vmem(1) + [any_space] + vmem(1)
    box_shapes = []
    if inside:
        ins, specs = ins + [own_three], specs + vmem(1)
        outs, out_specs = outs + [shape(3, shard, D)], out_specs + vmem(1)
        box_shapes = Scatter.box_shapes(width, rows, shard)
    else:
        gathered = lax.all_gather(lax.all_gather(own_three, "rows", axis=1, tiled=True), "width", axis=1)
        ins, specs = ins + [gathered], specs + [any_space]
        outs, out_specs = outs + [shape(3, width, D, D, dtype=BF16)], out_specs + [any_space]
    low = lambda *sizes: pltpu.VMEM(sizes, BF16)
    full = lambda *sizes: pltpu.VMEM(sizes, F32)
    scratch = [
        low(3, width, D, D), low(D, ext), low(D, own), full(width, 8, 2 * LANES), full(2, D, LANES), low(D, ext), full(8, ext),
        full(8, HALO + segments.shape[1]), full(2, HEAD // 2, ext), low(heads, HEAD, own), low(heads, HEAD, ext), low(heads, HEAD, ext),
        low(width, HEAD + group, own), low(heads, blocks, 2 * HALO, HALO), full(D, own), full(8, own),
        full(D, own), low(D, own), low(D, own), full(D, LANES), full(D, LANES), low(D, HALO), low(D, HALO), full(layers, 8, LANES),
        full(width, 8, 2 * LANES), full(width - 1, 8, 2 * LANES), full(digits, 2, 8, 2 * LANES),
    ]
    common = len(scratch)
    if inside:
        scratch += [low(3, width + 1, shard, D)] + [low(3, *one) for one in box_shapes]
    count = 6 * (width - 1) + 1 + (width - 1) + digits
    count += 3 * Gather.copies(width, rows) + 3 * Scatter.copies(width, rows)
    scratch += [
        pltpu.SemaphoreType.DMA((4,)), pltpu.SemaphoreType.DMA, pltpu.SemaphoreType.DMA((count,)), pltpu.SemaphoreType.DMA((count,)),
    ]

    def kernel(*refs):
        given, found, rest = refs[:6], refs[6:10], refs[10:]
        weights = (given[5], None) if inside else (None, given[5])
        results = (found[3], None) if inside else (None, found[3])
        kept, rest = rest[:common], rest[common:]
        last_box, boxes = None, ()
        if inside:
            last_box, boxes, rest = rest[0], rest[1 : 1 + len(box_shapes)], rest[1 + len(box_shapes) :]
        block_kernel(width, rows, per, *given[:5], *weights, *found[:3], *results, *kept, last_box, boxes, *rest)

    found = pl.pallas_call(
        kernel,
        out_shape=outs,
        in_specs=specs,
        out_specs=out_specs,
        scratch_shapes=scratch,
        compiler_params=pltpu.CompilerParams(collective_id=0, has_side_effects=True, vmem_limit_bytes=64 * MIB - 128 * 1024),
    )(*ins)
    if inside:
        return found
    total = lax.psum_scatter(found[3], "width", scatter_dimension=1)
    return (*found[:3], lax.psum_scatter(total, "rows", scatter_dimension=1, tiled=True).astype(F32))


def prepare_kernel(attend_ref, output_ref, expand_ref, reduce_ref, gains_ref, own_ref, box_ref):
    parts = [attend_ref[k] for k in range(3)] + [jnp.transpose(output_ref[...])]
    own_ref[0] = jnp.concatenate(parts, 1).astype(BF16)
    own_ref[1] = expand_ref[...].astype(BF16)
    own_ref[2] = reduce_ref[...].astype(BF16)
    box_ref[...] = jnp.zeros_like(box_ref)
    box_ref[0:2, 0 : gains_ref.shape[1]] = gains_ref[...]


def prepare(w_attend, w_output, w_expand, w_reduce, gains):
    shard, piece = w_expand.shape[0], gains.shape[1]
    if shard % 16 == 0:
        return pl.pallas_call(
            prepare_kernel,
            out_shape=[shape(3, shard, D, dtype=BF16), shape(8, 2 * LANES)],
            in_specs=vmem(5),
            out_specs=vmem(2),
            compiler_params=pltpu.CompilerParams(vmem_limit_bytes=60 * MIB),
        )(w_attend, w_output, w_expand, jnp.transpose(w_reduce), gains)
    first = jnp.concatenate([w_attend[0], w_attend[1], w_attend[2], jnp.transpose(w_output)], 1)
    own_three = jnp.stack([first, w_expand, jnp.transpose(w_reduce)]).astype(BF16)
    return own_three, jnp.pad(gains, ((0, 8 - gains.shape[0]), (0, 2 * LANES - piece)))


def finish_kernel(per_step, mix_ref, grad_ref, total_ref, out_ref, *refs):
    weights, (hist_ref, block_ref, *news) = refs[:12], refs[12:]
    at = pl.program_id(0)
    piece = grad_ref.shape[0]
    strip = 16

    def body(row):
        rows = pl.ds(pl.multiple_of(row * strip, strip), strip)
        g = grad_ref[rows, :].astype(F32)
        for j in range(per_step):
            hist_ref[j, rows, :] = (mix_ref[at * per_step + j] * g).astype(BF16)

    tiles(piece // strip, body)

    def update(which, gradient, rate):
        found = optimize(weights[3 * which][...], gradient, weights[3 * which + 1][...], weights[3 * which + 2][...], rate, DECAY)
        for ref, value in zip(news[3 * which : 3 * which + 3], found):
            ref[...] = value

    @pl.when(at == 0)
    def _():
        for k in range(3):
            gradient = total_ref[0, :, k * piece : (k + 1) * piece]
            found = optimize(weights[0][k], gradient, weights[1][k], weights[2][k], RATE_MATRIX, DECAY)
            for ref, value in zip(news[:3], found):
                ref[k] = value

    @pl.when(at == 1)
    def _():
        update(1, jnp.transpose(total_ref[0, :, 3 * piece :]), RATE_OUTPUT)

    @pl.when(at == 2)
    def _():
        update(2, total_ref[1], RATE_MATRIX)

    @pl.when(at == 3)
    def _():
        update(3, total_ref[2], RATE_MATRIX)
        block_ref[...] = out_ref[...]


def finish(mix, grad_stream, total, block_output, layers, weights):
    shard = total.shape[1]
    piece, tokens = grad_stream.shape
    if shard % 16 == 0 and layers % 5 == 0:
        weights = [jnp.transpose(one) if at // 3 == 3 else one for at, one in enumerate(weights)]
        held = [shape(*one.shape) for one in weights]
        per_step = layers // 5
        history_grad, block_output, *news = pl.pallas_call(
            functools.partial(finish_kernel, per_step),
            grid=(5,),
            out_shape=[shape(layers, piece, tokens, dtype=BF16), shape(piece, tokens, dtype=BF16)] + held,
            in_specs=[pl.BlockSpec(memory_space=pltpu.SMEM)] + vmem(3 + len(weights)),
            out_specs=[pl.BlockSpec((per_step, piece, tokens), lambda at: (at, 0, 0))] + vmem(1 + len(weights)),
            compiler_params=pltpu.CompilerParams(vmem_limit_bytes=60 * MIB),
        )(mix, grad_stream, total, block_output, *weights)
        return (history_grad, block_output, *[jnp.transpose(one) if at // 3 == 3 else one for at, one in enumerate(news)])
    history_grad = (mix[:, None, None] * grad_stream[None].astype(F32)).astype(BF16)
    first = total[0]
    gradients = (
        jnp.stack([first[:, k * piece : (k + 1) * piece] for k in range(3)]),
        jnp.transpose(first[:, 3 * piece :]), total[1], jnp.transpose(total[2]),
    )
    news = []
    for at, rate in enumerate((RATE_MATRIX, RATE_OUTPUT, RATE_MATRIX, RATE_MATRIX)):
        w, m, v = weights[3 * at : 3 * at + 3]
        news += optimize(w, gradients[at], m, v, rate, DECAY)
    return (history_grad, block_output, *news)


def on_device(
    width, rows, history, cotangent, segments, w_attend, m_attend, v_attend, w_output, m_output, v_output,
    w_expand, m_expand, v_expand, w_reduce, m_reduce, v_reduce, gains, m_gains, v_gains, mix, m_mix, v_mix,
):
    layers, piece, _ = history.shape
    own_three, box = prepare(w_attend, w_output, w_expand, w_reduce, gains)
    grad_stream, block_output, small, total = block(width, rows, mix, history, cotangent, segments, box, own_three)
    weights = (
        w_attend, m_attend, v_attend, w_output, m_output, v_output, w_expand, m_expand, v_expand, w_reduce, m_reduce, v_reduce,
    )
    history_grad, block_output, *news = finish(mix, grad_stream, total, block_output, layers, weights)
    new_gains = optimize(gains, small[0:2, :piece], m_gains, v_gains, RATE_GAIN, 0.0)
    new_mix = optimize(mix, small[2, :layers], m_mix, v_mix, RATE_MIX, 0.0)
    return (block_output, history_grad, *news, *new_gains, *new_mix)


def solution(mesh):
    square, tall, wide = P(None, "rows", "width"), P("width", "rows"), P("rows", "width")
    weights = (square,) * 3 + (tall,) * 3 + (wide,) * 3 + (tall,) * 3 + (P(None, "width"),) * 3 + (P(),) * 3
    return jax.shard_map(
        functools.partial(on_device, mesh.shape["width"], mesh.shape["rows"]),
        mesh=mesh,
        in_specs=(P(None, "width", "rows"), P("width", "rows"), P("rows", None)) + weights,
        out_specs=(P("width", "rows"), P(None, "width", "rows")) + weights,
        check_vma=False,
    )
```

```python
import functools
import math
from types import SimpleNamespace

import jax
import jax.numpy as jnp
from jax import lax
from jax.experimental import pallas as pl
from jax.experimental.pallas import tpu as pltpu
from jax.sharding import PartitionSpec as P

D = 768
HEAD = 64
STEP = 10
HALO = 256
LANES = 128


EPS_NORM = 1e-05
EPS_ADAM = 1e-08
BETA_ONE = 0.9
BETA_TWO = 0.95
RATE_MATRIX = 0.02
RATE_OUTPUT = 0.12
RATE_GAIN = 0.4
RATE_MIX = 0.05
DECAY = 0.1
MASKED = -1e30

MESH = pl.DeviceIdType.MESH
F32 = jnp.float32
BF16 = jnp.bfloat16
MIB = 1 << 20


def optimize(weight, gradient, first_moment, second_moment, rate, decay):
    first_moment = BETA_ONE * first_moment + (1.0 - BETA_ONE) * gradient
    second_moment = BETA_TWO * second_moment + (1.0 - BETA_TWO) * gradient * gradient
    first_fixed = first_moment / (1.0 - BETA_ONE**STEP)
    second_fixed = second_moment / (1.0 - BETA_TWO**STEP)
    weight = weight - rate * (first_fixed / (jnp.sqrt(second_fixed) + EPS_ADAM) + decay * weight)
    return (weight, first_moment, second_moment)


def flip(index, bit):
    return index + bit - 2 * bit * lax.rem(lax.div(index, jnp.int32(bit)), 2)


def flips(index, bits):
    for bit in bits:
        index = flip(index, bit)
    return index


def subsets(bits):
    found = [()]
    for bit in bits:
        found = found + [one + (bit,) for one in found]
    return found


def row_bits(rows):
    digits = [1 << place for place in range(rows.bit_length() - 1)]
    return digits[0], digits[1:]


def tiles(count, body):
    def step(at, carry):
        body(at)
        return carry

    lax.fori_loop(0, count, step, 0)


def lane_tile(at, size=LANES, base=0):
    return pl.ds(pl.multiple_of(base + at * size, LANES), size)


def dot(a, b):
    return jnp.dot(a, b, preferred_element_type=F32)


def dot_rows(a, b):
    return lax.dot_general(a, b, (((1,), (1,)), ((), ())), preferred_element_type=F32)


def dot_cols(a, b):
    return lax.dot_general(a, b, (((0,), (0,)), ((), ())), preferred_element_type=F32)


def plane_peers(r, rows):
    core, bits = row_bits(rows)
    chosen = [one for one in subsets([core] + bits) if one]
    if rows > 8:
        chosen = [(bit,) for bit in [core] + bits]
    return [flips(r, one) for one in chosen]


def greet(z, r, width, rows):
    bar = pltpu.get_barrier_semaphore()
    places = [(r, lax.rem(z + k, width)) for k in range(1, width)] + [(peer, z) for peer in plane_peers(r, rows)]
    for place in places:
        pl.semaphore_signal(bar, inc=1, device_id=place, device_id_type=MESH)
    pl.semaphore_wait(bar, len(places))


def at_steps(table):
    def hook(step):
        for at, actions in table.items():
            @pl.when(step == at)
            def _(actions=actions):
                for action in actions:
                    action()

    return hook


class Sends:
    def __init__(self, send, recv):
        self.send, self.recv, self.used = send, recv, 0

    def reserve(self, count):
        at = self.used
        self.used += count
        return at

    def copy(self, at, src, dst, place):
        return pltpu.make_async_remote_copy(
            src_ref=src, dst_ref=dst, send_sem=self.send.at[at], recv_sem=self.recv.at[at],
            device_id=place, device_id_type=MESH,
        )

    def make(self, src, dst, place):
        return self.copy(self.reserve(1), src, dst, place)


def arrival(z, at, width):
    found = 0
    for own in range(width):
        order = sorted(range(width), key=lambda w, own=own: (abs(w - own), w))
        for place, w in enumerate(order):
            if w:
                found = found + w * jnp.where((z == own) & (at == place), 1, 0)
    return found


class Plane:
    def __init__(self, chunk, z, r, width, rows, shard):
        self.core, self.bits = row_bits(rows)
        self.chunk, self.z, self.r, self.width, self.shard = chunk, z, r, width, shard
        self.hops = len(self.bits)
        self.per_slab = self.hops + 1

    def rows(self, index):
        return pl.ds(pl.multiple_of(index * self.shard, 16), self.shard)

    def bit(self, w, at):
        one, other = self.bits[at], self.bits[::-1][at]
        return one + (other - one) * lax.rem(w + self.chunk, 2)

    def place(self, index, w, code):
        for at in range(self.hops):
            if code >> at & 1:
                index = flip(index, self.bit(w, at))
        return index


class Gather(Plane):
    def __init__(self, sends, chunk, own, full, z, r, width, rows):
        super().__init__(chunk, z, r, width, rows, own.shape[0])
        self.sends, self.own, self.full = sends, own, full
        self.line_base = sends.reserve(2 * (width - 1))
        self.slab_base = sends.reserve(width * self.per_slab)

    @staticmethod
    def copies(width, rows):
        return 2 * (width - 1) + width * (rows.bit_length() - 1)

    def line(self, w, up, distance, target):
        part = self.full.at[w, self.rows(self.r)]
        at = self.line_base + (1 - up) * (self.width - 1) + distance
        return self.sends.copy(at, part, part, (self.r, target))

    def hold(self):
        self.full[self.z, self.rows(self.r), :] = self.own[...]

    def start(self, w):
        for up, there, target in ((1, self.z + 1 < self.width, self.z + 1), (0, self.z > 0, self.z - 1)):
            @pl.when(there)
            def _(up=up, target=target):
                self.line(self.z, up, 0, target).start()

    def hop(self, w):
        up = jnp.where(w < self.z, 1, 0)
        distance = (self.z - w) * (2 * up - 1)
        self.line(w, up, distance - 1, self.z).wait_recv()
        self.spread(w)

    def onward(self, w):
        up = jnp.where(w < self.z, 1, 0)
        distance = (self.z - w) * (2 * up - 1)
        target = self.z + 2 * up - 1
        return (target >= 0) & (target < self.width), self.line(w, up, distance, target)

    def forward(self, w):
        there, copy = self.onward(w)

        @pl.when(there)
        def _():
            copy.start()

    def step(self, w, at):
        peer = flip(self.r, self.bit(w, at) if at < self.hops else self.core)
        found = []
        for code in range(2**at):
            part = self.full.at[w, self.rows(self.place(self.r, w, code))]
            found.append(self.sends.copy(self.slab_base + w * self.per_slab + at, part, part, (peer, self.z)))
        return found

    def whole(self, w, at):
        part = self.full.at[w, pl.ds(0, 2**at * self.shard)]
        return self.sends.copy(self.slab_base + w * self.per_slab + at, part, part, (flip(self.r, self.core), self.z))

    def spread(self, w):
        for copy in self.step(w, 0):
            copy.start()

    def pass_on(self, w, at):
        self.whole(w, at - 1).wait_recv()
        for copy in self.step(w, at):
            copy.start()

    def to_chips(self, w):
        for at in range(1, self.hops):
            self.pass_on(w, at)

    def to_core(self, w):
        if self.hops:
            self.pass_on(w, self.hops)

    def take(self, w):
        self.whole(w, self.hops).wait_recv()

    def clear(self, w):
        for at in range(self.hops + 1):
            self.whole(w, at).wait_send()

        @pl.when(w == self.z)
        def _():
            for up, there, target in ((1, self.z + 1 < self.width, self.z + 1), (0, self.z > 0, self.z - 1)):
                @pl.when(there)
                def _(up=up, target=target):
                    self.line(self.z, up, 0, target).wait_send()

        there, onward = self.onward(w)

        @pl.when((w != self.z) & there)
        def _():
            onward.wait_send()


class Scatter(Plane):
    def __init__(self, sends, chunk, along, grads, boxes, last_box, total, z, r, width, rows):
        super().__init__(chunk, z, r, width, rows, total.shape[0])
        self.sends, self.grads, self.boxes, self.last_box, self.total = sends, grads, boxes, last_box, total
        self.along = along
        self.other = flip(r, self.core)
        self.slab_base = sends.reserve(width * self.per_slab)
        self.width_base = sends.reserve(width + 1)

    @staticmethod
    def copies(width, rows):
        return width + 1 + width * (rows.bit_length() - 1)

    @staticmethod
    def box_shapes(width, rows, shard):
        hops = rows.bit_length() - 2
        return [(2 ** (hops - at), width, shard, D) for at in range(hops + 1)]

    def step(self, w, at):
        base = self.slab_base + w * self.per_slab + at
        if at == 0:
            return [
                self.sends.copy(base, self.grads.at[w, self.rows(self.place(self.other, w, code))], self.boxes[0].at[code, w], (self.other, self.z))
                for code in range(2**self.hops)
            ]
        peer = flip(self.r, self.bit(w, at - 1))
        return [
            self.sends.copy(base, self.boxes[at - 1].at[2 * code + 1, w], self.boxes[at].at[code, w], (peer, self.z))
            for code in range(2 ** (self.hops - at))
        ]

    def whole(self, w, at):
        part = self.boxes[at].at[:, w]
        return self.sends.copy(self.slab_base + w * self.per_slab + at, part, part, (self.other, self.z))

    def over_width(self, w):
        if self.along:
            target = self.z + jnp.where(w > self.z, 1, -1)
            slot = jnp.where((target == w) & (w < self.z), self.width, w)
        else:
            target = w
            slot = lax.rem(w - self.z + self.width, self.width) - 1
        return self.sends.copy(self.width_base + slot, self.boxes[self.hops].at[0, w], self.last_box.at[slot], (self.r, target))

    def came(self, slot):
        return self.sends.copy(self.width_base + slot, self.last_box.at[slot], self.last_box.at[slot], (self.r, flip(self.z, 1)))

    def awaited(self, w):
        return jnp.where(w > self.z, self.z, self.width - 1 - self.z) > 0

    def relay(self, w):
        if self.along:
            @pl.when((w != self.z) & self.awaited(w))
            def _():
                self.came(w).wait_recv()
                box = self.boxes[self.hops].at[0, w]
                box[...] = (box[...].astype(F32) + self.last_box[w].astype(F32)).astype(BF16)
                self.over_width(w).start()

    def begin(self, w):
        for copy in self.step(w, 0):
            copy.start()

    def take(self, w, at):
        self.whole(w, at).wait_recv()
        for code in range(2 ** (self.hops - at)):
            box = self.boxes[at].at[code, w]
            if at == 0:
                kept = self.grads.at[w, self.rows(self.place(self.r, w, code))]
            else:
                kept = self.boxes[at - 1].at[2 * code, w]
            box[...] = (box[...].astype(F32) + kept[...].astype(F32)).astype(BF16)
        if at < self.hops:
            for copy in self.step(w, at + 1):
                copy.start()
        else:
            @pl.when((w != self.z) & jnp.logical_not(self.awaited(w)) if self.along else w != self.z)
            def _():
                self.over_width(w).start()

    def take_core(self, w):
        self.take(w, 0)

    def take_chips(self, w):
        for at in range(1, self.hops):
            self.take(w, at)

    def take_last(self, w):
        if self.hops:
            self.take(w, self.hops)

    def finish(self):
        self.total[...] = self.boxes[self.hops][0, self.z].astype(F32)
        if self.along:
            arrivals = ((self.z, self.z > 0), (self.width, self.z < self.width - 1))
        else:
            arrivals = [(slot, self.z >= 0) for slot in range(self.width - 1)]
        for slot, there in arrivals:
            @pl.when(there)
            def _(slot=slot):
                self.came(slot).wait_recv()
                self.total[...] += self.last_box[slot].astype(F32)

    def end(self):
        def one(w):
            for at in range(self.hops + 1):
                self.whole(w, at).wait_send()

            @pl.when(w != self.z)
            def _():
                self.over_width(w).wait_send()

        tiles(self.width, one)


def mix_stream(mix_ref, pair_ref, out_ref, base, layers):
    features, size = pair_ref.shape[1], pair_ref.shape[2]
    strip = 16

    def body(at):
        rows = pl.ds(pl.multiple_of(at * strip, strip), strip)
        total = mix_ref[0] * pair_ref[0, rows, :].astype(F32)
        for j in range(1, layers):
            total = total + mix_ref[j] * pair_ref[j, rows, :].astype(F32)
        out_ref[rows, base] = total.astype(BF16)

    tiles(features // strip, body)


def spread_gains(box_ref, gain_ref, width, piece):
    for w in range(width):
        for i in range(2):
            row = box_ref[w, pl.ds(i, 1), :]
            full = jnp.transpose(jnp.broadcast_to(row, (LANES, row.shape[1])))
            gain_ref[i, pl.ds(w * piece, piece), :] = full[:piece]


def norm_forward(x_ref, x_base, gain_ref, i, out_ref, stat_ref, count):
    def body(at):
        cols = lane_tile(at)
        x = x_ref[:, lane_tile(at, base=x_base)].astype(F32)
        centre = jnp.sum(x, 0, keepdims=True) / D
        spread = jnp.sum(x * x, 0, keepdims=True) / D - centre * centre
        scaling = lax.rsqrt(spread + EPS_NORM)
        out_ref[:, cols] = (gain_ref[i] * ((x - centre) * scaling)).astype(BF16)
        stat_ref[0:1, cols] = centre
        stat_ref[1:2, cols] = scaling

    tiles(count // LANES, body)


def norm_back(u_ref, u_base, x_ref, x_base, stat_ref, stat_base, gain_ref, i, residual, write, gain_acc, start, count):
    def body(step):
        at = step + start // LANES
        u = u_ref[:, lane_tile(at, base=u_base)].astype(F32)
        x = x_ref[:, lane_tile(at, base=x_base)].astype(F32)
        cols = lane_tile(at, base=stat_base)
        scaling = stat_ref[1:2, cols]
        centred = (x - stat_ref[0:1, cols]) * scaling
        gain_acc[...] += u * centred
        s = u * gain_ref[i]
        mean_s = jnp.sum(s, 0, keepdims=True) / D
        mean_c = jnp.sum(s * centred, 0, keepdims=True) / D
        write(lane_tile(at), residual(lane_tile(at)) + scaling * (s - mean_s - centred * mean_c))

    tiles(count // LANES, body)


def document_starts(seg_ref, start_ref, trig_ref, row, own_at, own):
    seg = seg_ref[pl.ds(row, 1), :]
    length = seg.shape[1]
    place = lax.broadcasted_iota(jnp.int32, (8, length), 1)
    seg = jnp.broadcast_to(seg, (8, length))
    before = pltpu.roll(seg, 1, 1)
    start = jnp.where((place > 0) & (seg == before), 0, place)
    step = 1
    while step < length:
        moved = pltpu.roll(start, step, 1)
        start = jnp.maximum(start, jnp.where(place >= step, moved, 0))
        step *= 2
    position = (place - start).astype(F32)
    scratch = start_ref.at[0:8]
    ext = HALO + own
    scratch[:, pl.ds(0, HALO)] = jnp.zeros((8, HALO), F32)
    scratch[:, pl.ds(HALO, length)] = position
    window = scratch[:, pl.ds(pl.multiple_of(own_at, LANES), ext)][0:1]
    half = HEAD // 2
    freq = jnp.exp(
        lax.broadcasted_iota(jnp.int32, (half, ext), 0).astype(F32) * (-2.0 * math.log(10000.0) / HEAD)
    )
    angle = freq * window
    trig_ref[0] = jnp.cos(angle)
    trig_ref[1] = jnp.sin(angle)
    scratch[:, pl.ds(HALO, length)] = start.astype(F32)
    kept = scratch[:, pl.ds(pl.multiple_of(own_at, LANES), ext)]
    scratch[:, pl.ds(0, ext)] = kept - (own_at - HALO).astype(F32)


def rotated(heads, cosine, sine):
    half = HEAD // 2
    a, b = heads[:half], heads[half:]
    return jnp.concatenate([a * cosine - b * sine, b * cosine + a * sine], 0)


def project(x_ref, wa_ref, trig_ref, q_ref, k_ref, v_ref, w, per):
    group = per * HEAD
    scale = HEAD**-0.5
    turned = jnp.transpose(wa_ref[w])
    queries = dot(turned[:group], x_ref[:, HALO:])
    cosine, sine = trig_ref[0], trig_ref[1]
    for i in range(per):
        rows = queries[i * HEAD : (i + 1) * HEAD]
        q_ref[w * per + i] = (rotated(rows, cosine[:, HALO:], sine[:, HALO:]).astype(BF16) * scale).astype(BF16)
    keys = dot(turned[group : 2 * group], x_ref[...])
    for i in range(per):
        rows = keys[i * HEAD : (i + 1) * HEAD]
        k_ref[w * per + i] = rotated(rows, cosine, sine).astype(BF16)
    values = dot(turned[2 * group : 3 * group], x_ref[...])
    for i in range(per):
        v_ref[w * per + i] = values[i * HEAD : (i + 1) * HEAD].astype(BF16)


def attend_bias(start_ref, bias_ref):
    for b in range(bias_ref.shape[0]):
        key_at = lax.broadcasted_iota(jnp.int32, (2 * HALO, HALO), 0).astype(F32) + float(b * HALO)
        query_at = lax.broadcasted_iota(jnp.int32, (2 * HALO, HALO), 1).astype(F32) + float((b + 1) * HALO)
        first = start_ref[0:1, (b + 1) * HALO : (b + 2) * HALO]
        bias_ref[b] = jnp.where((key_at >= first) & (key_at <= query_at), 0.0, MASKED)


def attend(q_ref, k_ref, v_ref, bias_ref, p_ref, ao_ref, w, per):
    ao_ref[w, 0:HEAD, :] = jnp.zeros((HEAD, ao_ref.shape[2]), BF16)
    for i in range(per):
        h = w * per + i
        for b in range(bias_ref.shape[0]):
            keys = k_ref[h, :, b * HALO : (b + 2) * HALO]
            scores = dot_cols(keys, q_ref[h, :, b * HALO : (b + 1) * HALO]) + bias_ref[b]
            top = jnp.max(scores, 0, keepdims=True)
            raised = jnp.exp(scores - top)
            total = jnp.sum(raised, 0, keepdims=True)
            p_ref[h, b] = (raised * (1.0 / total)).astype(BF16)
            out = dot(v_ref[h, :, b * HALO : (b + 2) * HALO], p_ref[h, b])
            ao_ref[w, (i + 1) * HEAD : (i + 2) * HEAD, b * HALO : (b + 1) * HALO] = out.astype(BF16)


def out_project(st_ref, wa_ref, ao_ref, mid_ref, width, per):
    group = 3 * per * HEAD - HEAD
    mid_ref[...] = st_ref[:, HALO:].astype(F32)

    def body(w):
        mid_ref[...] += dot(wa_ref[w, :, group:], ao_ref[w])

    tiles(width, body)


def feed_forward(xt_ref, wb_ref, wc_ref, acc_ref, pre_ref, hid_ref, slope_ref, width, slab, before):
    own = xt_ref.shape[0]
    strip = 32

    def body(at):
        w = slab(at)
        before(at, w)
        pre_ref[...] = dot(xt_ref[...], wb_ref[w])

        def gelu(part):
            rows = pl.ds(pl.multiple_of(part * strip, strip), strip)
            x = pre_ref[rows, :]
            root = math.sqrt(2.0 / math.pi)
            square = x * x
            bent = jnp.tanh(root * (x + 0.044715 * (square * x)))
            hid_ref[w, rows, :] = (0.5 * x * (1.0 + bent)).astype(BF16)
            slope = 0.5 * (1.0 + bent) + (0.5 * root) * x * (1.0 - bent * bent) * (1.0 + (3 * 0.044715) * square)
            slope_ref[w, rows, :] = slope.astype(BF16)

        tiles(own // strip, gelu)
        acc_ref[...] += dot_rows(wc_ref[w], hid_ref[w])

    tiles(width, body)


def feed_back(x_ref, ct_ref, ctt_ref, wb_ref, wc_ref, gb_ref, gc_ref, u_ref, gh_ref, hid_ref, slope_ref, width, slab, between, after):
    own = x_ref.shape[1]
    strip = 32
    u_ref[...] = jnp.zeros_like(u_ref)

    def body(at):
        w = slab(at)
        gh_ref[...] = dot(ctt_ref[...], wc_ref[w])
        between(at, w)

        def multiply(part):
            rows = pl.ds(pl.multiple_of(part * strip, strip), strip)
            slope_ref[w, rows, :] = (gh_ref[rows, :] * slope_ref[w, rows, :].astype(F32)).astype(BF16)

        tiles(own // strip, multiply)
        gc_ref[w] = dot(ct_ref[...], hid_ref[w]).astype(BF16)
        u_ref[...] += dot_rows(wb_ref[w], slope_ref[w])
        gb_ref[w] = dot(x_ref[...], slope_ref[w]).astype(BF16)
        after(at, w)

    tiles(width, body)


def attend_back(low_ref, wa_ref, p_ref, q_ref, k_ref, v_ref, trig_ref, gp_ref, w, per):
    group = per * HEAD
    ext = gp_ref.shape[2]
    blocks = ext // HALO - 1
    scale = HEAD**-0.5
    gp_ref[w, 3 * group :, :] = jnp.zeros((group, ext), BF16)
    gp_ref[w, :group, :HALO] = jnp.zeros((group, HALO), BF16)
    turned = jnp.transpose(wa_ref[w, :, 3 * group - HEAD :])
    upstream = dot(turned[HEAD:], low_ref[...]).astype(BF16)
    for i in range(per):
        h = w * per + i
        grad_keys, grad_values = [None] * (blocks + 1), [None] * (blocks + 1)
        for b in range(blocks):
            q = q_ref[h, :, b * HALO : (b + 1) * HALO]
            k = k_ref[h, :, b * HALO : (b + 2) * HALO]
            v = v_ref[h, :, b * HALO : (b + 2) * HALO]
            up = upstream[i * HEAD : (i + 1) * HEAD, b * HALO : (b + 1) * HALO]
            weights = p_ref[h, b]
            wide = weights.astype(F32)
            grad_weights = dot_cols(v, up)
            inner = jnp.sum(wide * grad_weights, 0, keepdims=True)
            grad_scores = (wide * (grad_weights - inner)).astype(BF16)
            gv = dot_rows(up, weights)
            gk = dot_rows(q, grad_scores)
            gq = dot(k, grad_scores) * scale
            cols = slice((b + 1) * HALO, (b + 2) * HALO)
            gp_ref[w, i * HEAD : (i + 1) * HEAD, cols] = rotated(gq, trig_ref[0, :, cols], -trig_ref[1, :, cols]).astype(BF16)
            for part in range(2):
                piece = slice(part * HALO, (part + 1) * HALO)
                at = b + part
                grad_keys[at] = gk[:, piece] if grad_keys[at] is None else grad_keys[at] + gk[:, piece]
                grad_values[at] = gv[:, piece] if grad_values[at] is None else grad_values[at] + gv[:, piece]
        for at in range(blocks + 1):
            cols = slice(at * HALO, (at + 1) * HALO)
            gp_ref[w, group + i * HEAD : group + (i + 1) * HEAD, cols] = rotated(
                grad_keys[at], trig_ref[0, :, cols], -trig_ref[1, :, cols]
            ).astype(BF16)
            gp_ref[w, 2 * group + i * HEAD : 2 * group + (i + 1) * HEAD, cols] = grad_values[at].astype(BF16)


def stream_back(wa_ref, gp_ref, u_ref, w):
    u_ref[...] += dot(wa_ref[w], gp_ref[w])


def project_back(x_ref, low_ref, ao_ref, gp_ref, ga_ref, w, per):
    group = 3 * per * HEAD - HEAD
    ga_ref[w, :, :group] = dot_rows(x_ref[...], gp_ref[w, :group, :]).astype(BF16)
    ga_ref[w, :, group:] = (
        dot_rows(x_ref[...], gp_ref[w, group:, :]) + dot_rows(low_ref[...], ao_ref[w])
    ).astype(BF16)


def block_kernel(width, rows, per, mix_ref, hist_ref, cot_ref, seg_ref, box_ref, own_ref, given_ref,
                 gcol_ref, bout_ref, small_ref, total_ref, left_ref,
                 full, st, ct, boxes_in, gain, x_one, stat_one, starts, trig, q, k, v, ao, prob, mid, stat_two, gmid, low, blk,
                 gacc_one, gacc_two, gs, hcol, macc, small_out, small_in, small_step,
                 last_box, boxes, load_sem, here_sem, send_sem, recv_sem):
    r, z = lax.axis_index("rows"), lax.axis_index("width")
    layers, piece, tokens = hist_ref.shape
    own = tokens // width
    ext = HALO + own
    per_row = seg_ref.shape[1] // own
    core, bits = row_bits(rows)
    hops = len(bits)
    cut = own // 2
    greet(z, r, width, rows)
    sends = Sends(send_sem, recv_sem)
    inside = own_ref is not None
    gathers = []
    if inside:
        gathers = [Gather(sends, at, own_ref.at[at], full.at[at], z, r, width, rows) for at in range(3)]
        first, second, third = gathers
    others = gathers[1:]
    slab = functools.partial(arrival, z, width=width)

    def each(*actions):
        for method, chosen, distances in actions:
            for away in distances:
                if away == 0:
                    for one in chosen:
                        getattr(one, method)(z)
                    continue
                for w, there in ((z - away, z >= away), (z + away, z + away < width)):
                    @pl.when(there)
                    def _(w=w, method=method, chosen=chosen):
                        for one in chosen:
                            getattr(one, method)(w)
    odd = lax.rem(z, 2) == 1
    mine = pl.ds(pl.multiple_of(z * piece, 16), piece)

    far = 1 - z // 2
    chunks = []
    for at in range(width):
        low_half = flip(far, 1) if at // 2 else far
        chunks.append(2 * low_half + at % 2)
    st_even = st.at[mine, pl.ds(HALO, own)]
    st_odd = st.at[mine, :]
    gain_sends = [sends.make(box_ref, boxes_in.at[z], (r, lax.rem(z + step, width))) for step in range(1, width)]
    base = sends.used
    sends.used += width - 1

    def scoped_stream(pair, mixed):
        def load(at):
            cols = pl.ds(pl.multiple_of(chunks[at // 2] * own + (at % 2) * cut, LANES), cut)
            return pltpu.make_async_copy(hist_ref.at[:, :, cols], pair.at[at % 3], load_sem.at[at % 3])

        def stream_copy(step, target, is_odd):
            start = pl.multiple_of(target * own, LANES)
            if is_odd:
                src, dst = mixed.at[:, pl.ds(pl.multiple_of(start - HALO, LANES), ext)], st_odd
            else:
                src, dst = mixed.at[:, pl.ds(start, own)], st_even
            return pltpu.make_async_remote_copy(
                src_ref=src, dst_ref=dst, send_sem=send_sem.at[base + step - 1], recv_sem=recv_sem.at[base + step - 1],
                device_id=(r, target), device_id_type=MESH,
            )

        for at in range(3):
            load(at).start()
        for copy in gain_sends:
            copy.start()
        boxes_in[z] = box_ref[...]
        when_stream = {}
        if inside:
            for gather in gathers:
                gather.hold()
            first.start(z)
            for gather in gathers:
                gather.spread(z)
            when_stream = {4: [lambda: each(("hop", [first], [1]), ("forward", [first], [1]))]}
        for at in range(2 * width):
            load(at).wait()
            target = chunks[at // 2]
            start = pl.multiple_of(target * own + (at % 2) * cut, LANES)
            mix_stream(mix_ref, pair.at[at % 3], mixed, pl.ds(start, cut), layers)
            if at + 3 < 2 * width:
                load(at + 3).start()
            for action in when_stream.get(at, ()):
                action()

        if inside:
            each(("hop", [first], [2]), ("forward", [first], [2]))
        for at in range(width):
            target, is_odd = chunks[at], at % 2 == 1
            for step in range(1, width):
                @pl.when(lax.rem(z + step, width) == target)
                def _(step=step, target=target, is_odd=is_odd):
                    stream_copy(step, target, is_odd).start()

            @pl.when(target == z)
            def _(is_odd=is_odd, target=target):
                start = pl.multiple_of(target * own, LANES)
                if is_odd:
                    st_odd[...] = mixed[:, pl.ds(pl.multiple_of(start - HALO, LANES), ext)]
                else:
                    st_even[...] = mixed[:, pl.ds(start, own)]
                    st[:, 0:HALO] = jnp.zeros((D, HALO), BF16)

        if inside:
            each(("to_chips", [first], [0]))
        for copy in gain_sends:
            copy.wait()
        spread_gains(boxes_in, gain, width, piece)
        document_starts(seg_ref, starts, trig, z // per_row, lax.rem(z, per_row) * own, own)
        if inside:
            each(
                ("to_chips", [first], [1]), ("to_core", [first], [0]),
                ("to_chips", others, [0]), ("hop", [first], [3]), ("start", others, [0]), ("to_chips", [first], [2]),
                ("to_core", [first], [1]), ("to_core", others, [0]),
            )
        for step in range(1, width):
            for is_odd in (False, True):
                @pl.when(lax.rem(z, 2) == int(is_odd))
                def _(step=step, is_odd=is_odd):
                    stream_copy(step, z, is_odd).wait_recv()

                @pl.when(lax.rem(z + step, 2) == int(is_odd))
                def _(step=step, is_odd=is_odd):
                    stream_copy(step, lax.rem(z + step, width), is_odd).wait_send()

        cot_here.start()

    cot_sends = []
    for step in range(1, width):
        target = lax.rem(z + step, width)
        cols = pl.ds(pl.multiple_of(target * own, LANES), own)
        cot_sends.append(sends.make(cot_ref.at[:, cols], ct.at[mine, :], (r, target)))
    cot_here = pltpu.make_async_copy(
        cot_ref.at[:, pl.ds(pl.multiple_of(z * own, LANES), own)], ct.at[mine, :], here_sem
    )
    if not inside:
        given = pltpu.make_async_copy(given_ref, full, load_sem.at[3])
        given.start()
    pl.run_scoped(scoped_stream, pltpu.VMEM((3, layers, piece, cut), BF16), pltpu.VMEM((piece, tokens), BF16))

    norm_forward(st, 0, gain, 0, x_one, stat_one, ext)
    if not inside:
        given.wait()

    def send_cotangent():
        for copy in cot_sends:
            copy.start()

    def scoped_attend(bias):
        attend_bias(starts, bias)
        if inside:
            serve = at_steps({
                0: [lambda: each(("to_core", [first], [2]))],
                1: [lambda: each(("to_chips", [first], [3]), ("hop", others, [1]), ("forward", others, [1]))],
                2: [lambda: each(("to_core", [first], [3]))],
                3: [lambda: each(("to_chips", others, [1]), ("hop", others, [2]), ("forward", others, [2]))],
            })

        def body(at):
            w = slab(at)
            if inside:
                serve(at)
            if inside:
                first.take(w)
            project(x_one, full.at[0], trig, q, k, v, w, per)
            attend(q, k, v, bias, prob, ao, w, per)

        tiles(width, body)

    pl.run_scoped(scoped_attend, pltpu.VMEM((own // HALO, 2 * HALO, HALO), F32))
    out_project(st, full.at[0], ao, mid, width, per)
    if inside:
        each(("to_core", others, [1]), ("to_chips", others, [2]), ("hop", others, [3]))
    send_cotangent()
    gmid[...] = mid[...]
    if inside:
        tiles(width, first.clear)

    scatters = []
    if inside:
        scatters = [
            Scatter(sends, at, True, full.at[at], [box.at[at] for box in boxes], last_box.at[at], total_ref.at[at], z, r, width, rows)
            for at in range(3)
        ]
    attending, pair_back = scatters[:1], scatters[1:]

    def back(method, chosen, at):
        for one in chosen:
            getattr(one, method)(turned(at))

    def later(method, chosen, at):
        return lambda: back(method, chosen, at)

    def turned(at):
        return slab(width - 1 - at)


    late = at_steps({})
    if inside:
        late = at_steps({
            0: [lambda: each(("to_core", others, [2]))],
            1: [lambda: each(("to_chips", others, [3]))],
            2: [lambda: each(("to_core", others, [3]))],
        })

    def feed_before(at, w):
        late(at)
        if inside:
            second.take(w)
            third.take(w)

    def feed_between(at, w):
        if inside:
            second.clear(w)
            third.clear(w)

        feed_service(at)

    feed_service = at_steps({
        1: [later("take_core", pair_back, 0)],
        3: [later("take_chips", pair_back, 0), later("take_core", pair_back, 1)],
    })

    def feed_after(at, w):
        for scatter in pair_back:
            scatter.begin(w)

    blk_sends, gs_sends = [], []
    here = pl.ds(pl.multiple_of(z * own, LANES), own)
    for step in range(1, width):
        target = lax.rem(z + step, width)
        part = pl.ds(pl.multiple_of(target * piece, 16), piece)
        blk_sends.append(sends.make(blk.at[part, :], bout_ref.at[:, here], (r, target)))

    blk_here = pltpu.make_async_copy(blk.at[mine, :], bout_ref.at[:, here], load_sem.at[3])

    def scoped_feed(x_two, turn, pre, hid, slope, u_two):
        norm_forward(mid, 0, gain, 1, x_two, stat_two, own)
        turn[...] = jnp.transpose(x_two[...])
        feed_forward(turn, full.at[1], full.at[2], gmid, pre, hid, slope, width, slab, feed_before)
        blk[...] = gmid[...].astype(BF16)
        for copy in blk_sends:
            copy.start()
        blk_here.start()
        for copy in cot_sends:
            copy.wait()
        cot_here.wait()
        turn[...] = jnp.transpose(ct[...])
        feed_back(
            x_two, ct, turn, full.at[1], full.at[2], full.at[1], full.at[2], u_two, pre, hid, slope, width, turned, feed_between, feed_after
        )

        def write(cols, value):
            gmid[:, cols] = value
            low[:, cols] = value.astype(BF16)

        gacc_two[...] = jnp.zeros_like(gacc_two)
        norm_back(u_two, 0, mid, 0, stat_two, 0, gain, 1, lambda cols: ct[:, cols].astype(F32), write, gacc_two, 0, own)

    pl.run_scoped(
        scoped_feed, pltpu.VMEM((D, own), BF16), pltpu.VMEM((own, D), BF16), pltpu.VMEM((own, D), F32),
        pltpu.VMEM((width, own, D), BF16), pltpu.VMEM((width, own, D), BF16), pltpu.VMEM((D, own), F32),
    )

    slab_start = at_steps({3: [later("take_last", pair_back, 1), later("relay", pair_back, 0)]})
    slab_middle = at_steps({
        1: [later("take_chips", pair_back, 1), later("take_core", pair_back, 2), later("take_last", pair_back, 0)],
        3: [later("take_chips", pair_back, 2), later("take_core", pair_back, 3)],
    })
    when_mix = {
        3: [
            later("take_chips", attending, 0), later("take_chips", attending, 1), later("take_last", pair_back, 3),
            later("relay", pair_back, 2),
        ]
    }
    half = own // 2
    halo_sends = []
    own_columns = pl.ds(HALO, own)
    for step in range(1, width):
        target = lax.rem(z + step, width)
        features = pl.ds(pl.multiple_of(target * piece, 16), piece)
        gs_sends.append(sends.make(gs.at[features, own_columns], gcol_ref.at[:, here], (r, target)))
        halo_sends.append(sends.make(gs.at[features, pl.ds(0, HALO)], hcol.at[lax.div(z, 2)], (r, target)))

    def scoped_back(gp, u):
        def weights_back(at):
            w = turned(at)
            project_back(x_one, low, ao, gp, full.at[0], w, per)
            for scatter in attending:
                scatter.begin(w)

        def body(at):
            w = turned(at)
            slab_start(at)
            attend_back(low, full.at[0], prob, q, k, v, trig, gp, w, per)
            slab_middle(at)
            stream_back(full.at[0], gp, u, w)

        u[...] = jnp.zeros_like(u)
        tiles(width, body)

        gs_own, gs_halo = gs.at[:, own_columns], gs.at[:, pl.ds(0, HALO)]

        def write_own(cols, value):
            gs_own[:, cols] = value.astype(BF16)

        def write_halo(cols, value):
            gs_halo[:, cols] = value.astype(BF16)

        gacc_one[...] = jnp.zeros_like(gacc_one)
        norm_back(u, 0, st, 0, stat_one, 0, gain, 0, lambda cols: 0.0, write_halo, gacc_one, 0, HALO)
        norm_back(u, HALO, st, HALO, stat_one, HALO, gain, 0, lambda cols: gmid[:, cols], write_own, gacc_one, 0, own)
        for copy in gs_sends:
            copy.start()
        gcol_ref[:, here] = gs[mine, own_columns]

        @pl.when(odd)
        def _():
            for copy in halo_sends:
                copy.start()
            hcol[lax.div(z, 2)] = gs[mine, pl.ds(0, HALO)]

        tiles(width, weights_back)
        back("take_core", attending, 0)
        back("take_core", attending, 1)
        back("take_last", pair_back, 2)
        back("relay", pair_back, 1)
        back("take_chips", pair_back, 3)
        back("take_core", attending, 2)
        back("take_core", attending, 3)

    pl.run_scoped(scoped_back, pltpu.VMEM((width, 4 * per * HEAD, ext), BF16), pltpu.VMEM((D, ext), F32))

    macc[...] = jnp.zeros_like(macc)
    strip = 16

    def scoped_mix(pair):
        def place(at):
            chunk = lax.rem(z + width - at % width, width)
            return pl.ds(pl.multiple_of(chunk * own + (at // width) * half, LANES), half)

        def load(at):
            return pltpu.make_async_copy(hist_ref.at[:, :, place(at)], pair.at[at % 3], load_sem.at[at % 3])

        for at in range(3):
            load(at).start()
        for at in range(2 * width):
            if 0 < at < width:
                gs_sends[at - 1].wait_recv()
            if at == width:
                for step in range(1, width):
                    @pl.when(lax.rem(z + step, 2) == 1)
                    def _(step=step):
                        halo_sends[step - 1].wait_recv()

                for pair_at in range(width // 2):
                    cols = pl.ds((2 * pair_at + 1) * own - HALO, HALO)
                    gcol_ref[:, cols] = (gcol_ref[:, cols].astype(F32) + hcol[pair_at].astype(F32)).astype(BF16)
            load(at).wait()
            cols = place(at)

            def body(row, at=at, cols=cols):
                part = pl.ds(pl.multiple_of(row * strip, strip), strip)
                g = gcol_ref[part, cols].astype(F32)
                for j in range(layers):
                    crossed = pair[at % 3, j, part, :].astype(F32) * g
                    folded = crossed[:8] + crossed[8:]
                    total = folded[:, :LANES]
                    for lane in range(1, cut // LANES):
                        total = total + folded[:, lane * LANES : (lane + 1) * LANES]
                    macc[j] += total

            tiles(piece // strip, body)
            if at + 3 < 2 * width:
                load(at + 3).start()
            for action in when_mix.get(at, ()):
                action()

    pl.run_scoped(scoped_mix, pltpu.VMEM((3, layers, piece, cut), BF16))

    small_out[...] = jnp.zeros_like(small_out)
    gain_one = jnp.sum(jnp.transpose(gacc_one[...]), 0, keepdims=True)
    gain_two = jnp.sum(jnp.transpose(gacc_two[...]), 0, keepdims=True)
    depth = jnp.sum(jnp.transpose(jnp.sum(macc[...], 1)), 0, keepdims=True)
    for w in range(width):
        small_out[w, 0:1, 0:piece] = gain_one[:, w * piece : (w + 1) * piece]
        small_out[w, 1:2, 0:piece] = gain_two[:, w * piece : (w + 1) * piece]
        small_out[w, 2:3, 0 : depth.shape[1]] = depth
    small_sends = [
        sends.make(small_out.at[lax.rem(z + step, width)], small_in.at[step - 1], (r, lax.rem(z + step, width)))
        for step in range(1, width)
    ]
    for copy in small_sends:
        copy.start()
    back("take_last", attending, 0)
    back("take_last", attending, 1)
    back("take_chips", attending, 2)
    back("take_chips", attending, 3)
    current = small_out[z]
    for step in range(1, width):
        small_sends[step - 1].wait_recv()
        current = current + small_in[step - 1]
    peers = plane_peers(r, rows)
    small_step[0, 0] = current
    if rows > 8:
        for at, peer in enumerate(peers):
            small_step[at, 0] = current
            copy = sends.make(small_step.at[at, 0], small_step.at[at, 1], (peer, z))
            copy.start()
            copy.wait_recv()
            current = current + small_step[at, 1]
            small_sends.append(copy)
    else:
        plane_sends = [
            sends.make(small_step.at[0, 0], small_step.at[at, 1], (peer, z)) for at, peer in enumerate(peers)
        ]
        for copy in plane_sends:
            copy.start()
        for at, copy in enumerate(plane_sends):
            copy.wait_recv()
            current = current + small_step[at, 1]
        small_sends += plane_sends
    small_ref[...] = current
    back("relay", attending, 0)
    back("relay", attending, 1)
    back("take_last", attending, 2)
    back("take_last", attending, 3)
    back("relay", attending, 2)
    for scatter in scatters:
        scatter.finish()
    for copy in blk_sends:
        copy.wait()
    blk_here.wait()
    for copy in gs_sends + small_sends:
        copy.wait_send()

    @pl.when(odd)
    def _():
        for copy in halo_sends:
            copy.wait_send()

    for scatter in scatters:
        scatter.end()
    if not inside:
        leave = pltpu.make_async_copy(full, left_ref, load_sem.at[3])
        leave.start()
        leave.wait()


def vmem(count):
    return [pl.BlockSpec(memory_space=pltpu.VMEM)] * count


def shape(*sizes, dtype=F32):
    return jax.ShapeDtypeStruct(sizes, dtype)


def block(width, rows, mix, history, cotangent, segments, box, own_three):
    layers, piece, tokens = history.shape
    shard = own_three.shape[1]
    own = tokens // width
    ext = HALO + own
    heads = D // HEAD
    per = heads // width
    group = per * HEAD
    blocks = own // HALO
    digits = rows.bit_length() - 1
    inside = shard % 16 == 0
    any_space = pl.BlockSpec(memory_space=pl.ANY)
    ins = [mix, history, cotangent, segments, box]
    specs = [pl.BlockSpec(memory_space=pltpu.SMEM), any_space, any_space] + vmem(2)
    outs = [shape(piece, tokens, dtype=BF16), shape(piece, tokens, dtype=BF16), shape(8, 2 * LANES)]
    out_specs = vmem(1) + [any_space] + vmem(1)
    box_shapes = []
    if inside:
        ins, specs = ins + [own_three], specs + vmem(1)
        outs, out_specs = outs + [shape(3, shard, D)], out_specs + vmem(1)
        box_shapes = Scatter.box_shapes(width, rows, shard)
    else:
        gathered = lax.all_gather(lax.all_gather(own_three, "rows", axis=1, tiled=True), "width", axis=1)
        ins, specs = ins + [gathered], specs + [any_space]
        outs, out_specs = outs + [shape(3, width, D, D, dtype=BF16)], out_specs + [any_space]
    low = lambda *sizes: pltpu.VMEM(sizes, BF16)
    full = lambda *sizes: pltpu.VMEM(sizes, F32)
    scratch = [
        low(3, width, D, D), low(D, ext), low(D, own), full(width, 8, 2 * LANES), full(2, D, LANES), low(D, ext), full(8, ext),
        full(8, HALO + segments.shape[1]), full(2, HEAD // 2, ext), low(heads, HEAD, own), low(heads, HEAD, ext), low(heads, HEAD, ext),
        low(width, HEAD + group, own), low(heads, blocks, 2 * HALO, HALO), full(D, own), full(8, own),
        full(D, own), low(D, own), low(D, own), full(D, LANES), full(D, LANES), low(D, ext), low(width // 2, piece, HALO), full(layers, 8, LANES),
        full(width, 8, 2 * LANES), full(width - 1, 8, 2 * LANES), full(max(digits, rows - 1 if rows <= 8 else 0), 2, 8, 2 * LANES),
    ]
    common = len(scratch)
    if inside:
        scratch += [low(3, width + 1, shard, D)] + [low(3, *one) for one in box_shapes]
    count = 6 * (width - 1) + (width - 1) + max(digits, rows - 1 if rows <= 8 else 0)
    count += 3 * Gather.copies(width, rows) + 3 * Scatter.copies(width, rows)
    scratch += [
        pltpu.SemaphoreType.DMA((4,)), pltpu.SemaphoreType.DMA, pltpu.SemaphoreType.DMA((count,)), pltpu.SemaphoreType.DMA((count,)),
    ]

    def kernel(*refs):
        given, found, rest = refs[:6], refs[6:10], refs[10:]
        weights = (given[5], None) if inside else (None, given[5])
        results = (found[3], None) if inside else (None, found[3])
        kept, rest = rest[:common], rest[common:]
        last_box, boxes = None, ()
        if inside:
            last_box, boxes, rest = rest[0], rest[1 : 1 + len(box_shapes)], rest[1 + len(box_shapes) :]
        block_kernel(width, rows, per, *given[:5], *weights, *found[:3], *results, *kept, last_box, boxes, *rest)

    found = pl.pallas_call(
        kernel,
        out_shape=outs,
        in_specs=specs,
        out_specs=out_specs,
        scratch_shapes=scratch,
        compiler_params=pltpu.CompilerParams(collective_id=0, has_side_effects=True, vmem_limit_bytes=64 * MIB - 128 * 1024),
    )(*ins)
    if inside:
        return found
    total = lax.psum_scatter(found[3], "width", scatter_dimension=1)
    return (*found[:3], lax.psum_scatter(total, "rows", scatter_dimension=1, tiled=True).astype(F32))


def prepare_kernel(attend_ref, output_ref, expand_ref, reduce_ref, gains_ref, own_ref, box_ref):
    parts = [attend_ref[k] for k in range(3)] + [jnp.transpose(output_ref[...])]
    own_ref[0] = jnp.concatenate(parts, 1).astype(BF16)
    own_ref[1] = expand_ref[...].astype(BF16)
    own_ref[2] = reduce_ref[...].astype(BF16)
    box_ref[...] = jnp.zeros_like(box_ref)
    box_ref[0:2, 0 : gains_ref.shape[1]] = gains_ref[...]


def prepare(w_attend, w_output, w_expand, w_reduce, gains):
    shard, piece = w_expand.shape[0], gains.shape[1]
    if shard % 16 == 0:
        return pl.pallas_call(
            prepare_kernel,
            out_shape=[shape(3, shard, D, dtype=BF16), shape(8, 2 * LANES)],
            in_specs=vmem(5),
            out_specs=vmem(2),
            compiler_params=pltpu.CompilerParams(vmem_limit_bytes=60 * MIB),
        )(w_attend, w_output, w_expand, jnp.transpose(w_reduce), gains)
    first = jnp.concatenate([w_attend[0], w_attend[1], w_attend[2], jnp.transpose(w_output)], 1)
    own_three = jnp.stack([first, w_expand, jnp.transpose(w_reduce)]).astype(BF16)
    return own_three, jnp.pad(gains, ((0, 8 - gains.shape[0]), (0, 2 * LANES - piece)))


def finish_kernel(mix_ref, grad_ref, total_ref, out_ref, *refs):
    weights, small_ref, rest, (hist_ref, block_ref, *news) = refs[:12], refs[12], refs[13:19], refs[19:-2]
    made, sems = refs[-2:]
    piece = grad_ref.shape[0]
    layers = hist_ref.shape[0]
    strip = 16

    def cut(at):
        return pl.ds(pl.multiple_of(at * strip, strip), strip)

    def store(at):
        return pltpu.make_async_copy(made.at[:, cut(at), :], hist_ref.at[:, cut(at), :], sems.at[at])

    def part(at):
        g = grad_ref[cut(at), :].astype(F32)
        for j in range(layers):
            made[j, cut(at), :] = (mix_ref[j] * g).astype(BF16)
        store(at).start()

    tiles(piece // strip, part)
    block_ref[...] = out_ref[...]

    def update(which, gradient, rate):
        found = optimize(weights[3 * which][...], gradient, weights[3 * which + 1][...], weights[3 * which + 2][...], rate, DECAY)
        for ref, value in zip(news[3 * which : 3 * which + 3], found):
            ref[...] = value

    for k in range(3):
        gradient = total_ref[0, :, k * piece : (k + 1) * piece]
        found = optimize(weights[0][k], gradient, weights[1][k], weights[2][k], RATE_MATRIX, DECAY)
        for ref, value in zip(news[:3], found):
            ref[k] = value
    update(1, jnp.transpose(total_ref[0, :, 3 * piece :]), RATE_OUTPUT)
    update(2, total_ref[1], RATE_MATRIX)
    update(3, total_ref[2], RATE_MATRIX)
    sums = (small_ref[0:2, 0:piece], small_ref[2:3, 0 : rest[3].shape[1]])
    for which, rate in enumerate((RATE_GAIN, RATE_MIX)):
        w, m, v = rest[3 * which : 3 * which + 3]
        found = optimize(w[...], sums[which], m[...], v[...], rate, 0.0)
        for ref, value in zip(news[12 + 3 * which : 15 + 3 * which], found):
            ref[...] = value
    tiles(piece // strip, lambda at: store(at).wait())


def finish(mix, grad_stream, total, small, block_output, layers, weights, rest):
    shard = total.shape[1]
    piece, tokens = grad_stream.shape
    if shard % 16 == 0:
        given = [jnp.transpose(one) if at // 3 == 3 else one for at, one in enumerate(weights)]
        given += [small] + list(rest[:3]) + [jnp.reshape(one, (1, layers)) for one in rest[3:]]
        held = [shape(*one.shape) for at, one in enumerate(given) if at != 12]
        history_grad, block_output, *news = pl.pallas_call(
            finish_kernel,
            out_shape=[shape(layers, piece, tokens, dtype=BF16), shape(piece, tokens, dtype=BF16)] + held,
            in_specs=[pl.BlockSpec(memory_space=pltpu.SMEM)] + vmem(3 + len(given)),
            out_specs=[pl.BlockSpec(memory_space=pl.ANY)] + vmem(1 + len(held)),
            scratch_shapes=[pltpu.VMEM((layers, piece, tokens), BF16), pltpu.SemaphoreType.DMA((piece // 16,))],
            compiler_params=pltpu.CompilerParams(vmem_limit_bytes=60 * MIB),
        )(mix, grad_stream, total, block_output, *given)
        news = [jnp.transpose(one) if at // 3 == 3 else one for at, one in enumerate(news)]
        return (block_output, history_grad, *news[:15], *[jnp.reshape(one, (layers,)) for one in news[15:]])
    history_grad = (mix[:, None, None] * grad_stream[None].astype(F32)).astype(BF16)
    first = total[0]
    gradients = (
        jnp.stack([first[:, k * piece : (k + 1) * piece] for k in range(3)]),
        jnp.transpose(first[:, 3 * piece :]), total[1], jnp.transpose(total[2]),
    )
    news = []
    for at, rate in enumerate((RATE_MATRIX, RATE_OUTPUT, RATE_MATRIX, RATE_MATRIX)):
        w, m, v = weights[3 * at : 3 * at + 3]
        news += optimize(w, gradients[at], m, v, rate, DECAY)
    news += optimize(rest[0], small[0:2, :piece], rest[1], rest[2], RATE_GAIN, 0.0)
    news += optimize(rest[3], small[2, :layers], rest[4], rest[5], RATE_MIX, 0.0)
    return (block_output, history_grad, *news)


def on_device(
    width, rows, history, cotangent, segments, w_attend, m_attend, v_attend, w_output, m_output, v_output,
    w_expand, m_expand, v_expand, w_reduce, m_reduce, v_reduce, gains, m_gains, v_gains, mix, m_mix, v_mix,
):
    layers, piece, _ = history.shape
    own_three, box = prepare(w_attend, w_output, w_expand, w_reduce, gains)
    grad_stream, block_output, small, total = block(width, rows, mix, history, cotangent, segments, box, own_three)
    weights = (
        w_attend, m_attend, v_attend, w_output, m_output, v_output, w_expand, m_expand, v_expand, w_reduce, m_reduce, v_reduce,
    )
    rest = (gains, m_gains, v_gains, mix, m_mix, v_mix)
    return finish(mix, grad_stream, total, small, block_output, layers, weights, rest)


def solution(mesh):
    square, tall, wide = P(None, "rows", "width"), P("width", "rows"), P("rows", "width")
    weights = (square,) * 3 + (tall,) * 3 + (wide,) * 3 + (tall,) * 3 + (P(None, "width"),) * 3 + (P(),) * 3
    return jax.shard_map(
        functools.partial(on_device, mesh.shape["width"], mesh.shape["rows"]),
        mesh=mesh,
        in_specs=(P(None, "width", "rows"), P("width", "rows"), P("rows", None)) + weights,
        out_specs=(P("width", "rows"), P(None, "width", "rows")) + weights,
        check_vma=False,
    )
```

```python
import functools
import math
from types import SimpleNamespace

import jax
import jax.numpy as jnp
from jax import lax
from jax.experimental import pallas as pl
from jax.experimental.pallas import tpu as pltpu
from jax.sharding import PartitionSpec as P

D = 768
HEAD = 64
STEP = 10
HALO = 256
LANES = 128


EPS_NORM = 1e-05
EPS_ADAM = 1e-08
BETA_ONE = 0.9
BETA_TWO = 0.95
RATE_MATRIX = 0.02
RATE_OUTPUT = 0.12
RATE_GAIN = 0.4
RATE_MIX = 0.05
DECAY = 0.1
MASKED = -1e30

MESH = pl.DeviceIdType.MESH
F32 = jnp.float32
BF16 = jnp.bfloat16
MIB = 1 << 20


def optimize(weight, gradient, first_moment, second_moment, rate, decay):
    first_moment = BETA_ONE * first_moment + (1.0 - BETA_ONE) * gradient
    second_moment = BETA_TWO * second_moment + (1.0 - BETA_TWO) * gradient * gradient
    first_fixed = first_moment / (1.0 - BETA_ONE**STEP)
    second_fixed = second_moment / (1.0 - BETA_TWO**STEP)
    weight = weight - rate * (first_fixed / (jnp.sqrt(second_fixed) + EPS_ADAM) + decay * weight)
    return (weight, first_moment, second_moment)


def flip(index, bit):
    return index + bit - 2 * bit * lax.rem(lax.div(index, jnp.int32(bit)), 2)


def flips(index, bits):
    for bit in bits:
        index = flip(index, bit)
    return index


def subsets(bits):
    found = [()]
    for bit in bits:
        found = found + [one + (bit,) for one in found]
    return found


def row_bits(rows):
    digits = [1 << place for place in range(rows.bit_length() - 1)]
    return digits[0], digits[1:]


def tiles(count, body):
    def step(at, carry):
        body(at)
        return carry

    lax.fori_loop(0, count, step, 0)


def lane_tile(at, size=LANES, base=0):
    return pl.ds(pl.multiple_of(base + at * size, LANES), size)


def dot(a, b):
    return jnp.dot(a, b, preferred_element_type=F32)


def dot_rows(a, b):
    return lax.dot_general(a, b, (((1,), (1,)), ((), ())), preferred_element_type=F32)


def dot_cols(a, b):
    return lax.dot_general(a, b, (((0,), (0,)), ((), ())), preferred_element_type=F32)


def plane_peers(r, rows):
    core, bits = row_bits(rows)
    chosen = [one for one in subsets([core] + bits) if one]
    if rows > 8:
        chosen = [(bit,) for bit in [core] + bits]
    return [flips(r, one) for one in chosen]


def greet(z, r, width, rows):
    bar = pltpu.get_barrier_semaphore()
    places = [(r, lax.rem(z + k, width)) for k in range(1, width)] + [(peer, z) for peer in plane_peers(r, rows)]
    for place in places:
        pl.semaphore_signal(bar, inc=1, device_id=place, device_id_type=MESH)
    pl.semaphore_wait(bar, len(places))


def at_steps(table):
    def hook(step):
        for at, actions in table.items():
            @pl.when(step == at)
            def _(actions=actions):
                for action in actions:
                    action()

    return hook


class Sends:
    def __init__(self, send, recv):
        self.send, self.recv, self.used = send, recv, 0

    def reserve(self, count):
        at = self.used
        self.used += count
        return at

    def copy(self, at, src, dst, place):
        return pltpu.make_async_remote_copy(
            src_ref=src, dst_ref=dst, send_sem=self.send.at[at], recv_sem=self.recv.at[at],
            device_id=place, device_id_type=MESH,
        )

    def make(self, src, dst, place):
        return self.copy(self.reserve(1), src, dst, place)


def arrival(z, at, width):
    found = 0
    for own in range(width):
        order = sorted(range(width), key=lambda w, own=own: (abs(w - own), w))
        for place, w in enumerate(order):
            if w:
                found = found + w * jnp.where((z == own) & (at == place), 1, 0)
    return found


class Plane:
    def __init__(self, chunk, z, r, width, rows, shard):
        self.core, self.bits = row_bits(rows)
        self.chunk, self.z, self.r, self.width, self.shard = chunk, z, r, width, shard
        self.hops = len(self.bits)
        self.per_slab = self.hops + 1

    def rows(self, index):
        return pl.ds(pl.multiple_of(index * self.shard, 16), self.shard)

    def bit(self, w, at):
        one, other = self.bits[at], self.bits[::-1][at]
        return one + (other - one) * lax.rem(w + self.chunk, 2)

    def place(self, index, w, code):
        for at in range(self.hops):
            if code >> at & 1:
                index = flip(index, self.bit(w, at))
        return index


class Gather(Plane):
    def __init__(self, sends, chunk, own, full, z, r, width, rows):
        super().__init__(chunk, z, r, width, rows, own.shape[0])
        self.sends, self.own, self.full = sends, own, full
        self.line_base = sends.reserve(2 * (width - 1))
        self.slab_base = sends.reserve(width * self.per_slab)

    @staticmethod
    def copies(width, rows):
        return 2 * (width - 1) + width * (rows.bit_length() - 1)

    def line(self, w, up, distance, target):
        part = self.full.at[w, self.rows(self.r)]
        at = self.line_base + (1 - up) * (self.width - 1) + distance
        return self.sends.copy(at, part, part, (self.r, target))

    def hold(self):
        self.full[self.z, self.rows(self.r), :] = self.own[...]

    def start(self, w):
        for up, there, target in ((1, self.z + 1 < self.width, self.z + 1), (0, self.z > 0, self.z - 1)):
            @pl.when(there)
            def _(up=up, target=target):
                self.line(self.z, up, 0, target).start()

    def hop(self, w):
        up = jnp.where(w < self.z, 1, 0)
        distance = (self.z - w) * (2 * up - 1)
        self.line(w, up, distance - 1, self.z).wait_recv()
        self.spread(w)

    def onward(self, w):
        up = jnp.where(w < self.z, 1, 0)
        distance = (self.z - w) * (2 * up - 1)
        target = self.z + 2 * up - 1
        return (target >= 0) & (target < self.width), self.line(w, up, distance, target)

    def forward(self, w):
        there, copy = self.onward(w)

        @pl.when(there)
        def _():
            copy.start()

    def step(self, w, at):
        peer = flip(self.r, self.bit(w, at) if at < self.hops else self.core)
        found = []
        for code in range(2**at):
            part = self.full.at[w, self.rows(self.place(self.r, w, code))]
            found.append(self.sends.copy(self.slab_base + w * self.per_slab + at, part, part, (peer, self.z)))
        return found

    def whole(self, w, at):
        part = self.full.at[w, pl.ds(0, 2**at * self.shard)]
        return self.sends.copy(self.slab_base + w * self.per_slab + at, part, part, (flip(self.r, self.core), self.z))

    def spread(self, w):
        for copy in self.step(w, 0):
            copy.start()

    def pass_on(self, w, at):
        self.whole(w, at - 1).wait_recv()
        for copy in self.step(w, at):
            copy.start()

    def to_chips(self, w):
        for at in range(1, self.hops):
            self.pass_on(w, at)

    def to_core(self, w):
        if self.hops:
            self.pass_on(w, self.hops)

    def take(self, w):
        self.whole(w, self.hops).wait_recv()

    def clear(self, w):
        for at in range(self.hops + 1):
            self.whole(w, at).wait_send()

        @pl.when(w == self.z)
        def _():
            for up, there, target in ((1, self.z + 1 < self.width, self.z + 1), (0, self.z > 0, self.z - 1)):
                @pl.when(there)
                def _(up=up, target=target):
                    self.line(self.z, up, 0, target).wait_send()

        there, onward = self.onward(w)

        @pl.when((w != self.z) & there)
        def _():
            onward.wait_send()


class Scatter(Plane):
    def __init__(self, sends, chunk, along, grads, boxes, last_box, total, z, r, width, rows):
        super().__init__(chunk, z, r, width, rows, total.shape[0])
        self.sends, self.grads, self.boxes, self.last_box, self.total = sends, grads, boxes, last_box, total
        self.along = along
        self.other = flip(r, self.core)
        self.slab_base = sends.reserve(width * self.per_slab)
        self.width_base = sends.reserve(width + 1)

    @staticmethod
    def copies(width, rows):
        return width + 1 + width * (rows.bit_length() - 1)

    @staticmethod
    def box_shapes(width, rows, shard):
        hops = rows.bit_length() - 2
        return [(2 ** (hops - at), width, shard, D) for at in range(hops + 1)]

    def step(self, w, at):
        base = self.slab_base + w * self.per_slab + at
        if at == 0:
            return [
                self.sends.copy(base, self.grads.at[w, self.rows(self.place(self.other, w, code))], self.boxes[0].at[code, w], (self.other, self.z))
                for code in range(2**self.hops)
            ]
        peer = flip(self.r, self.bit(w, at - 1))
        return [
            self.sends.copy(base, self.boxes[at - 1].at[2 * code + 1, w], self.boxes[at].at[code, w], (peer, self.z))
            for code in range(2 ** (self.hops - at))
        ]

    def whole(self, w, at):
        part = self.boxes[at].at[:, w]
        return self.sends.copy(self.slab_base + w * self.per_slab + at, part, part, (self.other, self.z))

    def over_width(self, w):
        if self.along:
            target = self.z + jnp.where(w > self.z, 1, -1)
            slot = jnp.where((target == w) & (w < self.z), self.width, w)
        else:
            target = w
            slot = lax.rem(w - self.z + self.width, self.width) - 1
        return self.sends.copy(self.width_base + slot, self.boxes[self.hops].at[0, w], self.last_box.at[slot], (self.r, target))

    def came(self, slot):
        return self.sends.copy(self.width_base + slot, self.last_box.at[slot], self.last_box.at[slot], (self.r, flip(self.z, 1)))

    def awaited(self, w):
        return jnp.where(w > self.z, self.z, self.width - 1 - self.z) > 0

    def relay(self, w):
        if self.along:
            @pl.when((w != self.z) & self.awaited(w))
            def _():
                self.came(w).wait_recv()
                box = self.boxes[self.hops].at[0, w]
                box[...] = (box[...].astype(F32) + self.last_box[w].astype(F32)).astype(BF16)
                self.over_width(w).start()

    def begin(self, w):
        for copy in self.step(w, 0):
            copy.start()

    def take(self, w, at):
        self.whole(w, at).wait_recv()
        for code in range(2 ** (self.hops - at)):
            box = self.boxes[at].at[code, w]
            if at == 0:
                kept = self.grads.at[w, self.rows(self.place(self.r, w, code))]
            else:
                kept = self.boxes[at - 1].at[2 * code, w]
            box[...] = (box[...].astype(F32) + kept[...].astype(F32)).astype(BF16)
        if at < self.hops:
            for copy in self.step(w, at + 1):
                copy.start()
        else:
            @pl.when((w != self.z) & jnp.logical_not(self.awaited(w)) if self.along else w != self.z)
            def _():
                self.over_width(w).start()

    def take_core(self, w):
        self.take(w, 0)

    def take_chips(self, w):
        for at in range(1, self.hops):
            self.take(w, at)

    def take_last(self, w):
        if self.hops:
            self.take(w, self.hops)

    def finish(self):
        self.total[...] = self.boxes[self.hops][0, self.z].astype(F32)
        if self.along:
            arrivals = ((self.z, self.z > 0), (self.width, self.z < self.width - 1))
        else:
            arrivals = [(slot, self.z >= 0) for slot in range(self.width - 1)]
        for slot, there in arrivals:
            @pl.when(there)
            def _(slot=slot):
                self.came(slot).wait_recv()
                self.total[...] += self.last_box[slot].astype(F32)

    def end(self):
        def one(w):
            for at in range(self.hops + 1):
                self.whole(w, at).wait_send()

            @pl.when(w != self.z)
            def _():
                self.over_width(w).wait_send()

        tiles(self.width, one)


def mix_stream(mix_ref, pair_ref, out_ref, base, layers):
    features, size = pair_ref.shape[1], pair_ref.shape[2]
    strip = 16

    def body(at):
        rows = pl.ds(pl.multiple_of(at * strip, strip), strip)
        total = mix_ref[0] * pair_ref[0, rows, :].astype(F32)
        for j in range(1, layers):
            total = total + mix_ref[j] * pair_ref[j, rows, :].astype(F32)
        out_ref[rows, base] = total.astype(BF16)

    tiles(features // strip, body)


def spread_gains(box_ref, gain_ref, width, piece):
    for w in range(width):
        for i in range(2):
            row = box_ref[w, pl.ds(i, 1), :]
            full = jnp.transpose(jnp.broadcast_to(row, (LANES, row.shape[1])))
            gain_ref[i, pl.ds(w * piece, piece), :] = full[:piece]


def norm_forward(x_ref, x_base, gain_ref, i, out_ref, stat_ref, count):
    def body(at):
        cols = lane_tile(at)
        x = x_ref[:, lane_tile(at, base=x_base)].astype(F32)
        centre = jnp.sum(x, 0, keepdims=True) / D
        spread = jnp.sum(x * x, 0, keepdims=True) / D - centre * centre
        scaling = lax.rsqrt(spread + EPS_NORM)
        out_ref[:, cols] = (gain_ref[i] * ((x - centre) * scaling)).astype(BF16)
        stat_ref[0:1, cols] = centre
        stat_ref[1:2, cols] = scaling

    tiles(count // LANES, body)


def norm_back(u_ref, u_base, x_ref, x_base, stat_ref, stat_base, gain_ref, i, residual, write, gain_acc, start, count):
    def body(step):
        at = step + start // LANES
        u = u_ref[:, lane_tile(at, base=u_base)].astype(F32)
        x = x_ref[:, lane_tile(at, base=x_base)].astype(F32)
        cols = lane_tile(at, base=stat_base)
        scaling = stat_ref[1:2, cols]
        centred = (x - stat_ref[0:1, cols]) * scaling
        gain_acc[...] += u * centred
        s = u * gain_ref[i]
        mean_s = jnp.sum(s, 0, keepdims=True) / D
        mean_c = jnp.sum(s * centred, 0, keepdims=True) / D
        write(lane_tile(at), residual(lane_tile(at)) + scaling * (s - mean_s - centred * mean_c))

    tiles(count // LANES, body)


def document_starts(seg_ref, start_ref, trig_ref, row, own_at, own):
    seg = seg_ref[pl.ds(row, 1), :]
    length = seg.shape[1]
    place = lax.broadcasted_iota(jnp.int32, (8, length), 1)
    seg = jnp.broadcast_to(seg, (8, length))
    before = pltpu.roll(seg, 1, 1)
    start = jnp.where((place > 0) & (seg == before), 0, place)
    step = 1
    while step < length:
        moved = pltpu.roll(start, step, 1)
        start = jnp.maximum(start, jnp.where(place >= step, moved, 0))
        step *= 2
    position = (place - start).astype(F32)
    scratch = start_ref.at[0:8]
    ext = HALO + own
    scratch[:, pl.ds(0, HALO)] = jnp.zeros((8, HALO), F32)
    scratch[:, pl.ds(HALO, length)] = position
    window = scratch[:, pl.ds(pl.multiple_of(own_at, LANES), ext)][0:1]
    half = HEAD // 2
    freq = jnp.exp(
        lax.broadcasted_iota(jnp.int32, (half, ext), 0).astype(F32) * (-2.0 * math.log(10000.0) / HEAD)
    )
    angle = freq * window
    trig_ref[0] = jnp.cos(angle)
    trig_ref[1] = jnp.sin(angle)
    scratch[:, pl.ds(HALO, length)] = start.astype(F32)
    kept = scratch[:, pl.ds(pl.multiple_of(own_at, LANES), ext)]
    scratch[:, pl.ds(0, ext)] = kept - (own_at - HALO).astype(F32)


def rotated(heads, cosine, sine):
    half = HEAD // 2
    a, b = heads[:half], heads[half:]
    return jnp.concatenate([a * cosine - b * sine, b * cosine + a * sine], 0)


def project(x_ref, wa_ref, trig_ref, q_ref, k_ref, v_ref, w, per):
    group = per * HEAD
    scale = HEAD**-0.5
    turned = jnp.transpose(wa_ref[w])
    queries = dot(turned[:group], x_ref[:, HALO:])
    cosine, sine = trig_ref[0], trig_ref[1]
    for i in range(per):
        rows = queries[i * HEAD : (i + 1) * HEAD]
        q_ref[w * per + i] = (rotated(rows, cosine[:, HALO:], sine[:, HALO:]).astype(BF16) * scale).astype(BF16)
    keys = dot(turned[group : 2 * group], x_ref[...])
    for i in range(per):
        rows = keys[i * HEAD : (i + 1) * HEAD]
        k_ref[w * per + i] = rotated(rows, cosine, sine).astype(BF16)
    values = dot(turned[2 * group : 3 * group], x_ref[...])
    for i in range(per):
        v_ref[w * per + i] = values[i * HEAD : (i + 1) * HEAD].astype(BF16)


def attend_bias(start_ref, bias_ref):
    for b in range(bias_ref.shape[0]):
        key_at = lax.broadcasted_iota(jnp.int32, (2 * HALO, HALO), 0).astype(F32) + float(b * HALO)
        query_at = lax.broadcasted_iota(jnp.int32, (2 * HALO, HALO), 1).astype(F32) + float((b + 1) * HALO)
        first = start_ref[0:1, (b + 1) * HALO : (b + 2) * HALO]
        bias_ref[b] = jnp.where((key_at >= first) & (key_at <= query_at), 0.0, MASKED)


def attend(q_ref, k_ref, v_ref, bias_ref, p_ref, ao_ref, w, per):
    ao_ref[w, 0:HEAD, :] = jnp.zeros((HEAD, ao_ref.shape[2]), BF16)
    for i in range(per):
        h = w * per + i
        for b in range(bias_ref.shape[0]):
            keys = k_ref[h, :, b * HALO : (b + 2) * HALO]
            scores = dot_cols(keys, q_ref[h, :, b * HALO : (b + 1) * HALO]) + bias_ref[b]
            top = jnp.max(scores, 0, keepdims=True)
            raised = jnp.exp(scores - top)
            total = jnp.sum(raised, 0, keepdims=True)
            p_ref[h, b] = (raised * (1.0 / total)).astype(BF16)
            out = dot(v_ref[h, :, b * HALO : (b + 2) * HALO], p_ref[h, b])
            ao_ref[w, (i + 1) * HEAD : (i + 2) * HEAD, b * HALO : (b + 1) * HALO] = out.astype(BF16)


def out_project(st_ref, wa_ref, ao_ref, mid_ref, width, per):
    group = 3 * per * HEAD - HEAD
    mid_ref[...] = st_ref[:, HALO:].astype(F32)

    def body(w):
        mid_ref[...] += dot(wa_ref[w, :, group:], ao_ref[w])

    tiles(width, body)


def feed_forward(xt_ref, wb_ref, wc_ref, acc_ref, pre_ref, hid_ref, slope_ref, width, slab, before):
    own = xt_ref.shape[0]
    strip = 32

    def body(at):
        w = slab(at)
        before(at, w)
        pre_ref[...] = dot(xt_ref[...], wb_ref[w])

        def gelu(part):
            rows = pl.ds(pl.multiple_of(part * strip, strip), strip)
            x = pre_ref[rows, :]
            root = math.sqrt(2.0 / math.pi)
            square = x * x
            bent = jnp.tanh(root * (x + 0.044715 * (square * x)))
            hid_ref[w, rows, :] = (0.5 * x * (1.0 + bent)).astype(BF16)
            slope = 0.5 * (1.0 + bent) + (0.5 * root) * x * (1.0 - bent * bent) * (1.0 + (3 * 0.044715) * square)
            slope_ref[w, rows, :] = slope.astype(BF16)

        tiles(own // strip, gelu)
        acc_ref[...] += dot_rows(wc_ref[w], hid_ref[w])

    tiles(width, body)


def feed_back(x_ref, ct_ref, ctt_ref, wb_ref, wc_ref, gb_ref, gc_ref, u_ref, gh_ref, hid_ref, slope_ref, width, slab, between, after):
    own = x_ref.shape[1]
    strip = 32
    u_ref[...] = jnp.zeros_like(u_ref)

    def body(at):
        w = slab(at)
        gh_ref[...] = dot(ctt_ref[...], wc_ref[w])
        between(at, w)

        def multiply(part):
            rows = pl.ds(pl.multiple_of(part * strip, strip), strip)
            slope_ref[w, rows, :] = (gh_ref[rows, :] * slope_ref[w, rows, :].astype(F32)).astype(BF16)

        tiles(own // strip, multiply)
        gc_ref[w] = dot(ct_ref[...], hid_ref[w]).astype(BF16)
        u_ref[...] += dot_rows(wb_ref[w], slope_ref[w])
        gb_ref[w] = dot(x_ref[...], slope_ref[w]).astype(BF16)
        after(at, w)

    tiles(width, body)


def attend_back(low_ref, wa_ref, p_ref, q_ref, k_ref, v_ref, trig_ref, gp_ref, w, per):
    group = per * HEAD
    ext = gp_ref.shape[2]
    blocks = ext // HALO - 1
    scale = HEAD**-0.5
    gp_ref[w, 3 * group :, :] = jnp.zeros((group, ext), BF16)
    gp_ref[w, :group, :HALO] = jnp.zeros((group, HALO), BF16)
    turned = jnp.transpose(wa_ref[w, :, 3 * group - HEAD :])
    upstream = dot(turned[HEAD:], low_ref[...]).astype(BF16)
    for i in range(per):
        h = w * per + i
        grad_keys, grad_values = [None] * (blocks + 1), [None] * (blocks + 1)
        for b in range(blocks):
            q = q_ref[h, :, b * HALO : (b + 1) * HALO]
            k = k_ref[h, :, b * HALO : (b + 2) * HALO]
            v = v_ref[h, :, b * HALO : (b + 2) * HALO]
            up = upstream[i * HEAD : (i + 1) * HEAD, b * HALO : (b + 1) * HALO]
            weights = p_ref[h, b]
            wide = weights.astype(F32)
            grad_weights = dot_cols(v, up)
            inner = jnp.sum(wide * grad_weights, 0, keepdims=True)
            grad_scores = (wide * (grad_weights - inner)).astype(BF16)
            gv = dot_rows(up, weights)
            gk = dot_rows(q, grad_scores)
            gq = dot(k, grad_scores) * scale
            cols = slice((b + 1) * HALO, (b + 2) * HALO)
            gp_ref[w, i * HEAD : (i + 1) * HEAD, cols] = rotated(gq, trig_ref[0, :, cols], -trig_ref[1, :, cols]).astype(BF16)
            for part in range(2):
                piece = slice(part * HALO, (part + 1) * HALO)
                at = b + part
                grad_keys[at] = gk[:, piece] if grad_keys[at] is None else grad_keys[at] + gk[:, piece]
                grad_values[at] = gv[:, piece] if grad_values[at] is None else grad_values[at] + gv[:, piece]
        for at in range(blocks + 1):
            cols = slice(at * HALO, (at + 1) * HALO)
            gp_ref[w, group + i * HEAD : group + (i + 1) * HEAD, cols] = rotated(
                grad_keys[at], trig_ref[0, :, cols], -trig_ref[1, :, cols]
            ).astype(BF16)
            gp_ref[w, 2 * group + i * HEAD : 2 * group + (i + 1) * HEAD, cols] = grad_values[at].astype(BF16)


def stream_back(wa_ref, gp_ref, u_ref, w):
    u_ref[...] += dot(wa_ref[w], gp_ref[w])


def project_back(x_ref, low_ref, ao_ref, gp_ref, ga_ref, w, per):
    group = 3 * per * HEAD - HEAD
    ga_ref[w, :, :group] = dot_rows(x_ref[...], gp_ref[w, :group, :]).astype(BF16)
    ga_ref[w, :, group:] = (
        dot_rows(x_ref[...], gp_ref[w, group:, :]) + dot_rows(low_ref[...], ao_ref[w])
    ).astype(BF16)


def block_kernel(width, rows, per, mix_ref, hist_ref, cot_ref, seg_ref, box_ref, own_ref, given_ref,
                 gcol_ref, bout_ref, small_ref, total_ref, left_ref,
                 full, st, ct, boxes_in, gain, x_one, stat_one, starts, trig, q, k, v, ao, prob, mid, stat_two, gmid, low, blk,
                 gacc_one, gacc_two, gs, hcol, macc, small_out, small_in, small_step,
                 last_box, boxes, load_sem, here_sem, send_sem, recv_sem):
    r, z = lax.axis_index("rows"), lax.axis_index("width")
    layers, piece, tokens = hist_ref.shape
    own = tokens // width
    ext = HALO + own
    per_row = seg_ref.shape[1] // own
    core, bits = row_bits(rows)
    hops = len(bits)
    cut = own // 2
    greet(z, r, width, rows)
    sends = Sends(send_sem, recv_sem)
    inside = own_ref is not None
    gathers = []
    if inside:
        gathers = [Gather(sends, at, own_ref.at[at], full.at[at], z, r, width, rows) for at in range(3)]
        first, second, third = gathers
    others = gathers[1:]
    slab = functools.partial(arrival, z, width=width)

    def each(*actions):
        for method, chosen, distances in actions:
            for away in distances:
                if away == 0:
                    for one in chosen:
                        getattr(one, method)(z)
                    continue
                for w, there in ((z - away, z >= away), (z + away, z + away < width)):
                    @pl.when(there)
                    def _(w=w, method=method, chosen=chosen):
                        for one in chosen:
                            getattr(one, method)(w)
    odd = lax.rem(z, 2) == 1
    mine = pl.ds(pl.multiple_of(z * piece, 16), piece)

    far = 1 - z // 2
    chunks = []
    for at in range(width):
        low_half = flip(far, 1) if at // 2 else far
        chunks.append(2 * low_half + at % 2)
    st_even = st.at[mine, pl.ds(HALO, own)]
    st_odd = st.at[mine, :]
    gain_sends = [sends.make(box_ref, boxes_in.at[z], (r, lax.rem(z + step, width))) for step in range(1, width)]
    base = sends.used
    sends.used += width - 1

    def scoped_stream(pair, mixed):
        def load(at):
            cols = pl.ds(pl.multiple_of(chunks[at // 2] * own + (at % 2) * cut, LANES), cut)
            return pltpu.make_async_copy(hist_ref.at[:, :, cols], pair.at[at % 3], load_sem.at[at % 3])

        def stream_copy(step, target, is_odd):
            start = pl.multiple_of(target * own, LANES)
            if is_odd:
                src, dst = mixed.at[:, pl.ds(pl.multiple_of(start - HALO, LANES), ext)], st_odd
            else:
                src, dst = mixed.at[:, pl.ds(start, own)], st_even
            return pltpu.make_async_remote_copy(
                src_ref=src, dst_ref=dst, send_sem=send_sem.at[base + step - 1], recv_sem=recv_sem.at[base + step - 1],
                device_id=(r, target), device_id_type=MESH,
            )

        for at in range(3):
            load(at).start()
        for copy in gain_sends:
            copy.start()
        boxes_in[z] = box_ref[...]
        when_stream = {}
        if inside:
            for gather in gathers:
                gather.hold()
            first.start(z)
            for gather in gathers:
                gather.spread(z)
            when_stream = {4: [lambda: each(("hop", [first], [1]), ("forward", [first], [1]))]}
        for at in range(2 * width):
            load(at).wait()
            target = chunks[at // 2]
            start = pl.multiple_of(target * own + (at % 2) * cut, LANES)
            mix_stream(mix_ref, pair.at[at % 3], mixed, pl.ds(start, cut), layers)
            if at + 3 < 2 * width:
                load(at + 3).start()
            for action in when_stream.get(at, ()):
                action()

        if inside:
            each(("hop", [first], [2]), ("forward", [first], [2]))
        for at in range(width):
            target, is_odd = chunks[at], at % 2 == 1
            for step in range(1, width):
                @pl.when(lax.rem(z + step, width) == target)
                def _(step=step, target=target, is_odd=is_odd):
                    stream_copy(step, target, is_odd).start()

            @pl.when(target == z)
            def _(is_odd=is_odd, target=target):
                start = pl.multiple_of(target * own, LANES)
                if is_odd:
                    st_odd[...] = mixed[:, pl.ds(pl.multiple_of(start - HALO, LANES), ext)]
                else:
                    st_even[...] = mixed[:, pl.ds(start, own)]
                    st[:, 0:HALO] = jnp.zeros((D, HALO), BF16)

        if inside:
            each(("to_chips", [first], [0]))
        for copy in gain_sends:
            copy.wait()
        spread_gains(boxes_in, gain, width, piece)
        document_starts(seg_ref, starts, trig, z // per_row, lax.rem(z, per_row) * own, own)
        if inside:
            each(
                ("to_chips", [first], [1]), ("to_core", [first], [0]),
                ("to_chips", others, [0]), ("hop", [first], [3]), ("start", others, [0]), ("to_chips", [first], [2]),
                ("to_core", [first], [1]), ("to_core", others, [0]),
            )
        for step in range(1, width):
            for is_odd in (False, True):
                @pl.when(lax.rem(z, 2) == int(is_odd))
                def _(step=step, is_odd=is_odd):
                    stream_copy(step, z, is_odd).wait_recv()

                @pl.when(lax.rem(z + step, 2) == int(is_odd))
                def _(step=step, is_odd=is_odd):
                    stream_copy(step, lax.rem(z + step, width), is_odd).wait_send()

        cot_here.start()

    cot_sends = []
    for step in range(1, width):
        target = lax.rem(z + step, width)
        cols = pl.ds(pl.multiple_of(target * own, LANES), own)
        cot_sends.append(sends.make(cot_ref.at[:, cols], ct.at[mine, :], (r, target)))
    cot_here = pltpu.make_async_copy(
        cot_ref.at[:, pl.ds(pl.multiple_of(z * own, LANES), own)], ct.at[mine, :], here_sem
    )
    if not inside:
        given = pltpu.make_async_copy(given_ref, full, load_sem.at[3])
        given.start()
    pl.run_scoped(scoped_stream, pltpu.VMEM((3, layers, piece, cut), BF16), pltpu.VMEM((piece, tokens), BF16))

    norm_forward(st, 0, gain, 0, x_one, stat_one, ext)
    if not inside:
        given.wait()

    def send_cotangent():
        for copy in cot_sends:
            copy.start()

    def scoped_attend(bias):
        attend_bias(starts, bias)
        if inside:
            serve = at_steps({
                0: [lambda: each(("to_core", [first], [2]))],
                1: [lambda: each(("to_chips", [first], [3]), ("hop", others, [1]), ("forward", others, [1]))],
                2: [lambda: each(("to_core", [first], [3]))],
                3: [lambda: each(("to_chips", others, [1]), ("hop", others, [2]), ("forward", others, [2]))],
            })

        def body(at):
            w = slab(at)
            if inside:
                serve(at)
            if inside:
                first.take(w)
            project(x_one, full.at[0], trig, q, k, v, w, per)
            attend(q, k, v, bias, prob, ao, w, per)

        tiles(width, body)

    pl.run_scoped(scoped_attend, pltpu.VMEM((own // HALO, 2 * HALO, HALO), F32))
    out_project(st, full.at[0], ao, mid, width, per)
    if inside:
        each(("to_core", others, [1]), ("to_chips", others, [2]), ("hop", others, [3]))
    send_cotangent()
    gmid[...] = mid[...]
    if inside:
        tiles(width, first.clear)

    scatters = []
    if inside:
        scatters = [
            Scatter(sends, at, True, full.at[at], [box.at[at] for box in boxes], last_box.at[at], total_ref.at[at], z, r, width, rows)
            for at in range(3)
        ]
    attending, pair_back = scatters[:1], scatters[1:]

    def back(method, chosen, at):
        for one in chosen:
            getattr(one, method)(turned(at))

    def later(method, chosen, at):
        return lambda: back(method, chosen, at)

    def turned(at):
        return slab(width - 1 - at)


    late = at_steps({})
    if inside:
        late = at_steps({
            0: [lambda: each(("to_core", others, [2]))],
            1: [lambda: each(("to_chips", others, [3]))],
            2: [lambda: each(("to_core", others, [3]))],
        })

    def feed_before(at, w):
        late(at)
        if inside:
            second.take(w)
            third.take(w)

    def feed_between(at, w):
        if inside:
            second.clear(w)
            third.clear(w)

        feed_service(at)

    feed_service = at_steps({
        1: [later("take_core", pair_back, 0)],
        3: [later("take_chips", pair_back, 0), later("take_core", pair_back, 1)],
    })

    def feed_after(at, w):
        for scatter in pair_back:
            scatter.begin(w)

    blk_sends, gs_sends = [], []
    here = pl.ds(pl.multiple_of(z * own, LANES), own)
    for step in range(1, width):
        target = lax.rem(z + step, width)
        part = pl.ds(pl.multiple_of(target * piece, 16), piece)
        blk_sends.append(sends.make(blk.at[part, :], bout_ref.at[:, here], (r, target)))

    blk_here = pltpu.make_async_copy(blk.at[mine, :], bout_ref.at[:, here], load_sem.at[3])

    def scoped_feed(x_two, turn, pre, hid, slope, u_two):
        norm_forward(mid, 0, gain, 1, x_two, stat_two, own)
        turn[...] = jnp.transpose(x_two[...])
        feed_forward(turn, full.at[1], full.at[2], gmid, pre, hid, slope, width, slab, feed_before)
        blk[...] = gmid[...].astype(BF16)
        for copy in blk_sends:
            copy.start()
        blk_here.start()
        for copy in cot_sends:
            copy.wait()
        cot_here.wait()
        turn[...] = jnp.transpose(ct[...])
        feed_back(
            x_two, ct, turn, full.at[1], full.at[2], full.at[1], full.at[2], u_two, pre, hid, slope, width, turned, feed_between, feed_after
        )

        def write(cols, value):
            gmid[:, cols] = value
            low[:, cols] = value.astype(BF16)

        gacc_two[...] = jnp.zeros_like(gacc_two)
        norm_back(u_two, 0, mid, 0, stat_two, 0, gain, 1, lambda cols: ct[:, cols].astype(F32), write, gacc_two, 0, own)

    pl.run_scoped(
        scoped_feed, pltpu.VMEM((D, own), BF16), pltpu.VMEM((own, D), BF16), pltpu.VMEM((own, D), F32),
        pltpu.VMEM((width, own, D), BF16), pltpu.VMEM((width, own, D), BF16), pltpu.VMEM((D, own), F32),
    )

    slab_start = at_steps({3: [later("take_last", pair_back, 1), later("relay", pair_back, 0)]})
    slab_middle = at_steps({
        1: [later("take_chips", pair_back, 1), later("take_core", pair_back, 2), later("take_last", pair_back, 0)],
        3: [later("take_chips", pair_back, 2), later("take_core", pair_back, 3)],
    })
    when_mix = {
        3: [
            later("take_chips", attending, 0), later("take_chips", attending, 1), later("take_last", pair_back, 3),
            later("relay", pair_back, 2),
        ]
    }
    half = own // 2
    halo_sends = []
    own_columns = pl.ds(HALO, own)
    for step in range(1, width):
        target = lax.rem(z + step, width)
        features = pl.ds(pl.multiple_of(target * piece, 16), piece)
        gs_sends.append(sends.make(gs.at[features, own_columns], gcol_ref.at[:, here], (r, target)))
        halo_sends.append(sends.make(gs.at[features, pl.ds(0, HALO)], hcol.at[lax.div(z, 2)], (r, target)))

    def scoped_back(gp, u):
        def weights_back(at):
            w = turned(at)
            project_back(x_one, low, ao, gp, full.at[0], w, per)
            for scatter in attending:
                scatter.begin(w)

        def body(at):
            w = turned(at)
            slab_start(at)
            attend_back(low, full.at[0], prob, q, k, v, trig, gp, w, per)
            slab_middle(at)
            stream_back(full.at[0], gp, u, w)

        u[...] = jnp.zeros_like(u)
        tiles(width, body)

        gs_own, gs_halo = gs.at[:, own_columns], gs.at[:, pl.ds(0, HALO)]

        def write_own(cols, value):
            gs_own[:, cols] = value.astype(BF16)

        def write_halo(cols, value):
            gs_halo[:, cols] = value.astype(BF16)

        gacc_one[...] = jnp.zeros_like(gacc_one)
        norm_back(u, 0, st, 0, stat_one, 0, gain, 0, lambda cols: 0.0, write_halo, gacc_one, 0, HALO)
        norm_back(u, HALO, st, HALO, stat_one, HALO, gain, 0, lambda cols: gmid[:, cols], write_own, gacc_one, 0, own)
        for copy in gs_sends:
            copy.start()
        gcol_ref[:, here] = gs[mine, own_columns]

        @pl.when(odd)
        def _():
            for copy in halo_sends:
                copy.start()
            hcol[lax.div(z, 2)] = gs[mine, pl.ds(0, HALO)]

        tiles(width, weights_back)
        back("take_core", attending, 0)
        back("take_core", attending, 1)
        back("take_last", pair_back, 2)
        back("relay", pair_back, 1)
        back("take_chips", pair_back, 3)
        back("take_core", attending, 2)
        back("take_core", attending, 3)

    pl.run_scoped(scoped_back, pltpu.VMEM((width, 4 * per * HEAD, ext), BF16), pltpu.VMEM((D, ext), F32))

    macc[...] = jnp.zeros_like(macc)
    strip = 16

    def scoped_mix(pair):
        def place(at):
            chunk = lax.rem(z + width - at % width, width)
            return pl.ds(pl.multiple_of(chunk * own + (at // width) * half, LANES), half)

        def load(at):
            return pltpu.make_async_copy(hist_ref.at[:, :, place(at)], pair.at[at % 3], load_sem.at[at % 3])

        for at in range(3):
            load(at).start()
        for at in range(2 * width):
            if 0 < at < width:
                gs_sends[at - 1].wait_recv()
            if at == width:
                for step in range(1, width):
                    @pl.when(lax.rem(z + step, 2) == 1)
                    def _(step=step):
                        halo_sends[step - 1].wait_recv()

                for pair_at in range(width // 2):
                    cols = pl.ds((2 * pair_at + 1) * own - HALO, HALO)
                    gcol_ref[:, cols] = (gcol_ref[:, cols].astype(F32) + hcol[pair_at].astype(F32)).astype(BF16)
            load(at).wait()
            cols = place(at)

            def body(row, at=at, cols=cols):
                part = pl.ds(pl.multiple_of(row * strip, strip), strip)
                g = gcol_ref[part, cols].astype(F32)
                for j in range(layers):
                    crossed = pair[at % 3, j, part, :].astype(F32) * g
                    folded = crossed[:8] + crossed[8:]
                    total = folded[:, :LANES]
                    for lane in range(1, cut // LANES):
                        total = total + folded[:, lane * LANES : (lane + 1) * LANES]
                    macc[j] += total

            tiles(piece // strip, body)
            if at + 3 < 2 * width:
                load(at + 3).start()
            for action in when_mix.get(at, ()):
                action()

    pl.run_scoped(scoped_mix, pltpu.VMEM((3, layers, piece, cut), BF16))

    small_out[...] = jnp.zeros_like(small_out)
    gain_one = jnp.sum(jnp.transpose(gacc_one[...]), 0, keepdims=True)
    gain_two = jnp.sum(jnp.transpose(gacc_two[...]), 0, keepdims=True)
    depth = jnp.sum(jnp.transpose(jnp.sum(macc[...], 1)), 0, keepdims=True)
    for w in range(width):
        small_out[w, 0:1, 0:piece] = gain_one[:, w * piece : (w + 1) * piece]
        small_out[w, 1:2, 0:piece] = gain_two[:, w * piece : (w + 1) * piece]
        small_out[w, 2:3, 0 : depth.shape[1]] = depth
    small_sends = [
        sends.make(small_out.at[lax.rem(z + step, width)], small_in.at[step - 1], (r, lax.rem(z + step, width)))
        for step in range(1, width)
    ]
    for copy in small_sends:
        copy.start()
    back("take_last", attending, 0)
    back("take_last", attending, 1)
    back("relay", attending, 0)
    back("take_chips", attending, 2)
    back("take_chips", attending, 3)
    back("relay", attending, 1)
    current = small_out[z]
    for step in range(1, width):
        small_sends[step - 1].wait_recv()
        current = current + small_in[step - 1]
    peers = plane_peers(r, rows)
    small_step[0, 0] = current
    if rows > 8:
        for at, peer in enumerate(peers):
            small_step[at, 0] = current
            copy = sends.make(small_step.at[at, 0], small_step.at[at, 1], (peer, z))
            copy.start()
            copy.wait_recv()
            current = current + small_step[at, 1]
            small_sends.append(copy)
    else:
        plane_sends = [
            sends.make(small_step.at[0, 0], small_step.at[at, 1], (peer, z)) for at, peer in enumerate(peers)
        ]
        for copy in plane_sends:
            copy.start()
        for at, copy in enumerate(plane_sends):
            copy.wait_recv()
            current = current + small_step[at, 1]
        small_sends += plane_sends
    small_ref[...] = current
    back("take_last", attending, 2)
    back("take_last", attending, 3)
    back("relay", attending, 2)
    for scatter in scatters:
        scatter.finish()
    for copy in blk_sends:
        copy.wait()
    blk_here.wait()
    for copy in gs_sends + small_sends:
        copy.wait_send()

    @pl.when(odd)
    def _():
        for copy in halo_sends:
            copy.wait_send()

    for scatter in scatters:
        scatter.end()
    if not inside:
        leave = pltpu.make_async_copy(full, left_ref, load_sem.at[3])
        leave.start()
        leave.wait()


def vmem(count):
    return [pl.BlockSpec(memory_space=pltpu.VMEM)] * count


def shape(*sizes, dtype=F32):
    return jax.ShapeDtypeStruct(sizes, dtype)


def block(width, rows, mix, history, cotangent, segments, box, own_three):
    layers, piece, tokens = history.shape
    shard = own_three.shape[1]
    own = tokens // width
    ext = HALO + own
    heads = D // HEAD
    per = heads // width
    group = per * HEAD
    blocks = own // HALO
    digits = rows.bit_length() - 1
    inside = shard % 16 == 0
    any_space = pl.BlockSpec(memory_space=pl.ANY)
    ins = [mix, history, cotangent, segments, box]
    specs = [pl.BlockSpec(memory_space=pltpu.SMEM), any_space, any_space] + vmem(2)
    outs = [shape(piece, tokens, dtype=BF16), shape(piece, tokens, dtype=BF16), shape(8, 2 * LANES)]
    out_specs = vmem(1) + [any_space] + vmem(1)
    box_shapes = []
    if inside:
        ins, specs = ins + [own_three], specs + vmem(1)
        outs, out_specs = outs + [shape(3, shard, D)], out_specs + vmem(1)
        box_shapes = Scatter.box_shapes(width, rows, shard)
    else:
        gathered = lax.all_gather(lax.all_gather(own_three, "rows", axis=1, tiled=True), "width", axis=1)
        ins, specs = ins + [gathered], specs + [any_space]
        outs, out_specs = outs + [shape(3, width, D, D, dtype=BF16)], out_specs + [any_space]
    low = lambda *sizes: pltpu.VMEM(sizes, BF16)
    full = lambda *sizes: pltpu.VMEM(sizes, F32)
    scratch = [
        low(3, width, D, D), low(D, ext), low(D, own), full(width, 8, 2 * LANES), full(2, D, LANES), low(D, ext), full(8, ext),
        full(8, HALO + segments.shape[1]), full(2, HEAD // 2, ext), low(heads, HEAD, own), low(heads, HEAD, ext), low(heads, HEAD, ext),
        low(width, HEAD + group, own), low(heads, blocks, 2 * HALO, HALO), full(D, own), full(8, own),
        full(D, own), low(D, own), low(D, own), full(D, LANES), full(D, LANES), low(D, ext), low(width // 2, piece, HALO), full(layers, 8, LANES),
        full(width, 8, 2 * LANES), full(width - 1, 8, 2 * LANES), full(max(digits, rows - 1 if rows <= 8 else 0), 2, 8, 2 * LANES),
    ]
    common = len(scratch)
    if inside:
        scratch += [low(3, width + 1, shard, D)] + [low(3, *one) for one in box_shapes]
    count = 6 * (width - 1) + (width - 1) + max(digits, rows - 1 if rows <= 8 else 0)
    count += 3 * Gather.copies(width, rows) + 3 * Scatter.copies(width, rows)
    scratch += [
        pltpu.SemaphoreType.DMA((4,)), pltpu.SemaphoreType.DMA, pltpu.SemaphoreType.DMA((count,)), pltpu.SemaphoreType.DMA((count,)),
    ]

    def kernel(*refs):
        given, found, rest = refs[:6], refs[6:10], refs[10:]
        weights = (given[5], None) if inside else (None, given[5])
        results = (found[3], None) if inside else (None, found[3])
        kept, rest = rest[:common], rest[common:]
        last_box, boxes = None, ()
        if inside:
            last_box, boxes, rest = rest[0], rest[1 : 1 + len(box_shapes)], rest[1 + len(box_shapes) :]
        block_kernel(width, rows, per, *given[:5], *weights, *found[:3], *results, *kept, last_box, boxes, *rest)

    found = pl.pallas_call(
        kernel,
        out_shape=outs,
        in_specs=specs,
        out_specs=out_specs,
        scratch_shapes=scratch,
        compiler_params=pltpu.CompilerParams(collective_id=0, has_side_effects=True, vmem_limit_bytes=64 * MIB - 128 * 1024),
    )(*ins)
    if inside:
        return found
    total = lax.psum_scatter(found[3], "width", scatter_dimension=1)
    return (*found[:3], lax.psum_scatter(total, "rows", scatter_dimension=1, tiled=True).astype(F32))


def prepare_kernel(attend_ref, output_ref, expand_ref, reduce_ref, gains_ref, own_ref, box_ref):
    parts = [attend_ref[k] for k in range(3)] + [jnp.transpose(output_ref[...])]
    own_ref[0] = jnp.concatenate(parts, 1).astype(BF16)
    own_ref[1] = expand_ref[...].astype(BF16)
    own_ref[2] = reduce_ref[...].astype(BF16)
    box_ref[...] = jnp.zeros_like(box_ref)
    box_ref[0:2, 0 : gains_ref.shape[1]] = gains_ref[...]


def prepare(w_attend, w_output, w_expand, w_reduce, gains):
    shard, piece = w_expand.shape[0], gains.shape[1]
    if shard % 16 == 0:
        return pl.pallas_call(
            prepare_kernel,
            out_shape=[shape(3, shard, D, dtype=BF16), shape(8, 2 * LANES)],
            in_specs=vmem(5),
            out_specs=vmem(2),
            compiler_params=pltpu.CompilerParams(vmem_limit_bytes=60 * MIB),
        )(w_attend, w_output, w_expand, jnp.transpose(w_reduce), gains)
    first = jnp.concatenate([w_attend[0], w_attend[1], w_attend[2], jnp.transpose(w_output)], 1)
    own_three = jnp.stack([first, w_expand, jnp.transpose(w_reduce)]).astype(BF16)
    return own_three, jnp.pad(gains, ((0, 8 - gains.shape[0]), (0, 2 * LANES - piece)))


def finish_kernel(mix_ref, grad_ref, total_ref, out_ref, *refs):
    weights, small_ref, rest, (hist_ref, block_ref, *news) = refs[:12], refs[12], refs[13:19], refs[19:-2]
    made, sems = refs[-2:]
    piece = grad_ref.shape[0]
    layers = hist_ref.shape[0]
    strip = 16

    def cut(at):
        return pl.ds(pl.multiple_of(at * strip, strip), strip)

    def store(at):
        return pltpu.make_async_copy(made.at[:, cut(at), :], hist_ref.at[:, cut(at), :], sems.at[at])

    def part(at):
        g = grad_ref[cut(at), :].astype(F32)
        for j in range(layers):
            made[j, cut(at), :] = (mix_ref[j] * g).astype(BF16)
        store(at).start()

    tiles(piece // strip, part)
    block_ref[...] = out_ref[...]

    def update(which, gradient, rate):
        found = optimize(weights[3 * which][...], gradient, weights[3 * which + 1][...], weights[3 * which + 2][...], rate, DECAY)
        for ref, value in zip(news[3 * which : 3 * which + 3], found):
            ref[...] = value

    for k in range(3):
        gradient = total_ref[0, :, k * piece : (k + 1) * piece]
        found = optimize(weights[0][k], gradient, weights[1][k], weights[2][k], RATE_MATRIX, DECAY)
        for ref, value in zip(news[:3], found):
            ref[k] = value
    update(1, jnp.transpose(total_ref[0, :, 3 * piece :]), RATE_OUTPUT)
    update(2, total_ref[1], RATE_MATRIX)
    update(3, total_ref[2], RATE_MATRIX)
    sums = (small_ref[0:2, 0:piece], small_ref[2:3, 0 : rest[3].shape[1]])
    for which, rate in enumerate((RATE_GAIN, RATE_MIX)):
        w, m, v = rest[3 * which : 3 * which + 3]
        found = optimize(w[...], sums[which], m[...], v[...], rate, 0.0)
        for ref, value in zip(news[12 + 3 * which : 15 + 3 * which], found):
            ref[...] = value
    tiles(piece // strip, lambda at: store(at).wait())


def finish(mix, grad_stream, total, small, block_output, layers, weights, rest):
    shard = total.shape[1]
    piece, tokens = grad_stream.shape
    if shard % 16 == 0:
        given = [jnp.transpose(one) if at // 3 == 3 else one for at, one in enumerate(weights)]
        given += [small] + list(rest[:3]) + [jnp.reshape(one, (1, layers)) for one in rest[3:]]
        held = [shape(*one.shape) for at, one in enumerate(given) if at != 12]
        history_grad, block_output, *news = pl.pallas_call(
            finish_kernel,
            out_shape=[shape(layers, piece, tokens, dtype=BF16), shape(piece, tokens, dtype=BF16)] + held,
            in_specs=[pl.BlockSpec(memory_space=pltpu.SMEM)] + vmem(3 + len(given)),
            out_specs=[pl.BlockSpec(memory_space=pl.ANY)] + vmem(1 + len(held)),
            scratch_shapes=[pltpu.VMEM((layers, piece, tokens), BF16), pltpu.SemaphoreType.DMA((piece // 16,))],
            compiler_params=pltpu.CompilerParams(vmem_limit_bytes=60 * MIB),
        )(mix, grad_stream, total, block_output, *given)
        news = [jnp.transpose(one) if at // 3 == 3 else one for at, one in enumerate(news)]
        return (block_output, history_grad, *news[:15], *[jnp.reshape(one, (layers,)) for one in news[15:]])
    history_grad = (mix[:, None, None] * grad_stream[None].astype(F32)).astype(BF16)
    first = total[0]
    gradients = (
        jnp.stack([first[:, k * piece : (k + 1) * piece] for k in range(3)]),
        jnp.transpose(first[:, 3 * piece :]), total[1], jnp.transpose(total[2]),
    )
    news = []
    for at, rate in enumerate((RATE_MATRIX, RATE_OUTPUT, RATE_MATRIX, RATE_MATRIX)):
        w, m, v = weights[3 * at : 3 * at + 3]
        news += optimize(w, gradients[at], m, v, rate, DECAY)
    news += optimize(rest[0], small[0:2, :piece], rest[1], rest[2], RATE_GAIN, 0.0)
    news += optimize(rest[3], small[2, :layers], rest[4], rest[5], RATE_MIX, 0.0)
    return (block_output, history_grad, *news)


def on_device(
    width, rows, history, cotangent, segments, w_attend, m_attend, v_attend, w_output, m_output, v_output,
    w_expand, m_expand, v_expand, w_reduce, m_reduce, v_reduce, gains, m_gains, v_gains, mix, m_mix, v_mix,
):
    layers, piece, _ = history.shape
    own_three, box = prepare(w_attend, w_output, w_expand, w_reduce, gains)
    grad_stream, block_output, small, total = block(width, rows, mix, history, cotangent, segments, box, own_three)
    weights = (
        w_attend, m_attend, v_attend, w_output, m_output, v_output, w_expand, m_expand, v_expand, w_reduce, m_reduce, v_reduce,
    )
    rest = (gains, m_gains, v_gains, mix, m_mix, v_mix)
    return finish(mix, grad_stream, total, small, block_output, layers, weights, rest)


def solution(mesh):
    square, tall, wide = P(None, "rows", "width"), P("width", "rows"), P("rows", "width")
    weights = (square,) * 3 + (tall,) * 3 + (wide,) * 3 + (tall,) * 3 + (P(None, "width"),) * 3 + (P(),) * 3
    return jax.shard_map(
        functools.partial(on_device, mesh.shape["width"], mesh.shape["rows"]),
        mesh=mesh,
        in_specs=(P(None, "width", "rows"), P("width", "rows"), P("rows", None)) + weights,
        out_specs=(P("width", "rows"), P(None, "width", "rows")) + weights,
        check_vma=False,
    )
```
